512 devices in a mesh: dp: 8 (over x, y_lo), seq: 64 (over y_hi, z, core).
Axes of the slice: x: 4, y: 8 (y_hi: 4, y_lo: 2; y = y_hi * 2 + y_lo), z: 8, core: 2. Of those that a mesh axis runs over, the one named last changes fastest.
Arguments:
- tokens: bfloat16 [8, 64, 128, 1152], P('dp', 'seq'), may hold values from -6 to 6
- spatial_qkv: bfloat16 [8, 64, 128, 1728], P('dp', 'seq'), may hold values from -160 to 160
- spatial_out_weight: bfloat16 [576, 1152], P('seq'), may hold values from -0.25 to 0.25
- temporal_qkv_weight: bfloat16 [1152, 1728], P(None, 'seq'), may hold values from -8 to 8
- temporal_out_weight: bfloat16 [576, 1152], P('seq'), may hold values from -0.25 to 0.25
- modulation: float32 [8, 4, 1152], P('dp'), may hold values from -3 to 3
- cotangent: bfloat16 [8, 64, 128, 1152], P('dp', 'seq'), may hold values from -30 to 30
Outputs:
- token_grad: bfloat16 [8, 64, 128, 1152], P('dp', 'seq')
- qkv_grad: bfloat16 [8, 64, 128, 1728], P('dp', 'seq')
- modulation_grad: float32 [8, 4, 1152], P('dp')
- out_weight_grad: float32 [576, 1152], P('seq')
The draws below stay inside these ranges and needn't reach their ends.
All inputs are finite; a program needn't handle non-finite values.
Results may differ from the reference program's by a relative error of at most 0.025.
Values may be sent and summed in bfloat16 or wider, within the bound.
No kernel may reach another device: no remote copies, remote signals or barrier semaphores. Data moves between devices by JAX's collectives and lax.ppermute only.
A program may use at most 64 MiB of HBM per device.

```python
import math
import jax
import jax.numpy as jnp
from jax import lax

D = 1152
HEADS = 8
HS = 72
ATT = 576
S = 128
FRAMES = 64
BATCH = 8


def draw_spatial_qkv(key, part):
    key = jax.random.fold_in(key, 11)
    key_base = jax.random.fold_in(key, 0)
    full_shape = (BATCH, FRAMES, S, 3 * ATT)
    samples = jax.random.normal(key_base, full_shape, jnp.float32)
    return jnp.clip(samples, -6.0, 6.0).astype(jnp.bfloat16)


def draw_temporal_qkv_weight(key, part):
    key = jax.random.fold_in(key, 12)
    key_base = jax.random.fold_in(key, 0)
    full_shape = (D, 3 * ATT)
    samples = jax.random.normal(key_base, full_shape, jnp.float32) * D ** (-0.5)
    return jnp.clip(samples, -8.0, 8.0).astype(jnp.bfloat16)


def draw_cotangent(key, part):
    key = jax.random.fold_in(key, 13)
    key_base = jax.random.fold_in(key, 0)
    full_shape = (BATCH, FRAMES, S, D)
    video_pos = jnp.arange(BATCH, dtype=jnp.float32) / max(BATCH - 1, 1)
    frame_pos = jnp.arange(FRAMES, dtype=jnp.float32) / max(FRAMES - 1, 1)
    place_pos = jnp.arange(S, dtype=jnp.float32) / max(S - 1, 1)
    samples = jax.random.normal(key_base, full_shape, jnp.float32)
    power = 1.0
    rising = ((0.6 + 1.2 * video_pos)[:, None, None, None] * (0.6 + 1.2 * frame_pos)[None, :, None, None] * (0.6 + 1.2 * place_pos)[None, None, :, None]) ** power
    return jnp.clip(samples * rising, -30.0, 30.0).astype(jnp.bfloat16)


def shard_levels(rng, extent, shards, least, high):
    def one(dim, parts):
        steps = jax.random.uniform(jax.random.fold_in(jax.random.fold_in(rng, 6), dim), (parts,), jnp.float32, least / len(shards), high / len(shards))
        return jnp.repeat(jnp.exp(steps), extent[dim] // parts).reshape((-1,) + (1,) * (len(extent) - dim - 1))

    loudness = one(*shards[0])
    for cut in shards[1:]:
        loudness = loudness * one(*cut)
    return loudness


def centred(stream_key, shape, spread, reach, pieces=(), kind=jnp.bfloat16):
    factor_of = shard_levels(stream_key, shape, pieces, -0.22, 0.18) if pieces else 1.0
    drawn = jax.random.normal(stream_key, shape, jnp.float32) * spread * factor_of
    return jnp.minimum(jnp.maximum(drawn, -reach), reach).astype(kind)


def setup_inputs(seed: int = 0) -> dict:
    key_of = jax.random.split(jax.random.key(seed), 8)
    return {
        "tokens": centred(key_of[0], (BATCH, FRAMES, S, D), 1.0, 6.0, ((0, 8), (1, 64))),
        "spatial_qkv": draw_spatial_qkv(jax.random.fold_in(key_of[7], 71), 0),
        "spatial_out_weight": centred(key_of[2], (ATT, D), ATT ** -0.5, 0.25, ((0, 64),)),
        "temporal_qkv_weight": draw_temporal_qkv_weight(jax.random.fold_in(key_of[7], 71), 0),
        "temporal_out_weight": centred(key_of[4], (ATT, D), ATT ** -0.5, 0.25, ((0, 64),)),
        "modulation": centred(key_of[5], (BATCH, 4, D), 0.6, 3.0, ((0, 8),), jnp.float32),
        "cotangent": draw_cotangent(jax.random.fold_in(key_of[7], 71), 0),
    }


def spatial_block(states, packed, gate_row, out_weight):
    groups, length, _ = packed.shape
    queries = packed[..., :ATT].reshape(groups, length, HEADS, HS).astype(jnp.float32)
    keys_part = packed[..., ATT:2 * ATT].reshape(groups, length, HEADS, HS).astype(jnp.float32)
    values_part = packed[..., 2 * ATT:].reshape(groups, length, HEADS, HS).astype(jnp.float32)
    scores = jnp.einsum('gqhe,gkhe->ghqk', queries, keys_part) * (1.0 / math.sqrt(HS))
    row_max = lax.stop_gradient(lax.optimization_barrier(jnp.max(scores, -1, keepdims=True)))
    weights = jnp.exp(scores - row_max)
    probabilities = lax.optimization_barrier((weights / lax.optimization_barrier(jnp.sum(weights, -1, keepdims=True))).astype(jnp.bfloat16))
    mixture = jnp.einsum('ghqk,gkhe->gqhe', probabilities.astype(jnp.float32), values_part)
    mixture = mixture.astype(jnp.bfloat16).reshape(groups * length, ATT)
    project = jnp.dot(mixture, out_weight, preferred_element_type=jnp.float32).reshape(states.shape)
    return (states.astype(jnp.float32) + gate_row * project).astype(jnp.bfloat16)

def temporal_norm(states, shift_row, scale_row, weight):
    average = lax.optimization_barrier(jnp.mean(states, -1, keepdims=True))
    centered = states - average
    variance = lax.optimization_barrier(jnp.mean(centered * centered, -1, keepdims=True))
    normed = (centered * lax.rsqrt(variance + 1e-06) * (1.0 + scale_row) + shift_row).astype(jnp.bfloat16)
    flattened = normed.reshape(-1, states.shape[-1])
    packed = jnp.dot(flattened, weight, preferred_element_type=jnp.float32).astype(jnp.bfloat16)
    return packed.reshape(states.shape[:-1] + (3 * ATT,))

def temporal_attend(packed):
    frames, places, _ = packed.shape
    queries = packed[..., :ATT].reshape(frames, places, HEADS, HS).astype(jnp.float32)
    keys_part = packed[..., ATT:2 * ATT].reshape(frames, places, HEADS, HS).astype(jnp.float32)
    values_part = packed[..., 2 * ATT:].reshape(frames, places, HEADS, HS).astype(jnp.float32)
    scores = jnp.einsum('fphe,gphe->phfg', queries, keys_part) * (1.0 / math.sqrt(HS))
    row_max = lax.stop_gradient(lax.optimization_barrier(jnp.max(scores, -1, keepdims=True)))
    weights = jnp.exp(scores - row_max)
    probabilities = lax.optimization_barrier((weights / lax.optimization_barrier(jnp.sum(weights, -1, keepdims=True))).astype(jnp.bfloat16))
    mixture = jnp.einsum('phfg,gphe->fphe', probabilities.astype(jnp.float32), values_part)
    return mixture.astype(jnp.bfloat16).reshape(frames, places, ATT)

def temporal_out(states, mixture, gate_row, weight):
    project = jnp.dot(mixture.reshape(-1, ATT), weight, preferred_element_type=jnp.float32)
    return states + gate_row * project.reshape(states.shape)

def temporal_full(states, shift_row, scale_row, gate_row, qkv_weight, out_weight):
    packed = temporal_norm(states, shift_row, scale_row, qkv_weight)
    mixture = temporal_attend(packed)
    return (temporal_out(states, mixture, gate_row, out_weight), mixture)

def reference(tokens, spatial_qkv, spatial_out_weight, temporal_qkv_weight, temporal_out_weight, modulation, cotangent):
    videos = tokens.shape[0]

    def spatial_frame(frame_states, frame_packed, gate_row):
        return spatial_block(frame_states[None], frame_packed[None], gate_row, spatial_out_weight)[0]
    spatial_saved = jax.checkpoint(spatial_frame)

    def forward(states_in, packed_in, factors):
        frame_states = states_in.reshape(videos * FRAMES, S, D)
        frame_packed = packed_in.reshape(videos * FRAMES, S, 3 * ATT)
        frame_gates = jnp.repeat(factors[:, 0], FRAMES, axis=0)
        hidden = lax.map(lambda members: spatial_saved(members[0], members[1], members[2]), (frame_states, frame_packed, frame_gates))
        hidden_states = hidden.reshape(states_in.shape).astype(jnp.float32)

        def per_video(states, shift_row, scale_row, gate_row):
            return temporal_full(states, shift_row, scale_row, gate_row, temporal_qkv_weight, temporal_out_weight)
        return jax.vmap(per_video)(hidden_states, factors[:, 1], factors[:, 2], factors[:, 3])
    result, backward, mixture = jax.vjp(forward, tokens, spatial_qkv, modulation, has_aux=True)
    incoming = cotangent.astype(jnp.float32)
    token_grad, qkv_grad, modulation_grad = backward(incoming)
    scaled = (incoming * modulation[:, 3][:, None, None, :]).astype(jnp.bfloat16)
    out_weight_grad = jnp.dot(mixture.reshape(-1, ATT).T, scaled.reshape(-1, D), preferred_element_type=jnp.float32)
    return (token_grad, qkv_grad, modulation_grad, out_weight_grad)
```

```python
import math

import jax
import jax.numpy as jnp
from jax import lax
from jax.experimental import pallas as pl
from jax.experimental.pallas import tpu as pltpu
from jax.sharding import Mesh
from jax.sharding import PartitionSpec as P

D = 1152
HEADS = 8
HS = 72
ATT = 576
ROWS = 128
SCALE = 1.0 / math.sqrt(HS)
SEQ = ("yhi", "z", "core")
CHIPS = ("yhi", "z")
DP = ("x", "ylo")
BF = jnp.bfloat16
F32 = jnp.float32


def nn(a, b):
    return lax.dot_general(a, b, (((1,), (0,)), ((), ())), preferred_element_type=F32)


def nt(a, b):
    return lax.dot_general(a, b, (((1,), (1,)), ((), ())), preferred_element_type=F32)


def tn(a, b):
    return lax.dot_general(a, b, (((0,), (0,)), ((), ())), preferred_element_type=F32)


def head_masks():
    head = lax.broadcasted_iota(jnp.int32, (ROWS, ATT), 1) // HS
    return [head == h for h in range(HEADS)]


def stack_heads(masks, a):
    zero = jnp.zeros_like(a)
    return jnp.concatenate([jnp.where(m, a, zero) for m in masks], 0)


def pick_heads(masks, a):
    out = a[:ROWS]
    for h in range(1, HEADS):
        out = jnp.where(masks[h], a[h * ROWS : (h + 1) * ROWS], out)
    return out


def softmax_rows(scores):
    top = jnp.max(scores, -1, keepdims=True)
    weights = jnp.exp(scores - top)
    return weights / jnp.sum(weights, -1, keepdims=True)


def attend(masks, q, k, v, same):
    q_stack = stack_heads(masks, q)
    scores = nt(q_stack, k) * SCALE
    if same is not None:
        scores = jnp.where(same, scores, -1e30)
    probs = softmax_rows(scores)
    probs_b = probs.astype(BF)
    mixed = pick_heads(masks, nn(probs_b, v)).astype(BF)
    return q_stack, probs, probs_b, mixed


def attend_back(masks, q_stack, k, v, probs, probs_b, d_mixed):
    d_stack = stack_heads(masks, d_mixed)
    d_probs = nt(d_stack, v).astype(BF).astype(F32)
    d_v = tn(probs_b, d_stack)
    d_scores = probs * (d_probs - jnp.sum(d_probs * probs, -1, keepdims=True)) * SCALE
    d_scores = d_scores.astype(BF)
    d_q = pick_heads(masks, nn(d_scores, k))
    d_k = tn(d_scores, q_stack)
    return d_q.astype(BF), d_k.astype(BF), d_v.astype(BF)


def spatial_forward_kernel(qkv, mixed):
    q, k, v = qkv[:, :ATT], qkv[:, ATT : 2 * ATT], qkv[:, 2 * ATT :]
    mixed[...] = attend(head_masks(), q, k, v, None)[3]


def spatial_backward_kernel(qkv, d_mixed, out):
    q, k, v = qkv[:, :ATT], qkv[:, ATT : 2 * ATT], qkv[:, 2 * ATT :]
    masks = head_masks()
    q_stack, probs, probs_b, _ = attend(masks, q, k, v, None)
    d_q, d_k, d_v = attend_back(masks, q_stack, k, v, probs, probs_b, d_mixed[...])
    out[:, :ATT] = d_q
    out[:, ATT : 2 * ATT] = d_k
    out[:, 2 * ATT :] = d_v


def temporal_kernel(
    core, tokens, cotangent, mixed_s, w_so, w_qkv, w_out, factors,
    hidden_grad, d_mixed_s, factor_grads, out_keep, out_send,
):
    gate_s, shift, scale, gate_t = (factors[i : i + 1, :] for i in range(4))
    project = nn(mixed_s[...], w_so[...])
    hidden = (tokens[...].astype(F32) + gate_s * project).astype(BF).astype(F32)
    centered = hidden - jnp.mean(hidden, -1, keepdims=True)
    inverse = lax.rsqrt(jnp.mean(centered * centered, -1, keepdims=True) + 1e-06)
    unit = centered * inverse
    normed = (unit * (1.0 + scale) + shift).astype(BF)
    wq, wk, wv = (w_qkv[i * ATT : (i + 1) * ATT, :] for i in range(3))
    q, k, v = (nt(normed, w).astype(BF) for w in (wq, wk, wv))

    masks = head_masks()
    row = lax.broadcasted_iota(jnp.int32, (HEADS * ROWS, ROWS), 0)
    col = lax.broadcasted_iota(jnp.int32, (HEADS * ROWS, ROWS), 1)
    same = ((row ^ col) & 1) == 0
    q_stack, probs, probs_b, mixed = attend(masks, q, k, v, same)

    cot = cotangent[...].astype(F32)
    scaled = (cot * gate_t).astype(BF)
    me = core[0]
    source = lax.broadcasted_iota(jnp.int32, (ATT, ATT), 0)
    target = lax.broadcasted_iota(jnp.int32, (ATT, ATT), 1)
    half = target // 288
    rest = target - half * 288
    chip = rest // 9
    wanted = chip * 18 + (half ^ me) * 9 + (rest - chip * 9)
    order = jnp.where(source == wanted, 1.0, 0.0).astype(BF)
    product = tn(nn(mixed, order).astype(BF), scaled)
    out_keep[...] = product[:288]
    out_send[...] = product[288:].astype(BF)

    d_mixed = nt(scaled, w_out[...]).astype(BF)
    d_q, d_k, d_v = attend_back(masks, q_stack, k, v, probs, probs_b, d_mixed)
    d_normed = (nn(d_q, wq) + nn(d_k, wk) + nn(d_v, wv)).astype(BF).astype(F32)
    d_unit = d_normed * (1.0 + scale)
    d_hidden = inverse * (
        d_unit
        - jnp.mean(d_unit, -1, keepdims=True)
        - unit * jnp.mean(d_unit * unit, -1, keepdims=True)
    )
    grad = (cot + d_hidden).astype(BF)
    hidden_grad[...] = grad
    grad = grad.astype(F32)
    d_mixed_s[...] = nt((grad * gate_s).astype(BF), w_so[...]).astype(BF)
    project_t = nn(mixed, w_out[...])
    factor_grads[0:1, :] = jnp.sum(grad * project, 0, keepdims=True)
    factor_grads[1:2, :] = jnp.sum(d_normed, 0, keepdims=True)
    factor_grads[2:3, :] = jnp.sum(d_normed * unit, 0, keepdims=True)
    factor_grads[3:4, :] = jnp.sum(cot * project_t, 0, keepdims=True)


def call(kernel, outs, *args, scalars=0, flops=10**9):
    specs = [pl.BlockSpec(memory_space=pltpu.SMEM)] * scalars
    specs += [pl.BlockSpec(memory_space=pltpu.VMEM)] * (len(args) - scalars)
    out_shape = [jax.ShapeDtypeStruct(s, d) for s, d in outs]
    return pl.pallas_call(
        kernel,
        out_shape=out_shape,
        in_specs=specs,
        out_specs=[pl.BlockSpec(memory_space=pltpu.VMEM)] * len(outs),
        compiler_params=pltpu.CompilerParams(vmem_limit_bytes=48 * 2**20),
        cost_estimate=pl.CostEstimate(flops=flops, bytes_accessed=10**7, transcendentals=10**5),
    )(*args)


def exchange(a):
    return lax.all_to_all(a, SEQ, 0, 0, tiled=True)


def body(tokens, qkv, w_so, w_qkv, w_out, factors, cotangent):
    tokens, qkv, cotangent, factors = tokens[0, 0], qkv[0, 0], cotangent[0, 0], factors[0]
    shard = jnp.concatenate([w_so, w_out, w_qkv.T], 0)
    gathered = lax.all_gather(shard, SEQ, axis=0)
    w_so = gathered[:, :9].reshape(ATT, D)
    w_out = gathered[:, 9:18].reshape(ATT, D)
    w_qkv = gathered[:, 18:].reshape(3 * ATT, D)

    tokens_p = exchange(tokens.reshape(64, 2, D)).reshape(ROWS, D)
    cot_p = exchange(cotangent.reshape(64, 2, D)).reshape(ROWS, D)
    (mixed_s,) = call(spatial_forward_kernel, [((ROWS, ATT), BF)], qkv)
    mixed_p = exchange(mixed_s.reshape(64, 2, ATT)).reshape(ROWS, ATT)

    core = lax.axis_index("core").astype(jnp.int32).reshape(1)
    hidden_grad, d_mixed, factor_part, out_keep, out_send = call(
        temporal_kernel,
        [((ROWS, D), BF), ((ROWS, ATT), BF), ((4, D), F32), ((288, D), F32), ((288, D), BF)],
        core, tokens_p, cot_p, mixed_p, w_so, w_qkv, w_out, factors,
        scalars=1, flops=4 * 10**9,
    )

    out_other = lax.ppermute(out_send, "core", [(0, 1), (1, 0)])
    packed = jnp.concatenate([hidden_grad, d_mixed], 1)
    back = exchange(packed.reshape(64, 2, D + ATT)).reshape(ROWS, D + ATT)
    token_grad = back[:, :D]
    (qkv_grad,) = call(spatial_backward_kernel, [((ROWS, 3 * ATT), BF)], qkv, back[:, D:])

    out_part = (out_keep + out_other.astype(F32)).astype(BF).reshape(32, 2, 9 * D // 2)
    out_part = lax.all_to_all(out_part, CHIPS, 0, 0, tiled=True)
    out_part = jnp.sum(out_part.astype(F32), 0)
    out_part = lax.all_to_all(jnp.broadcast_to(out_part[None], (8, 2, 9 * D // 2)), DP, 0, 0, tiled=True)
    out_grad = jnp.sum(out_part, 0).reshape(9, D)

    factor_part = jnp.sum(exchange(factor_part.reshape(64, 1, 72)), 0)
    factor_grad = exchange(jnp.broadcast_to(factor_part[None], (64, 1, 72)))
    factor_grad = factor_grad.reshape(4, D)
    return token_grad[None, None], qkv_grad[None, None], factor_grad[None], out_grad


def solution(mesh):
    fine = Mesh(mesh.devices.reshape(4, 2, 4, 8, 2), DP + SEQ)
    frames = P(DP, SEQ, None, None)
    return jax.shard_map(
        body,
        mesh=fine,
        in_specs=(
            frames,
            frames,
            P(SEQ, None),
            P(None, SEQ),
            P(SEQ, None),
            P(DP, None, None),
            frames,
        ),
        out_specs=(frames, frames, P(DP, None, None), P(SEQ, None)),
        check_vma=False,
    )
```

```python
import math

import jax
import jax.numpy as jnp
from jax import lax
from jax.experimental import pallas as pl
from jax.experimental.pallas import tpu as pltpu
from jax.sharding import Mesh
from jax.sharding import PartitionSpec as P

D = 1152
HEADS = 8
HS = 72
ATT = 576
ROWS = 128
SCALE = 1.0 / math.sqrt(HS)
SEQ = ("yhi", "z", "core")
CHIPS = ("yhi", "z")
DP = ("x", "ylo")
BF = jnp.bfloat16
F32 = jnp.float32


def nn(a, b):
    return lax.dot_general(a, b, (((1,), (0,)), ((), ())), preferred_element_type=F32)


def nt(a, b):
    return lax.dot_general(a, b, (((1,), (1,)), ((), ())), preferred_element_type=F32)


def tn(a, b):
    return lax.dot_general(a, b, (((0,), (0,)), ((), ())), preferred_element_type=F32)


def head_masks():
    head = lax.broadcasted_iota(jnp.int32, (ROWS, ATT), 1) // HS
    return [head == h for h in range(HEADS)]


def stack_heads(masks, a):
    zero = jnp.zeros_like(a)
    return jnp.concatenate([jnp.where(m, a, zero) for m in masks], 0)


def pick_heads(masks, a):
    out = a[:ROWS]
    for h in range(1, HEADS):
        out = jnp.where(masks[h], a[h * ROWS : (h + 1) * ROWS], out)
    return out


def softmax_rows(scores):
    top = jnp.max(scores, -1, keepdims=True)
    weights = jnp.exp(scores - top)
    return weights / jnp.sum(weights, -1, keepdims=True)


def attend(masks, q, k, v, same):
    q_stack = stack_heads(masks, q)
    scores = nt(q_stack, k) * SCALE
    if same is not None:
        scores = jnp.where(same, scores, -1e30)
    probs = softmax_rows(scores)
    probs_b = probs.astype(BF)
    mixed = pick_heads(masks, nn(probs_b, v)).astype(BF)
    return q_stack, probs, probs_b, mixed


def attend_back(masks, q_stack, k, v, probs, probs_b, d_mixed):
    d_stack = stack_heads(masks, d_mixed)
    d_probs = nt(d_stack, v).astype(BF).astype(F32)
    d_v = tn(probs_b, d_stack)
    d_scores = probs * (d_probs - jnp.sum(d_probs * probs, -1, keepdims=True)) * SCALE
    d_scores = d_scores.astype(BF)
    d_q = pick_heads(masks, nn(d_scores, k))
    d_k = tn(d_scores, q_stack)
    return d_q.astype(BF), d_k.astype(BF), d_v.astype(BF)


def spatial_forward_kernel(qkv, mixed):
    q, k, v = qkv[:, :ATT], qkv[:, ATT : 2 * ATT], qkv[:, 2 * ATT :]
    mixed[...] = attend(head_masks(), q, k, v, None)[3]


def spatial_backward_kernel(qkv, d_mixed, out):
    q, k, v = qkv[:, :ATT], qkv[:, ATT : 2 * ATT], qkv[:, 2 * ATT :]
    masks = head_masks()
    q_stack, probs, probs_b, _ = attend(masks, q, k, v, None)
    d_q, d_k, d_v = attend_back(masks, q_stack, k, v, probs, probs_b, d_mixed[...])
    out[:, :ATT] = d_q
    out[:, ATT : 2 * ATT] = d_k
    out[:, 2 * ATT :] = d_v


def compact_kernel(core, shards, own_so, own_out, own_qkv, h0, h1, c0, c1, c2, c3, so, out, qkv):
    for i in range(16):
        shard = shards[i].astype(F32)
        so[9 * i : 9 * i + 9, :] = shard[:9]
        out[9 * i : 9 * i + 9, :] = shard[9:18]
        qkv[27 * i : 27 * i + 27, :] = shard[18:]
    own_so[...] = so[...].astype(BF)
    own_out[...] = out[...].astype(BF)
    own_qkv[...] = qkv[...].astype(BF)
    at_qkv = pl.multiple_of(core[0] * 208, 16)
    at = pl.multiple_of(core[0] * 64, 16)
    h0[...] = own_qkv[pl.ds(at_qkv, 192), :]
    h1[0:32, :] = own_qkv[pl.ds(pl.multiple_of(at_qkv + 192, 16), 32), :]
    h1[32:112, :] = own_so[pl.ds(at, 80), :]
    h1[112:192, :] = own_out[pl.ds(at, 80), :]
    c0[...] = h0[0:96, :]
    c1[...] = h0[96:192, :]
    c2[...] = h1[0:96, :]
    c3[...] = h1[96:192, :]


SECTIONS = ((0, 0, 224), (1, 224, 304), (2, 304, 384))
BLOCK = (432, 144, 144)
STEP = (208, 64, 64)


def part_copies(ref, start, lo, hi, half, block, targets):
    copies = []
    for section, first, last in SECTIONS:
        first = first + 16 * half
        a, b = max(lo, first), min(hi, last)
        if a < b:
            row = a - SECTIONS[section][1] + STEP[section] * half
            to = pl.multiple_of(block * BLOCK[section] + row, 16)
            copies.append(
                (ref.at[pl.ds(start + a - lo, b - a)], targets[section].at[pl.ds(to, b - a)])
            )
    return copies


def assemble(place, own, near, swapped, targets, sems):
    own_so, own_out, own_qkv = own
    b0, b1, c0, c1, d0, d1, d2, d3 = near
    o1, o2 = swapped
    for me in range(2):

        @pl.when(place[0] == me)
        def _():
            cls = place[1]
            b, c, d = cls ^ 2, cls ^ 1, cls ^ 3
            pairs = []
            for ref, section in ((own_qkv, 0), (own_so, 1), (own_out, 2)):
                to = pl.multiple_of(cls * BLOCK[section], 16)
                pairs.append((ref, targets[section].at[pl.ds(to, BLOCK[section])]))
            for ref0, ref1, block in ((b0, b1, b), (c0, c1, c)):
                pairs += part_copies(ref0, 0, 0, 192, me, block, targets)
                pairs += part_copies(ref1, 0, 192, 384, me, block, targets)
            for i, ref in enumerate((d0, d1, d2, d3)):
                pairs += part_copies(ref, 0, 96 * i, 96 * i + 96, me, d, targets)
            pairs += part_copies(o1, 0, 0, 384, 1 - me, b, targets)
            pairs += part_copies(o1, 384, 0, 384, 1 - me, c, targets)
            pairs += part_copies(o2, 0, 0, 384, 1 - me, d, targets)
            copies = [pltpu.make_async_copy(a, z, sems.at[i]) for i, (a, z) in enumerate(pairs)]
            for copy in copies:
                copy.start()
            for copy in copies:
                copy.wait()


def temporal_kernel(
    place, tokens, cotangent, mixed_s, factors,
    own_so, own_out, own_qkv, b0, b1, c0, c1, d0, d1, d2, d3, o1, o2,
    hidden_grad, d_mixed_s, factor_grads, out_keep, out_send,
    w_qkv, w_so, w_out, sems,
):
    assemble(
        place, (own_so, own_out, own_qkv), (b0, b1, c0, c1, d0, d1, d2, d3), (o1, o2),
        (w_qkv, w_so, w_out), sems,
    )
    gate_s, shift, scale, gate_t = (factors[i : i + 1, :] for i in range(4))
    project = nn(mixed_s[...], w_so[...])
    hidden = (tokens[...].astype(F32) + gate_s * project).astype(BF).astype(F32)
    centered = hidden - jnp.mean(hidden, -1, keepdims=True)
    inverse = lax.rsqrt(jnp.mean(centered * centered, -1, keepdims=True) + 1e-06)
    unit = centered * inverse
    normed = (unit * (1.0 + scale) + shift).astype(BF)
    wq, wk, wv = (w_qkv[i * ATT : (i + 1) * ATT, :] for i in range(3))
    q, k, v = (nt(normed, w).astype(BF) for w in (wq, wk, wv))

    masks = head_masks()
    row = lax.broadcasted_iota(jnp.int32, (HEADS * ROWS, ROWS), 0)
    col = lax.broadcasted_iota(jnp.int32, (HEADS * ROWS, ROWS), 1)
    same = ((row ^ col) & 1) == 0
    q_stack, probs, probs_b, mixed = attend(masks, q, k, v, same)

    cot = cotangent[...].astype(F32)
    scaled = (cot * gate_t).astype(BF)
    left, right = scaled[:, :ATT], scaled[:, ATT:]
    first = place[0] == 0
    out_keep[...] = tn(mixed, jnp.where(first, left, right))
    out_send[...] = tn(mixed, jnp.where(first, right, left)).astype(BF)

    d_mixed = nt(scaled, w_out[...]).astype(BF)
    d_q, d_k, d_v = attend_back(masks, q_stack, k, v, probs, probs_b, d_mixed)
    d_normed = (nn(d_q, wq) + nn(d_k, wk) + nn(d_v, wv)).astype(BF).astype(F32)
    d_unit = d_normed * (1.0 + scale)
    d_hidden = inverse * (
        d_unit
        - jnp.mean(d_unit, -1, keepdims=True)
        - unit * jnp.mean(d_unit * unit, -1, keepdims=True)
    )
    grad = (cot + d_hidden).astype(BF)
    hidden_grad[...] = grad
    grad = grad.astype(F32)
    d_mixed_s[...] = nt((grad * gate_s).astype(BF), w_so[...]).astype(BF)
    project_t = nn(mixed, w_out[...])
    factor_grads[0:1, :] = jnp.sum(grad * project, 0, keepdims=True)
    factor_grads[1:2, :] = jnp.sum(d_normed, 0, keepdims=True)
    factor_grads[2:3, :] = jnp.sum(d_normed * unit, 0, keepdims=True)
    factor_grads[3:4, :] = jnp.sum(cot * project_t, 0, keepdims=True)


def call(kernel, outs, *args, scalars=0, remote=0, scratch=(), flops=10**9):
    vmem = pl.BlockSpec(memory_space=pltpu.VMEM)
    specs = [pl.BlockSpec(memory_space=pltpu.SMEM)] * scalars
    specs += [vmem] * (len(args) - scalars - remote)
    specs += [pl.BlockSpec(memory_space=pl.ANY)] * remote
    return pl.pallas_call(
        kernel,
        out_shape=[jax.ShapeDtypeStruct(s, d) for s, d in outs],
        in_specs=specs,
        out_specs=[vmem] * len(outs),
        scratch_shapes=list(scratch),
        compiler_params=pltpu.CompilerParams(vmem_limit_bytes=48 * 2**20),
        cost_estimate=pl.CostEstimate(flops=flops, bytes_accessed=10**7, transcendentals=10**5),
    )(*args)


def exchange(a):
    return lax.all_to_all(a, SEQ, 0, 0, tiled=True)


PLANE = ("x", "ylo", "yhi")


def plane_index(x, y):
    return (x % 4) * 8 + (y % 2) * 4 + (y % 8) // 2


def from_neighbour(a, dx, dy):
    pairs = [(plane_index(x + dx, y + dy), plane_index(x, y)) for x in range(4) for y in range(8)]
    return lax.ppermute(a, PLANE, pairs)


def transpose_classes(a):
    pairs = []
    for x in range(4):
        for ylo in range(2):
            for yhi in range(4):
                cls = (x % 2) * 2 + ylo
                source = ((x // 2) * 2 + yhi // 2) * 8 + (yhi % 2) * 4 + cls
                pairs.append((source, x * 8 + ylo * 4 + yhi))
    return lax.ppermute(a, PLANE, pairs)


def swap_cores(a):
    return lax.ppermute(a, "core", [(0, 1), (1, 0)])


def gather_weights(w_so, w_qkv, w_out, core):
    shard = jnp.concatenate([w_so, w_out, w_qkv.T], 0)
    shard = transpose_classes(shard)
    shards = lax.all_gather(shard, "core", axis=0)
    shards = lax.all_gather(shards, "z", axis=0).reshape(16, 45, D)
    rows = lambda n: ((n, D), BF)
    own_so, own_out, own_qkv, h0, h1, *corners = call(
        compact_kernel,
        [rows(144), rows(144), rows(432), rows(192), rows(192)] + [rows(96)] * 4,
        core, shards, scalars=1,
        scratch=[pltpu.VMEM((144, D), F32), pltpu.VMEM((144, D), F32), pltpu.VMEM((432, D), F32)],
    )
    near = [
        from_neighbour(h0, 1, 0),
        from_neighbour(h1, -1, 0),
        from_neighbour(h0, 0, 1),
        from_neighbour(h1, 0, -1),
    ]
    steps = ((1, 1), (1, -1), (-1, 1), (-1, -1))
    diagonal = [from_neighbour(a, dx, dy) for a, (dx, dy) in zip(corners, steps)]
    swapped = [swap_cores(jnp.concatenate(near, 0)), swap_cores(jnp.concatenate(diagonal, 0))]
    return [own_so, own_out, own_qkv] + near + diagonal + swapped


def body(tokens, qkv, w_so, w_qkv, w_out, factors, cotangent):
    tokens, qkv, cotangent, factors = tokens[0, 0], qkv[0, 0], cotangent[0, 0], factors[0]
    core = lax.axis_index("core").astype(jnp.int32)
    cls = (lax.axis_index("x") % 2) * 2 + lax.axis_index("ylo")
    place = jnp.stack([core, cls.astype(jnp.int32)])
    weights = gather_weights(w_so, w_qkv, w_out, core.reshape(1))

    (mixed_s,) = call(spatial_forward_kernel, [((ROWS, ATT), BF)], qkv)
    sent = jnp.concatenate([tokens, cotangent, mixed_s], 1).reshape(64, 2, 2 * D + ATT)
    sent = exchange(sent).reshape(ROWS, 2 * D + ATT)

    hidden_grad, d_mixed, factor_part, out_keep, out_send = call(
        temporal_kernel,
        [((ROWS, D), BF), ((ROWS, ATT), BF), ((4, D), F32), ((ATT, ATT), F32), ((ATT, ATT), BF)],
        place, sent[:, :D], sent[:, D : 2 * D], sent[:, 2 * D :], factors, *weights,
        scalars=1, remote=len(weights), flops=4 * 10**9,
        scratch=[
            pltpu.VMEM((3 * ATT, D), BF),
            pltpu.VMEM((ATT, D), BF),
            pltpu.VMEM((ATT, D), BF),
            pltpu.SemaphoreType.DMA((48,)),
        ],
    )

    out_part = (out_keep + swap_cores(out_send).astype(F32)).astype(BF)
    packed = jnp.concatenate(
        [
            jnp.concatenate([hidden_grad, d_mixed], 1).reshape(64, 2, D + ATT),
            out_part.reshape(64, 2, 9 * ATT // 2),
            jnp.broadcast_to(factor_part.astype(BF).reshape(1, 2, 2, D), (32, 2, 2, D)).reshape(64, 2, D),
            jnp.zeros((64, 2, 32), BF),
        ],
        2,
    )
    back = exchange(packed)
    rows = back[:, :, : D + ATT].reshape(ROWS, D + ATT)
    token_grad = rows[:, :D]
    (qkv_grad,) = call(spatial_backward_kernel, [((ROWS, 3 * ATT), BF)], qkv, rows[:, D:])

    out_part = back[:, :, D + ATT : D + ATT + 9 * ATT // 2].astype(F32)
    out_part = jnp.sum(out_part.reshape(32, 2, 2, 9 * ATT // 2), 0)
    out_part = jnp.broadcast_to(out_part.reshape(1, 2, 9 * ATT), (8, 2, 9 * ATT))
    out_part = jnp.sum(lax.all_to_all(out_part, DP, 0, 0, tiled=True), 0)
    out_grad = out_part.reshape(2, 9, ATT).transpose(1, 0, 2).reshape(9, D)

    mine = jnp.sum(back[:, :, D + ATT + 9 * ATT // 2 :][:, :, :D].astype(F32), 0)
    other = swap_cores(mine)
    factor_grad = jnp.where(core == 0, jnp.stack([mine, other]), jnp.stack([other, mine]))
    return token_grad[None, None], qkv_grad[None, None], factor_grad.reshape(1, 4, D), out_grad


def solution(mesh):
    fine = Mesh(mesh.devices.reshape(4, 2, 4, 8, 2), DP + SEQ)
    frames = P(DP, SEQ, None, None)
    return jax.shard_map(
        body,
        mesh=fine,
        in_specs=(
            frames,
            frames,
            P(SEQ, None),
            P(None, SEQ),
            P(SEQ, None),
            P(DP, None, None),
            frames,
        ),
        out_specs=(frames, frames, P(DP, None, None), P(SEQ, None)),
        check_vma=False,
    )
```

```python
import math

import jax
import jax.numpy as jnp
from jax import lax
from jax.experimental import pallas as pl
from jax.experimental.pallas import tpu as pltpu
from jax.sharding import Mesh
from jax.sharding import PartitionSpec as P

D = 1152
HEADS = 8
HS = 72
ATT = 576
ROWS = 128
SCALE = 1.0 / math.sqrt(HS)
SEQ = ("yhi", "z", "core")
CHIPS = ("yhi", "z")
DP = ("x", "ylo")
BF = jnp.bfloat16
F32 = jnp.float32


def nn(a, b):
    return lax.dot_general(a, b, (((1,), (0,)), ((), ())), preferred_element_type=F32)


def nt(a, b):
    return lax.dot_general(a, b, (((1,), (1,)), ((), ())), preferred_element_type=F32)


def tn(a, b):
    return lax.dot_general(a, b, (((0,), (0,)), ((), ())), preferred_element_type=F32)


def head_masks():
    head = lax.broadcasted_iota(jnp.int32, (ROWS, ATT), 1) // HS
    return [head == h for h in range(HEADS)]


def stack_heads(masks, a):
    zero = jnp.zeros_like(a)
    return jnp.concatenate([jnp.where(m, a, zero) for m in masks], 0)


def pick_heads(masks, a):
    out = a[:ROWS]
    for h in range(1, HEADS):
        out = jnp.where(masks[h], a[h * ROWS : (h + 1) * ROWS], out)
    return out


def softmax_rows(scores):
    top = jnp.max(scores, -1, keepdims=True)
    weights = jnp.exp(scores - top)
    return weights / jnp.sum(weights, -1, keepdims=True)


def attend(masks, q, k, v, same):
    q_stack = stack_heads(masks, q)
    scores = nt(q_stack, k) * SCALE
    if same is not None:
        scores = jnp.where(same, scores, -1e30)
    probs = softmax_rows(scores)
    probs_b = probs.astype(BF)
    mixed = pick_heads(masks, nn(probs_b, v)).astype(BF)
    return q_stack, probs, probs_b, mixed


def attend_back(masks, q_stack, k, v, probs, probs_b, d_mixed):
    d_stack = stack_heads(masks, d_mixed)
    d_probs = nt(d_stack, v).astype(BF).astype(F32)
    d_v = tn(probs_b, d_stack)
    d_scores = probs * (d_probs - jnp.sum(d_probs * probs, -1, keepdims=True)) * SCALE
    d_scores = d_scores.astype(BF)
    d_q = pick_heads(masks, nn(d_scores, k))
    d_k = tn(d_scores, q_stack)
    return d_q.astype(BF), d_k.astype(BF), d_v.astype(BF)


def spatial_forward_kernel(qkv, mixed):
    q, k, v = qkv[:, :ATT], qkv[:, ATT : 2 * ATT], qkv[:, 2 * ATT :]
    mixed[...] = attend(head_masks(), q, k, v, None)[3]


def spatial_backward_kernel(qkv, d_mixed, out):
    q, k, v = qkv[:, :ATT], qkv[:, ATT : 2 * ATT], qkv[:, 2 * ATT :]
    masks = head_masks()
    q_stack, probs, probs_b, _ = attend(masks, q, k, v, None)
    d_q, d_k, d_v = attend_back(masks, q_stack, k, v, probs, probs_b, d_mixed[...])
    out[:, :ATT] = d_q
    out[:, ATT : 2 * ATT] = d_k
    out[:, 2 * ATT :] = d_v


def compact_kernel(place, mine, other, own_so, own_out, own_qkv, part, slots, so, out, qkv):
    core, z = place[0], place[2]
    for i in range(4):
        slots[core * 4 + i] = mine[i]
        slots[(1 - core) * 4 + i] = other[i]
    for target in range(8):
        delta = (target - z) & 7
        slot = jnp.where(delta <= 4, delta, 12 - delta)
        for c in range(2):
            i = target * 2 + c
            shard = slots[slot, c].astype(F32)
            so[9 * i : 9 * i + 9, :] = shard[:9]
            out[9 * i : 9 * i + 9, :] = shard[9:18]
            qkv[27 * i : 27 * i + 27, :] = shard[18:]
    own_so[...] = so[...].astype(BF)
    own_out[...] = out[...].astype(BF)
    own_qkv[...] = qkv[...].astype(BF)
    at_qkv = pl.multiple_of(core * 208, 16)
    at = pl.multiple_of(core * 64, 16)
    part[0:224, :] = own_qkv[pl.ds(at_qkv, 224), :]
    part[224:304, :] = own_so[pl.ds(at, 80), :]
    part[304:384, :] = own_out[pl.ds(at, 80), :]


SECTIONS = ((0, 0, 224), (1, 224, 304), (2, 304, 384))
BLOCK = (432, 144, 144)
STEP = (208, 64, 64)


def part_copies(ref, half, block, targets):
    copies = []
    for section, first, last in SECTIONS:
        first = first + 16 * half
        row = first - SECTIONS[section][1] + STEP[section] * half
        to = pl.multiple_of(block * BLOCK[section] + row, 16)
        rows = last - first
        copies.append((ref.at[pl.ds(first, rows)], targets[section].at[pl.ds(to, rows)]))
    return copies


def assemble(place, own, near, swapped, targets, sems):
    for me in range(2):

        @pl.when(place[0] == me)
        def _():
            cls = place[1]
            pairs = []
            for section, ref in enumerate(own):
                to = pl.multiple_of(cls * BLOCK[section], 16)
                pairs.append((ref, targets[section].at[pl.ds(to, BLOCK[section])]))
            for flip, ref, other in zip((2, 1, 3), near, swapped):
                pairs += part_copies(ref, me, cls ^ flip, targets)
                pairs += part_copies(other, 1 - me, cls ^ flip, targets)
            copies = [pltpu.make_async_copy(a, z, sems.at[i]) for i, (a, z) in enumerate(pairs)]
            for copy in copies:
                copy.start()
            for copy in copies:
                copy.wait()


def temporal_kernel(
    place, sent, factors, own_qkv, own_so, own_out, b, c, d, other_b, other_c, other_d,
    packed, out_keep, out_send, w_qkv, w_so, w_out, sems,
):
    assemble(
        place, (own_qkv, own_so, own_out), (b, c, d), (other_b, other_c, other_d),
        (w_qkv, w_so, w_out), sems,
    )
    tokens, cotangent, mixed_s = sent[:, :D], sent[:, D : 2 * D], sent[:, 2 * D :]
    gate_s, shift, scale, gate_t = (factors[i : i + 1, :] for i in range(4))
    project = nn(mixed_s, w_so[...])
    hidden = (tokens.astype(F32) + gate_s * project).astype(BF).astype(F32)
    centered = hidden - jnp.mean(hidden, -1, keepdims=True)
    inverse = lax.rsqrt(jnp.mean(centered * centered, -1, keepdims=True) + 1e-06)
    unit = centered * inverse
    normed = (unit * (1.0 + scale) + shift).astype(BF)
    wq, wk, wv = (w_qkv[i * ATT : (i + 1) * ATT, :] for i in range(3))
    q, k, v = (nt(normed, w).astype(BF) for w in (wq, wk, wv))

    masks = head_masks()
    row = lax.broadcasted_iota(jnp.int32, (HEADS * ROWS, ROWS), 0)
    col = lax.broadcasted_iota(jnp.int32, (HEADS * ROWS, ROWS), 1)
    same = ((row ^ col) & 1) == 0
    q_stack, probs, probs_b, mixed = attend(masks, q, k, v, same)

    cot = cotangent.astype(F32)
    scaled = (cot * gate_t).astype(BF)
    left, right = scaled[:, :ATT], scaled[:, ATT:]
    first = place[0] == 0
    out_keep[...] = tn(mixed, jnp.where(first, left, right))
    out_send[...] = tn(mixed, jnp.where(first, right, left)).astype(BF)

    d_mixed = nt(scaled, w_out[...]).astype(BF)
    d_q, d_k, d_v = attend_back(masks, q_stack, k, v, probs, probs_b, d_mixed)
    d_normed = (nn(d_q, wq) + nn(d_k, wk) + nn(d_v, wv)).astype(BF).astype(F32)
    d_unit = d_normed * (1.0 + scale)
    d_hidden = inverse * (
        d_unit
        - jnp.mean(d_unit, -1, keepdims=True)
        - unit * jnp.mean(d_unit * unit, -1, keepdims=True)
    )
    grad = (cot + d_hidden).astype(BF)
    packed[:, :D] = grad
    grad = grad.astype(F32)
    d_mixed_s = nt((grad * gate_s).astype(BF), w_so[...]).astype(BF)
    packed[:, D : D + 640] = jnp.concatenate([d_mixed_s, jnp.zeros((ROWS, 64), BF)], 1)
    project_t = nn(mixed, w_out[...])
    factor_grads = [
        jnp.sum(grad * project, 0, keepdims=True),
        jnp.sum(d_normed, 0, keepdims=True),
        jnp.sum(d_normed * unit, 0, keepdims=True),
        jnp.sum(cot * project_t, 0, keepdims=True),
    ]
    tile = jnp.concatenate(factor_grads * 4, 0).astype(BF)
    for i in range(8):
        packed[16 * i : 16 * i + 16, D + 640 :] = tile


def call(kernel, outs, *args, scalars=0, remote=0, scratch=(), flops=10**9):
    vmem = pl.BlockSpec(memory_space=pltpu.VMEM)
    specs = [pl.BlockSpec(memory_space=pltpu.SMEM)] * scalars
    specs += [vmem] * (len(args) - scalars - remote)
    specs += [pl.BlockSpec(memory_space=pl.ANY)] * remote
    return pl.pallas_call(
        kernel,
        out_shape=[jax.ShapeDtypeStruct(s, d) for s, d in outs],
        in_specs=specs,
        out_specs=[vmem] * len(outs),
        scratch_shapes=list(scratch),
        compiler_params=pltpu.CompilerParams(vmem_limit_bytes=48 * 2**20),
        cost_estimate=pl.CostEstimate(flops=flops, bytes_accessed=10**7, transcendentals=10**5),
    )(*args)


def exchange(a):
    return lax.all_to_all(a, SEQ, 0, 0, tiled=True)


AXES = DP + SEQ


def device(x, y, z, core):
    ylo, yhi = y % 2, (y % 8) // 2
    return ((((x % 4) * 2 + ylo) * 4 + yhi) * 8 + z % 8) * 2 + core


def receive(a, source):
    pairs = []
    for x in range(4):
        for y in range(8):
            for z in range(8):
                for core in range(2):
                    pairs.append((device(*source(x, y, z, core), core), device(x, y, z, core)))
    return lax.ppermute(a, AXES, pairs)


def swap_cores(a):
    return lax.ppermute(a, "core", [(0, 1), (1, 0)])


OFFSETS = ((0, 1, 2, 3), (4, -1, -2, -3))


def shard_source(step):
    def source(x, y, z, core):
        ylo, yhi = y % 2, y // 2
        cls = (x % 2) * 2 + ylo
        return (x // 2) * 2 + yhi // 2, cls * 2 + yhi % 2, z + OFFSETS[core][step]

    return source


def near_source(dx, dy):
    def source(x, y, z, core):
        sign = 1 - 2 * core
        return x + sign * dx, y + sign * dy, z

    return source


def gather_weights(w_so, w_qkv, w_out, place, packed):
    shard = jnp.concatenate([w_so, w_out, w_qkv.T], 0)
    shards = lax.all_gather(shard, "core", axis=0)
    mine = [receive(shards, shard_source(i)) for i in range(4)]
    mine, packed = lax.optimization_barrier((jnp.stack(mine), packed))
    other = swap_cores(mine)
    rows = lambda n: ((n, D), BF)
    own_so, own_out, own_qkv, part = call(
        compact_kernel, [rows(144), rows(144), rows(432), rows(384)], place, mine, other, scalars=1,
        scratch=[
            pltpu.VMEM((8, 2, 45, D), BF),
            pltpu.VMEM((144, D), F32),
            pltpu.VMEM((144, D), F32),
            pltpu.VMEM((432, D), F32),
        ],
    )
    part, packed = lax.optimization_barrier((part, packed))
    near = [receive(part, near_source(dx, dy)) for dx, dy in ((1, 0), (0, 1), (1, 1))]
    return [own_qkv, own_so, own_out] + near + [swap_cores(a) for a in near], packed


def body(tokens, qkv, w_so, w_qkv, w_out, factors, cotangent):
    tokens, qkv, cotangent, factors = tokens[0, 0], qkv[0, 0], cotangent[0, 0], factors[0]
    core = lax.axis_index("core")
    cls = (lax.axis_index("x") % 2) * 2 + lax.axis_index("ylo")
    place = jnp.stack([core, cls, lax.axis_index("z")]).astype(jnp.int32)

    (mixed_s,) = call(spatial_forward_kernel, [((ROWS, ATT), BF)], qkv)
    sent = jnp.concatenate([tokens, cotangent, mixed_s], 1).reshape(64, 2, 2 * D + ATT)
    weights, sent = gather_weights(w_so, w_qkv, w_out, place, sent)
    sent = exchange(sent).reshape(ROWS, 2 * D + ATT)

    packed, out_keep, out_send = call(
        temporal_kernel,
        [((ROWS, 2 * D + 640), BF), ((ATT, ATT), F32), ((ATT, ATT), BF)],
        place, sent, factors, *weights,
        scalars=1, remote=len(weights), flops=4 * 10**9,
        scratch=[
            pltpu.VMEM((3 * ATT, D), BF),
            pltpu.VMEM((ATT, D), BF),
            pltpu.VMEM((ATT, D), BF),
            pltpu.SemaphoreType.DMA((24,)),
        ],
    )

    out_part = (out_keep + swap_cores(out_send).astype(F32)).astype(BF)
    out_part = out_part.reshape(64, 2, 9 * ATT // 2)
    width = 2 * D + 640
    back = exchange(jnp.concatenate([packed.reshape(64, 2, width), out_part], 2))

    out_part = back[:, :, width:].astype(F32).reshape(32, 2, 2, 9 * ATT // 2)
    out_part = jnp.sum(out_part, 0).reshape(1, 2, 9 * ATT)
    out_part = jnp.broadcast_to(out_part, (8, 2, 9 * ATT))
    out_part = jnp.sum(lax.all_to_all(out_part, DP, 0, 0, tiled=True), 0)
    out_grad = out_part.reshape(2, 9, ATT).transpose(1, 0, 2).reshape(9, D)

    rows = back[:, :, : D + ATT].reshape(ROWS, D + ATT)
    token_grad = rows[:, :D]
    (qkv_grad,) = call(spatial_backward_kernel, [((ROWS, 3 * ATT), BF)], qkv, rows[:, D:])

    mine = jnp.sum(back[:, :, D + 640 : width].astype(F32), 0)
    other = swap_cores(mine)
    factor_grad = jnp.where(core == 0, jnp.stack([mine, other]), jnp.stack([other, mine]))
    return token_grad[None, None], qkv_grad[None, None], factor_grad.reshape(1, 4, D), out_grad


def solution(mesh):
    fine = Mesh(mesh.devices.reshape(4, 2, 4, 8, 2), DP + SEQ)
    frames = P(DP, SEQ, None, None)
    return jax.shard_map(
        body,
        mesh=fine,
        in_specs=(
            frames,
            frames,
            P(SEQ, None),
            P(None, SEQ),
            P(SEQ, None),
            P(DP, None, None),
            frames,
        ),
        out_specs=(frames, frames, P(DP, None, None), P(SEQ, None)),
        check_vma=False,
    )
```

```python
import math

import jax
import jax.numpy as jnp
from jax import lax
from jax.experimental import pallas as pl
from jax.experimental.pallas import tpu as pltpu
from jax.sharding import Mesh
from jax.sharding import PartitionSpec as P

D = 1152
HEADS = 8
HS = 72
ATT = 576
ROWS = 128
SCALE = 1.0 / math.sqrt(HS)
SEQ = ("yhi", "z", "core")
CHIPS = ("yhi", "z")
DP = ("x", "ylo")
BF = jnp.bfloat16
F32 = jnp.float32


def nn(a, b):
    return lax.dot_general(a, b, (((1,), (0,)), ((), ())), preferred_element_type=F32)


def nt(a, b):
    return lax.dot_general(a, b, (((1,), (1,)), ((), ())), preferred_element_type=F32)


def tn(a, b):
    return lax.dot_general(a, b, (((0,), (0,)), ((), ())), preferred_element_type=F32)


def head_masks():
    head = lax.broadcasted_iota(jnp.int32, (ROWS, ATT), 1) // HS
    return [head == h for h in range(HEADS)]


def stack_heads(masks, a):
    zero = jnp.zeros_like(a)
    return jnp.concatenate([jnp.where(m, a, zero) for m in masks], 0)


def pick_heads(masks, a):
    out = a[:ROWS]
    for h in range(1, HEADS):
        out = jnp.where(masks[h], a[h * ROWS : (h + 1) * ROWS], out)
    return out


def softmax_rows(scores):
    top = jnp.max(scores, -1, keepdims=True)
    weights = jnp.exp(scores - top)
    return weights / jnp.sum(weights, -1, keepdims=True)


def attend(masks, q, k, v, same):
    q_stack = stack_heads(masks, q)
    scores = nt(q_stack, k) * SCALE
    if same is not None:
        scores = jnp.where(same, scores, -1e30)
    probs = softmax_rows(scores)
    probs_b = probs.astype(BF)
    mixed = pick_heads(masks, nn(probs_b, v)).astype(BF)
    return q_stack, probs, probs_b, mixed


def attend_back(masks, q_stack, k, v, probs, probs_b, d_mixed):
    d_stack = stack_heads(masks, d_mixed)
    d_probs = nt(d_stack, v).astype(BF).astype(F32)
    d_v = tn(probs_b, d_stack)
    d_scores = probs * (d_probs - jnp.sum(d_probs * probs, -1, keepdims=True)) * SCALE
    d_scores = d_scores.astype(BF)
    d_q = pick_heads(masks, nn(d_scores, k))
    d_k = tn(d_scores, q_stack)
    return d_q.astype(BF), d_k.astype(BF), d_v.astype(BF)


def spatial_forward_kernel(qkv, mixed):
    q, k, v = qkv[:, :ATT], qkv[:, ATT : 2 * ATT], qkv[:, 2 * ATT :]
    mixed[...] = attend(head_masks(), q, k, v, None)[3]


def spatial_backward_kernel(qkv, hidden_grad, factors, w_so, out):
    q, k, v = qkv[:, :ATT], qkv[:, ATT : 2 * ATT], qkv[:, 2 * ATT :]
    masks = head_masks()
    gated = (hidden_grad[...].astype(F32) * factors[0:1, :]).astype(BF)
    d_mixed = nt(gated, w_so[...]).astype(BF)
    q_stack, probs, probs_b, _ = attend(masks, q, k, v, None)
    d_q, d_k, d_v = attend_back(masks, q_stack, k, v, probs, probs_b, d_mixed)
    out[:, :ATT] = d_q
    out[:, ATT : 2 * ATT] = d_k
    out[:, 2 * ATT :] = d_v


def compact_kernel(place, mine, other, own_so, own_out, own_qkv, part, slots, so, out, qkv):
    core, z = place[0], place[2]
    for i in range(4):
        slots[core * 4 + i] = mine[i]
        slots[(1 - core) * 4 + i] = other[i]
    for target in range(8):
        delta = (target - z) & 7
        slot = jnp.where(delta <= 4, delta, 12 - delta)
        for c in range(2):
            i = target * 2 + c
            shard = slots[slot, c].astype(F32)
            so[9 * i : 9 * i + 9, :] = shard[:9]
            out[9 * i : 9 * i + 9, :] = shard[9:18]
            qkv[27 * i : 27 * i + 27, :] = shard[18:]
    own_so[...] = so[...].astype(BF)
    own_out[...] = out[...].astype(BF)
    own_qkv[...] = qkv[...].astype(BF)
    at_qkv = pl.multiple_of(core * 208, 16)
    at = pl.multiple_of(core * 64, 16)
    part[0:224, :] = own_qkv[pl.ds(at_qkv, 224), :]
    part[224:304, :] = own_so[pl.ds(at, 80), :]
    part[304:384, :] = own_out[pl.ds(at, 80), :]


SECTIONS = ((0, 0, 224), (1, 224, 304), (2, 304, 384))
BLOCK = (432, 144, 144)
STEP = (208, 64, 64)


def part_copies(ref, half, block, targets):
    copies = []
    for section, first, last in SECTIONS:
        first = first + 16 * half
        row = first - SECTIONS[section][1] + STEP[section] * half
        to = pl.multiple_of(block * BLOCK[section] + row, 16)
        rows = last - first
        copies.append((ref.at[pl.ds(first, rows)], targets[section].at[pl.ds(to, rows)]))
    return copies


def assemble(place, own, near, swapped, targets, sems):
    for me in range(2):

        @pl.when(place[0] == me)
        def _():
            cls = place[1]
            pairs = []
            for section, ref in enumerate(own):
                to = pl.multiple_of(cls * BLOCK[section], 16)
                pairs.append((ref, targets[section].at[pl.ds(to, BLOCK[section])]))
            for flip, ref, other in zip((2, 1, 3), near, swapped):
                pairs += part_copies(ref, me, cls ^ flip, targets)
                pairs += part_copies(other, 1 - me, cls ^ flip, targets)
            copies = [pltpu.make_async_copy(a, z, sems.at[i]) for i, (a, z) in enumerate(pairs)]
            for copy in copies:
                copy.start()
            for copy in copies:
                copy.wait()


def temporal_kernel(
    place, sent, factors, own_qkv, own_so, own_out, b, c, d, other_b, other_c, other_d,
    hidden_grad, factor_grads, out_keep, out_send, w_so, w_qkv, w_out, sems,
):
    assemble(
        place, (own_qkv, own_so, own_out), (b, c, d), (other_b, other_c, other_d),
        (w_qkv, w_so, w_out), sems,
    )
    tokens, cotangent, mixed_s = sent[:, :D], sent[:, D : 2 * D], sent[:, 2 * D :]
    gate_s, shift, scale, gate_t = (factors[i : i + 1, :] for i in range(4))
    project = nn(mixed_s, w_so[...])
    hidden = (tokens.astype(F32) + gate_s * project).astype(BF).astype(F32)
    centered = hidden - jnp.mean(hidden, -1, keepdims=True)
    inverse = lax.rsqrt(jnp.mean(centered * centered, -1, keepdims=True) + 1e-06)
    unit = centered * inverse
    normed = (unit * (1.0 + scale) + shift).astype(BF)
    wq, wk, wv = (w_qkv[i * ATT : (i + 1) * ATT, :] for i in range(3))
    q, k, v = (nt(normed, w).astype(BF) for w in (wq, wk, wv))

    masks = head_masks()
    row = lax.broadcasted_iota(jnp.int32, (HEADS * ROWS, ROWS), 0)
    col = lax.broadcasted_iota(jnp.int32, (HEADS * ROWS, ROWS), 1)
    same = ((row ^ col) & 1) == 0
    q_stack, probs, probs_b, mixed = attend(masks, q, k, v, same)

    cot = cotangent.astype(F32)
    scaled = (cot * gate_t).astype(BF)
    left, right = scaled[:, :ATT], scaled[:, ATT:]
    first = place[0] == 0
    out_keep[...] = tn(mixed, jnp.where(first, left, right))
    out_send[...] = tn(mixed, jnp.where(first, right, left)).astype(BF)

    d_mixed = nt(scaled, w_out[...]).astype(BF)
    d_q, d_k, d_v = attend_back(masks, q_stack, k, v, probs, probs_b, d_mixed)
    d_normed = (nn(d_q, wq) + nn(d_k, wk) + nn(d_v, wv)).astype(BF).astype(F32)
    d_unit = d_normed * (1.0 + scale)
    d_hidden = inverse * (
        d_unit
        - jnp.mean(d_unit, -1, keepdims=True)
        - unit * jnp.mean(d_unit * unit, -1, keepdims=True)
    )
    grad = (cot + d_hidden).astype(BF)
    hidden_grad[...] = grad
    grad = grad.astype(F32)
    project_t = nn(mixed, w_out[...])
    factor_grads[0:1, :] = jnp.sum(grad * project, 0, keepdims=True)
    factor_grads[1:2, :] = jnp.sum(d_normed, 0, keepdims=True)
    factor_grads[2:3, :] = jnp.sum(d_normed * unit, 0, keepdims=True)
    factor_grads[3:4, :] = jnp.sum(cot * project_t, 0, keepdims=True)


def call(kernel, outs, *args, scalars=0, remote=0, scratch=(), flops=10**9):
    vmem = pl.BlockSpec(memory_space=pltpu.VMEM)
    specs = [pl.BlockSpec(memory_space=pltpu.SMEM)] * scalars
    specs += [vmem] * (len(args) - scalars - remote)
    specs += [pl.BlockSpec(memory_space=pl.ANY)] * remote
    return pl.pallas_call(
        kernel,
        out_shape=[jax.ShapeDtypeStruct(s, d) for s, d in outs],
        in_specs=specs,
        out_specs=[vmem] * len(outs),
        scratch_shapes=list(scratch),
        compiler_params=pltpu.CompilerParams(vmem_limit_bytes=48 * 2**20),
        cost_estimate=pl.CostEstimate(flops=flops, bytes_accessed=10**7, transcendentals=10**5),
    )(*args)


def exchange(a):
    return lax.all_to_all(a, SEQ, 0, 0, tiled=True)


AXES = DP + SEQ


def device(x, y, z, core):
    ylo, yhi = y % 2, (y % 8) // 2
    return ((((x % 4) * 2 + ylo) * 4 + yhi) * 8 + z % 8) * 2 + core


def receive(a, source):
    pairs = []
    for x in range(4):
        for y in range(8):
            for z in range(8):
                for core in range(2):
                    pairs.append((device(*source(x, y, z, core), core), device(x, y, z, core)))
    return lax.ppermute(a, AXES, pairs)


def swap_cores(a):
    return lax.ppermute(a, "core", [(0, 1), (1, 0)])


OFFSETS = ((0, 1, 2, 3), (4, -1, -2, -3))


def class_source(x, y, z, core):
    ylo, yhi = y % 2, y // 2
    cls = (x % 2) * 2 + ylo
    return (x // 2) * 2 + yhi // 2, cls * 2 + yhi % 2, z


def line_source(step):
    return lambda x, y, z, core: (x, y, z + OFFSETS[core][step])


def near_source(dx, dy):
    def source(x, y, z, core):
        sign = 1 - 2 * core
        return x + sign * dx, y + sign * dy, z

    return source


def gather_weights(w_so, w_qkv, w_out, place, sent):
    shard = receive(jnp.concatenate([w_so, w_out, w_qkv.T], 0), class_source)
    shards = lax.all_gather(shard, "core", axis=0)
    mine = [receive(shards, line_source(i)) for i in range(4)]
    mine, sent = lax.optimization_barrier((jnp.stack(mine), exchange(sent)))
    other = swap_cores(mine)
    rows = lambda n: ((n, D), BF)
    own_so, own_out, own_qkv, part = call(
        compact_kernel, [rows(144), rows(144), rows(432), rows(384)], place, mine, other, scalars=1,
        scratch=[
            pltpu.VMEM((8, 2, 45, D), BF),
            pltpu.VMEM((144, D), F32),
            pltpu.VMEM((144, D), F32),
            pltpu.VMEM((432, D), F32),
        ],
    )
    near = [receive(part, near_source(dx, dy)) for dx, dy in ((1, 0), (0, 1), (1, 1))]
    return [own_qkv, own_so, own_out] + near + [swap_cores(a) for a in near], sent


def body(tokens, qkv, w_so, w_qkv, w_out, factors, cotangent):
    tokens, qkv, cotangent, factors = tokens[0, 0], qkv[0, 0], cotangent[0, 0], factors[0]
    core, yhi = lax.axis_index("core"), lax.axis_index("yhi")
    cls = (lax.axis_index("x") % 2) * 2 + lax.axis_index("ylo")
    place = jnp.stack([core, cls, lax.axis_index("z")]).astype(jnp.int32)

    (mixed_s,) = call(spatial_forward_kernel, [((ROWS, ATT), BF)], qkv)
    sent = jnp.concatenate([tokens, cotangent, mixed_s], 1).reshape(64, 2, 2 * D + ATT)
    weights, sent = gather_weights(w_so, w_qkv, w_out, place, sent)
    sent = sent.reshape(ROWS, 2 * D + ATT)

    hidden_grad, factor_part, out_keep, out_send, w_so = call(
        temporal_kernel,
        [((ROWS, D), BF), ((4, D), F32), ((ATT, ATT), F32), ((ATT, ATT), BF), ((ATT, D), BF)],
        place, sent, factors, *weights,
        scalars=1, remote=len(weights), flops=4 * 10**9,
        scratch=[
            pltpu.VMEM((3 * ATT, D), BF),
            pltpu.VMEM((ATT, D), BF),
            pltpu.SemaphoreType.DMA((24,)),
        ],
    )

    out_part = (out_keep + swap_cores(out_send).astype(F32)).astype(BF)
    half = 9 * ATT // 2
    factor_part = factor_part.astype(BF).reshape(1, 2, 1, 2, 2, D // 2)
    factor_part = jnp.broadcast_to(factor_part, (2, 2, 8, 2, 2, D // 2)).reshape(64, 2, D // 2)
    packed = [hidden_grad.reshape(64, 2, D), out_part.reshape(64, 2, half), factor_part]
    back = exchange(jnp.concatenate(packed, 2))

    out_part = back[:, :, D : D + half].astype(F32).reshape(32, 2, 2, half)
    out_part = jnp.sum(out_part, 0).reshape(1, 2, 9 * ATT)
    out_part = jnp.broadcast_to(out_part, (8, 2, 9 * ATT))
    out_part = jnp.sum(lax.all_to_all(out_part, DP, 0, 0, tiled=True), 0)
    out_grad = out_part.reshape(2, 9, ATT).transpose(1, 0, 2).reshape(9, D)

    token_grad = back[:, :, :D].reshape(ROWS, D)
    (qkv_grad,) = call(
        spatial_backward_kernel, [((ROWS, 3 * ATT), BF)], qkv, token_grad, factors, w_so
    )

    mine = jnp.sum(back[:, :, D + half :].astype(F32), 0).reshape(1, D)
    other = swap_cores(mine)
    rows = jnp.where(core == 0, jnp.concatenate([mine, other]), jnp.concatenate([other, mine]))
    other = lax.ppermute(rows, "yhi", [(0, 1), (1, 0), (2, 3), (3, 2)])
    low = yhi % 2 == 0
    factor_grad = jnp.where(low, jnp.concatenate([rows, other]), jnp.concatenate([other, rows]))
    return token_grad[None, None], qkv_grad[None, None], factor_grad[None], out_grad


def solution(mesh):
    fine = Mesh(mesh.devices.reshape(4, 2, 4, 8, 2), DP + SEQ)
    frames = P(DP, SEQ, None, None)
    return jax.shard_map(
        body,
        mesh=fine,
        in_specs=(
            frames,
            frames,
            P(SEQ, None),
            P(None, SEQ),
            P(SEQ, None),
            P(DP, None, None),
            frames,
        ),
        out_specs=(frames, frames, P(DP, None, None), P(SEQ, None)),
        check_vma=False,
    )
```

```python
import math

import jax
import jax.numpy as jnp
from jax import lax
from jax.experimental import pallas as pl
from jax.experimental.pallas import tpu as pltpu
from jax.sharding import Mesh
from jax.sharding import PartitionSpec as P

D = 1152
HEADS = 8
HS = 72
ATT = 576
ROWS = 128
SCALE = 1.0 / math.sqrt(HS)
SEQ = ("yhi", "z", "core")
CHIPS = ("yhi", "z")
DP = ("x", "ylo")
BF = jnp.bfloat16
F32 = jnp.float32


def nn(a, b):
    return lax.dot_general(a, b, (((1,), (0,)), ((), ())), preferred_element_type=F32)


def nt(a, b):
    return lax.dot_general(a, b, (((1,), (1,)), ((), ())), preferred_element_type=F32)


def tn(a, b):
    return lax.dot_general(a, b, (((0,), (0,)), ((), ())), preferred_element_type=F32)


def head_masks():
    head = lax.broadcasted_iota(jnp.int32, (ROWS, ATT), 1) // HS
    return [head == h for h in range(HEADS)]


def stack_heads(masks, a):
    zero = jnp.zeros_like(a)
    return jnp.concatenate([jnp.where(m, a, zero) for m in masks], 0)


def pick_heads(masks, a):
    out = a[:ROWS]
    for h in range(1, HEADS):
        out = jnp.where(masks[h], a[h * ROWS : (h + 1) * ROWS], out)
    return out


def softmax_rows(scores):
    top = jnp.max(scores, -1, keepdims=True)
    weights = jnp.exp(scores - top)
    return weights / jnp.sum(weights, -1, keepdims=True)


def attend(masks, q, k, v, same):
    q_stack = stack_heads(masks, q)
    scores = nt(q_stack, k) * SCALE
    if same is not None:
        scores = jnp.where(same, scores, -1e30)
    probs = softmax_rows(scores)
    probs_b = probs.astype(BF)
    mixed = pick_heads(masks, nn(probs_b, v)).astype(BF)
    return q_stack, probs, probs_b, mixed


def attend_back(masks, q_stack, k, v, probs, probs_b, d_mixed):
    d_stack = stack_heads(masks, d_mixed)
    d_probs = nt(d_stack, v).astype(BF).astype(F32)
    d_v = tn(probs_b, d_stack)
    d_scores = probs * (d_probs - jnp.sum(d_probs * probs, -1, keepdims=True)) * SCALE
    d_scores = d_scores.astype(BF)
    d_q = pick_heads(masks, nn(d_scores, k))
    d_k = tn(d_scores, q_stack)
    return d_q.astype(BF), d_k.astype(BF), d_v.astype(BF)


def spatial_forward_kernel(qkv, mixed):
    q, k, v = qkv[:, :ATT], qkv[:, ATT : 2 * ATT], qkv[:, 2 * ATT :]
    mixed[...] = attend(head_masks(), q, k, v, None)[3]


def spatial_backward_kernel(qkv, hidden_grad, factors, w_so, out):
    q, k, v = qkv[:, :ATT], qkv[:, ATT : 2 * ATT], qkv[:, 2 * ATT :]
    masks = head_masks()
    gated = (hidden_grad[...].astype(F32) * factors[0:1, :]).astype(BF)
    d_mixed = nt(gated, w_so[...]).astype(BF)
    q_stack, probs, probs_b, _ = attend(masks, q, k, v, None)
    d_q, d_k, d_v = attend_back(masks, q_stack, k, v, probs, probs_b, d_mixed)
    out[:, :ATT] = d_q
    out[:, ATT : 2 * ATT] = d_k
    out[:, 2 * ATT :] = d_v


def compact_kernel(place, mine, other, own_so, own_out, own_qkv, part, slots, so, out, qkv):
    core, z = place[0], place[2]
    for i in range(4):
        slots[core * 4 + i] = mine[i]
        slots[(1 - core) * 4 + i] = other[i]
    for target in range(8):
        delta = (target - z) & 7
        slot = jnp.where(delta < 2, 1 - delta, delta)
        slot = jnp.where(delta == 4, 5, jnp.where(delta == 7, 4, slot))
        slot = jnp.where(delta == 5, 7, slot)
        for c in range(2):
            i = target * 2 + c
            shard = slots[slot, c].astype(F32)
            so[9 * i : 9 * i + 9, :] = shard[:9]
            out[9 * i : 9 * i + 9, :] = shard[9:18]
            qkv[27 * i : 27 * i + 27, :] = shard[18:]
    own_so[...] = so[...].astype(BF)
    own_out[...] = out[...].astype(BF)
    own_qkv[...] = qkv[...].astype(BF)
    at_qkv = pl.multiple_of(core * 208, 16)
    at = pl.multiple_of(core * 64, 16)
    part[0:224, :] = own_qkv[pl.ds(at_qkv, 224), :]
    part[224:304, :] = own_so[pl.ds(at, 80), :]
    part[304:384, :] = own_out[pl.ds(at, 80), :]


SECTIONS = ((0, 0, 224), (1, 224, 304), (2, 304, 384))
BLOCK = (432, 144, 144)
STEP = (208, 64, 64)


def part_copies(ref, half, block, targets):
    copies = []
    for section, first, last in SECTIONS:
        first = first + 16 * half
        row = first - SECTIONS[section][1] + STEP[section] * half
        to = pl.multiple_of(block * BLOCK[section] + row, 16)
        rows = last - first
        copies.append((ref.at[pl.ds(first, rows)], targets[section].at[pl.ds(to, rows)]))
    return copies


def assemble(place, own, near, swapped, targets, sems):
    for me in range(2):

        @pl.when(place[0] == me)
        def _():
            cls = place[1]
            pairs = []
            for section, ref in enumerate(own):
                to = pl.multiple_of(cls * BLOCK[section], 16)
                pairs.append((ref, targets[section].at[pl.ds(to, BLOCK[section])]))
            for flip, ref, other in zip((2, 1, 3), near, swapped):
                pairs += part_copies(ref, me, cls ^ flip, targets)
                pairs += part_copies(other, 1 - me, cls ^ flip, targets)
            copies = [pltpu.make_async_copy(a, z, sems.at[i]) for i, (a, z) in enumerate(pairs)]
            for copy in copies:
                copy.start()
            for copy in copies:
                copy.wait()


def temporal_forward_kernel(
    place, sent, factors, own_qkv, own_so, own_out, b, c, d, other_b, other_c, other_d,
    out_keep, out_send, w_so, w_out, w_qkv, q_out, k_out, v_out, probs_out, mixed_out,
    unit_out, inverse_out, project_out, sems,
):
    assemble(
        place, (own_qkv, own_so, own_out), (b, c, d), (other_b, other_c, other_d),
        (w_qkv, w_so, w_out), sems,
    )
    tokens, cotangent, mixed_s = sent[:, :D], sent[:, D : 2 * D], sent[:, 2 * D :]
    gate_s, shift, scale, gate_t = (factors[i : i + 1, :] for i in range(4))
    project = nn(mixed_s, w_so[...])
    project_out[...] = project
    hidden = (tokens.astype(F32) + gate_s * project).astype(BF).astype(F32)
    centered = hidden - jnp.mean(hidden, -1, keepdims=True)
    inverse = lax.rsqrt(jnp.mean(centered * centered, -1, keepdims=True) + 1e-06)
    inverse_out[...] = jnp.broadcast_to(inverse, (ROWS, 128))
    unit = centered * inverse
    unit_out[...] = unit
    normed = (unit * (1.0 + scale) + shift).astype(BF)
    q, k, v = (nt(normed, w_qkv[i * ATT : (i + 1) * ATT, :]).astype(BF) for i in range(3))
    q_out[...], k_out[...], v_out[...] = q, k, v

    row = lax.broadcasted_iota(jnp.int32, (HEADS * ROWS, ROWS), 0)
    col = lax.broadcasted_iota(jnp.int32, (HEADS * ROWS, ROWS), 1)
    same = ((row ^ col) & 1) == 0
    _, probs, _, mixed = attend(head_masks(), q, k, v, same)
    probs_out[...] = probs
    mixed_out[...] = mixed

    scaled = (cotangent.astype(F32) * gate_t).astype(BF)
    left, right = scaled[:, :ATT], scaled[:, ATT:]
    first = place[0] == 0
    out_keep[...] = tn(mixed, jnp.where(first, left, right))
    out_send[...] = tn(mixed, jnp.where(first, right, left)).astype(BF)


def temporal_backward_kernel(
    sent, factors, w_so, w_out, w_qkv, q, k, v, probs, mixed, unit, inverse, project, packed
):
    scale, gate_t = factors[2:3, :], factors[3:4, :]
    cot = sent[:, D : 2 * D].astype(F32)
    scaled = (cot * gate_t).astype(BF)
    masks = head_masks()
    q, k, v, probs = q[...], k[...], v[...], probs[...]
    d_mixed = nt(scaled, w_out[...]).astype(BF)
    q_stack = stack_heads(masks, q)
    d_q, d_k, d_v = attend_back(masks, q_stack, k, v, probs, probs.astype(BF), d_mixed)
    wq, wk, wv = (w_qkv[i * ATT : (i + 1) * ATT, :] for i in range(3))
    d_normed = (nn(d_q, wq) + nn(d_k, wk) + nn(d_v, wv)).astype(BF).astype(F32)
    unit = unit[...]
    d_unit = d_normed * (1.0 + scale)
    d_hidden = inverse[:, 0:1] * (
        d_unit
        - jnp.mean(d_unit, -1, keepdims=True)
        - unit * jnp.mean(d_unit * unit, -1, keepdims=True)
    )
    grad = (cot + d_hidden).astype(BF)
    packed[:, :D] = grad
    project_t = nn(mixed[...], w_out[...])
    factor_grads = (
        jnp.sum(grad.astype(F32) * project[...], 0, keepdims=True),
        jnp.sum(d_normed, 0, keepdims=True),
        jnp.sum(d_normed * unit, 0, keepdims=True),
        jnp.sum(cot * project_t, 0, keepdims=True),
    )
    zeros = jnp.zeros((16, 64), BF)
    for parity in range(2):
        rows = [
            factor_grads[2 * parity + core][:, part * ATT : part * ATT + ATT]
            for core in range(2)
            for part in range(2)
        ]
        tile = jnp.concatenate([jnp.concatenate(rows * 4, 0).astype(BF), zeros], 1)
        for yhi in (parity, parity + 2):
            packed[32 * yhi : 32 * yhi + 16, D:] = tile
            packed[32 * yhi + 16 : 32 * yhi + 32, D:] = tile


def call(kernel, outs, *args, scalars=0, remote=0, scratch=(), flops=10**9):
    vmem = pl.BlockSpec(memory_space=pltpu.VMEM)
    specs = [pl.BlockSpec(memory_space=pltpu.SMEM)] * scalars
    specs += [vmem] * (len(args) - scalars - remote)
    specs += [pl.BlockSpec(memory_space=pl.ANY)] * remote
    return pl.pallas_call(
        kernel,
        out_shape=[jax.ShapeDtypeStruct(s, d) for s, d in outs],
        in_specs=specs,
        out_specs=[vmem] * len(outs),
        scratch_shapes=list(scratch),
        compiler_params=pltpu.CompilerParams(vmem_limit_bytes=32 * 2**20),
        cost_estimate=pl.CostEstimate(flops=flops, bytes_accessed=10**7, transcendentals=10**5),
    )(*args)


def exchange(a):
    return lax.all_to_all(a, SEQ, 0, 0, tiled=True)


AXES = DP + SEQ


def device(x, y, z, core):
    ylo, yhi = y % 2, (y % 8) // 2
    return ((((x % 4) * 2 + ylo) * 4 + yhi) * 8 + z % 8) * 2 + core


def receive(a, source):
    pairs = []
    for x in range(4):
        for y in range(8):
            for z in range(8):
                for core in range(2):
                    pairs.append((device(*source(x, y, z, core), core), device(x, y, z, core)))
    return lax.ppermute(a, AXES, pairs)


def swap_cores(a):
    return lax.ppermute(a, "core", [(0, 1), (1, 0)])


OFFSETS = ((1, 0, 2, 3), (-1, 4, -2, -3))


def class_source(x, y, z, core):
    ylo, yhi = y % 2, y // 2
    cls = (x % 2) * 2 + ylo
    return (x // 2) * 2 + yhi // 2, cls * 2 + yhi % 2, z


def line_source(step):
    return lambda x, y, z, core: (x, y, z + OFFSETS[core][step])


def near_source(dx, dy):
    def source(x, y, z, core):
        sign = 1 - 2 * core
        return x + sign * dx, y + sign * dy, z

    return source


def gather_weights(w_so, w_qkv, w_out, place, sent):
    shard = receive(jnp.concatenate([w_so, w_out, w_qkv.T], 0), class_source)
    shards = lax.all_gather(shard, "core", axis=0)
    mine = [receive(shards, line_source(i)) for i in range(4)]
    mine[0], sent = lax.optimization_barrier((mine[0], sent))
    mine, sent = lax.optimization_barrier((jnp.stack(mine), exchange(sent)))
    other = swap_cores(mine)
    rows = lambda n: ((n, D), BF)
    own_so, own_out, own_qkv, part = call(
        compact_kernel, [rows(144), rows(144), rows(432), rows(384)], place, mine, other, scalars=1,
        scratch=[
            pltpu.VMEM((8, 2, 45, D), BF),
            pltpu.VMEM((144, D), F32),
            pltpu.VMEM((144, D), F32),
            pltpu.VMEM((432, D), F32),
        ],
    )
    near = [receive(part, near_source(dx, dy)) for dx, dy in ((1, 0), (0, 1), (1, 1))]
    return [own_qkv, own_so, own_out] + near + [swap_cores(a) for a in near], sent


def body(tokens, qkv, w_so, w_qkv, w_out, factors, cotangent):
    tokens, qkv, cotangent, factors = tokens[0, 0], qkv[0, 0], cotangent[0, 0], factors[0]
    core, yhi = lax.axis_index("core"), lax.axis_index("yhi")
    cls = (lax.axis_index("x") % 2) * 2 + lax.axis_index("ylo")
    place = jnp.stack([core, cls, lax.axis_index("z")]).astype(jnp.int32)

    (mixed_s,) = call(spatial_forward_kernel, [((ROWS, ATT), BF)], qkv)
    sent = jnp.concatenate([tokens, cotangent, mixed_s], 1).reshape(64, 2, 2 * D + ATT)
    weights, sent = gather_weights(w_so, w_qkv, w_out, place, sent)
    sent = sent.reshape(ROWS, 2 * D + ATT)

    rows = lambda n, kind=BF: ((ROWS, n), kind)
    out_keep, out_send, *saved = call(
        temporal_forward_kernel,
        [
            ((ATT, ATT), F32), ((ATT, ATT), BF), ((ATT, D), BF), ((ATT, D), BF), ((3 * ATT, D), BF),
            rows(ATT), rows(ATT), rows(ATT), ((HEADS * ROWS, ROWS), F32), rows(ATT),
            rows(D, F32), rows(128, F32), rows(D, F32),
        ],
        place, sent, factors, *weights,
        scalars=1, remote=len(weights), flops=4 * 10**9,
        scratch=[pltpu.SemaphoreType.DMA((24,))],
    )
    w_so = saved[0]
    out_other = swap_cores(out_send)
    (packed,) = call(temporal_backward_kernel, [rows(D + 640)], sent, factors, *saved, flops=4 * 10**9)

    half = 9 * ATT // 2
    out_part = (out_keep + out_other.astype(F32)).astype(BF).reshape(64, 2, half)
    back = exchange(jnp.concatenate([packed.reshape(64, 2, D + 640), out_part], 2))

    out_part = back[:, :, D + 640 :].astype(F32).reshape(32, 2, 2, half)
    out_part = jnp.sum(out_part, 0).reshape(1, 2, 9 * ATT)
    out_part = jnp.broadcast_to(out_part, (8, 2, 9 * ATT))
    out_part = jnp.sum(lax.all_to_all(out_part, DP, 0, 0, tiled=True), 0)
    out_grad = out_part.reshape(2, 9, ATT).transpose(1, 0, 2).reshape(9, D)

    token_grad = back[:, :, :D].reshape(ROWS, D)
    (qkv_grad,) = call(
        spatial_backward_kernel, [((ROWS, 3 * ATT), BF)], qkv, token_grad, factors, w_so
    )

    mine = jnp.sum(back[:, :, D : D + ATT].astype(F32), 0).reshape(1, D)
    other = swap_cores(mine)
    rows = jnp.where(core == 0, jnp.concatenate([mine, other]), jnp.concatenate([other, mine]))
    other = lax.ppermute(rows, "yhi", [(0, 1), (1, 0), (2, 3), (3, 2)])
    low = yhi % 2 == 0
    factor_grad = jnp.where(low, jnp.concatenate([rows, other]), jnp.concatenate([other, rows]))
    return token_grad[None, None], qkv_grad[None, None], factor_grad[None], out_grad


def solution(mesh):
    fine = Mesh(mesh.devices.reshape(4, 2, 4, 8, 2), DP + SEQ)
    frames = P(DP, SEQ, None, None)
    return jax.shard_map(
        body,
        mesh=fine,
        in_specs=(
            frames,
            frames,
            P(SEQ, None),
            P(None, SEQ),
            P(SEQ, None),
            P(DP, None, None),
            frames,
        ),
        out_specs=(frames, frames, P(DP, None, None), P(SEQ, None)),
        check_vma=False,
    )
```

```python
import math

import jax
import jax.numpy as jnp
from jax import lax
from jax.experimental import pallas as pl
from jax.experimental.pallas import tpu as pltpu
from jax.sharding import Mesh
from jax.sharding import PartitionSpec as P

D = 1152
HEADS = 8
HS = 72
ATT = 576
ROWS = 128
SCALE = 1.0 / math.sqrt(HS)
SEQ = ("yhi", "z", "core")
CHIPS = ("yhi", "z")
DP = ("x", "ylo")
BF = jnp.bfloat16
F32 = jnp.float32


def nn(a, b):
    return lax.dot_general(a, b, (((1,), (0,)), ((), ())), preferred_element_type=F32)


def nt(a, b):
    return lax.dot_general(a, b, (((1,), (1,)), ((), ())), preferred_element_type=F32)


def tn(a, b):
    return lax.dot_general(a, b, (((0,), (0,)), ((), ())), preferred_element_type=F32)


def head_masks():
    head = lax.broadcasted_iota(jnp.int32, (ROWS, ATT), 1) // HS
    return [head == h for h in range(HEADS)]


def stack_heads(masks, a):
    zero = jnp.zeros_like(a)
    return jnp.concatenate([jnp.where(m, a, zero) for m in masks], 0)


def pick_heads(masks, a):
    out = a[:ROWS]
    for h in range(1, HEADS):
        out = jnp.where(masks[h], a[h * ROWS : (h + 1) * ROWS], out)
    return out


def softmax_rows(scores):
    top = jnp.max(scores, -1, keepdims=True)
    weights = jnp.exp(scores - top)
    return weights / jnp.sum(weights, -1, keepdims=True)


def attend(masks, q, k, v, same):
    q_stack = stack_heads(masks, q)
    scores = nt(q_stack, k) * SCALE
    if same is not None:
        scores = jnp.where(same, scores, -1e30)
    probs = softmax_rows(scores)
    probs_b = probs.astype(BF)
    mixed = pick_heads(masks, nn(probs_b, v)).astype(BF)
    return q_stack, probs, probs_b, mixed


def attend_back(masks, q_stack, k, v, probs, probs_b, d_mixed):
    d_stack = stack_heads(masks, d_mixed)
    d_probs = nt(d_stack, v).astype(BF).astype(F32)
    d_v = tn(probs_b, d_stack)
    d_scores = probs * (d_probs - jnp.sum(d_probs * probs, -1, keepdims=True)) * SCALE
    d_scores = d_scores.astype(BF)
    d_q = pick_heads(masks, nn(d_scores, k))
    d_k = tn(d_scores, q_stack)
    return d_q.astype(BF), d_k.astype(BF), d_v.astype(BF)


def spatial_forward_kernel(qkv, mixed):
    q, k, v = qkv[:, :ATT], qkv[:, ATT : 2 * ATT], qkv[:, 2 * ATT :]
    mixed[...] = attend(head_masks(), q, k, v, None)[3]


def spatial_backward_kernel(qkv, hidden_grad, factors, w_so, out):
    q, k, v = qkv[:, :ATT], qkv[:, ATT : 2 * ATT], qkv[:, 2 * ATT :]
    masks = head_masks()
    gated = (hidden_grad[...].astype(F32) * factors[0:1, :]).astype(BF)
    d_mixed = nt(gated, w_so[...]).astype(BF)
    q_stack, probs, probs_b, _ = attend(masks, q, k, v, None)
    d_q, d_k, d_v = attend_back(masks, q_stack, k, v, probs, probs_b, d_mixed)
    out[:, :ATT] = d_q
    out[:, ATT : 2 * ATT] = d_k
    out[:, 2 * ATT :] = d_v


def compact_kernel(place, mine, other, own_so, own_out, own_qkv, part, slots, so, out, qkv):
    core, z = place[0], place[2]
    for i in range(4):
        slots[core * 4 + i] = mine[i]
        slots[(1 - core) * 4 + i] = other[i]
    for target in range(8):
        delta = (target - z) & 7
        slot = jnp.where(delta < 2, 1 - delta, delta)
        slot = jnp.where(delta == 4, 5, jnp.where(delta == 7, 4, slot))
        slot = jnp.where(delta == 5, 7, slot)
        for c in range(2):
            i = target * 2 + c
            shard = slots[slot, c].astype(F32)
            so[9 * i : 9 * i + 9, :] = shard[:9]
            out[9 * i : 9 * i + 9, :] = shard[9:18]
            qkv[27 * i : 27 * i + 27, :] = shard[18:]
    own_so[...] = so[...].astype(BF)
    own_out[...] = out[...].astype(BF)
    own_qkv[...] = qkv[...].astype(BF)
    at_qkv = pl.multiple_of(core * 208, 16)
    at = pl.multiple_of(core * 64, 16)
    part[0:224, :] = own_qkv[pl.ds(at_qkv, 224), :]
    part[224:304, :] = own_so[pl.ds(at, 80), :]
    part[304:384, :] = own_out[pl.ds(at, 80), :]


SECTIONS = ((0, 0, 224), (1, 224, 304), (2, 304, 384))
BLOCK = (432, 144, 144)
STEP = (208, 64, 64)


def part_copies(ref, half, block, targets):
    copies = []
    for section, first, last in SECTIONS:
        first = first + 16 * half
        row = first - SECTIONS[section][1] + STEP[section] * half
        to = pl.multiple_of(block * BLOCK[section] + row, 16)
        rows = last - first
        copies.append((ref.at[pl.ds(first, rows)], targets[section].at[pl.ds(to, rows)]))
    return copies


def assemble(place, own, near, swapped, targets, sems):
    for me in range(2):

        @pl.when(place[0] == me)
        def _():
            cls = place[1]
            pairs = []
            for section, ref in enumerate(own):
                to = pl.multiple_of(cls * BLOCK[section], 16)
                pairs.append((ref, targets[section].at[pl.ds(to, BLOCK[section])]))
            for flip, ref, other in zip((2, 1, 3), near, swapped):
                pairs += part_copies(ref, me, cls ^ flip, targets)
                pairs += part_copies(other, 1 - me, cls ^ flip, targets)
            copies = [pltpu.make_async_copy(a, z, sems.at[i]) for i, (a, z) in enumerate(pairs)]
            for copy in copies:
                copy.start()
            for copy in copies:
                copy.wait()


def temporal_forward_kernel(
    place, sent, factors, own_qkv, own_so, own_out, b, c, d, other_b, other_c, other_d,
    out_keep, out_send, w_so, w_out, w_qkv, q_out, k_out, v_out, probs_out, mixed_out,
    unit_out, inverse_out, project_out, sems,
):
    assemble(
        place, (own_qkv, own_so, own_out), (b, c, d), (other_b, other_c, other_d),
        (w_qkv, w_so, w_out), sems,
    )
    tokens, cotangent, mixed_s = sent[:, :D], sent[:, D : 2 * D], sent[:, 2 * D :]
    gate_s, shift, scale, gate_t = (factors[i : i + 1, :] for i in range(4))
    project = nn(mixed_s, w_so[...])
    project_out[...] = project
    hidden = (tokens.astype(F32) + gate_s * project).astype(BF).astype(F32)
    centered = hidden - jnp.mean(hidden, -1, keepdims=True)
    inverse = lax.rsqrt(jnp.mean(centered * centered, -1, keepdims=True) + 1e-06)
    inverse_out[...] = jnp.broadcast_to(inverse, (ROWS, 128))
    unit = centered * inverse
    unit_out[...] = unit
    normed = (unit * (1.0 + scale) + shift).astype(BF)
    q, k, v = (nt(normed, w_qkv[i * ATT : (i + 1) * ATT, :]).astype(BF) for i in range(3))
    q_out[...], k_out[...], v_out[...] = q, k, v

    row = lax.broadcasted_iota(jnp.int32, (HEADS * ROWS, ROWS), 0)
    col = lax.broadcasted_iota(jnp.int32, (HEADS * ROWS, ROWS), 1)
    same = ((row ^ col) & 1) == 0
    _, probs, _, mixed = attend(head_masks(), q, k, v, same)
    probs_out[...] = probs
    mixed_out[...] = mixed

    scaled = (cotangent.astype(F32) * gate_t).astype(BF)
    left, right = scaled[:, :ATT], scaled[:, ATT:]
    first = place[0] == 0
    out_keep[...] = tn(mixed, jnp.where(first, left, right))
    out_send[...] = tn(mixed, jnp.where(first, right, left)).astype(BF)


def temporal_backward_kernel(
    sent, factors, w_so, w_out, w_qkv, q, k, v, probs, mixed, unit, inverse, project, packed
):
    scale, gate_t = factors[2:3, :], factors[3:4, :]
    cot = sent[:, D : 2 * D].astype(F32)
    scaled = (cot * gate_t).astype(BF)
    masks = head_masks()
    q, k, v, probs = q[...], k[...], v[...], probs[...]
    d_mixed = nt(scaled, w_out[...]).astype(BF)
    q_stack = stack_heads(masks, q)
    d_q, d_k, d_v = attend_back(masks, q_stack, k, v, probs, probs.astype(BF), d_mixed)
    wq, wk, wv = (w_qkv[i * ATT : (i + 1) * ATT, :] for i in range(3))
    d_normed = (nn(d_q, wq) + nn(d_k, wk) + nn(d_v, wv)).astype(BF).astype(F32)
    unit = unit[...]
    d_unit = d_normed * (1.0 + scale)
    d_hidden = inverse[:, 0:1] * (
        d_unit
        - jnp.mean(d_unit, -1, keepdims=True)
        - unit * jnp.mean(d_unit * unit, -1, keepdims=True)
    )
    grad = (cot + d_hidden).astype(BF)
    packed[:, :D] = grad
    project_t = nn(mixed[...], w_out[...])
    factor_grads = (
        jnp.sum(grad.astype(F32) * project[...], 0, keepdims=True),
        jnp.sum(d_normed, 0, keepdims=True),
        jnp.sum(d_normed * unit, 0, keepdims=True),
        jnp.sum(cot * project_t, 0, keepdims=True),
    )
    tile = jnp.concatenate(factor_grads * 4, 0).astype(BF)
    for i in range(8):
        packed[16 * i : 16 * i + 16, D:] = tile


def call(kernel, outs, *args, scalars=0, remote=0, scratch=(), flops=10**9):
    vmem = pl.BlockSpec(memory_space=pltpu.VMEM)
    specs = [pl.BlockSpec(memory_space=pltpu.SMEM)] * scalars
    specs += [vmem] * (len(args) - scalars - remote)
    specs += [pl.BlockSpec(memory_space=pl.ANY)] * remote
    return pl.pallas_call(
        kernel,
        out_shape=[jax.ShapeDtypeStruct(s, d) for s, d in outs],
        in_specs=specs,
        out_specs=[vmem] * len(outs),
        scratch_shapes=list(scratch),
        compiler_params=pltpu.CompilerParams(vmem_limit_bytes=32 * 2**20),
        cost_estimate=pl.CostEstimate(flops=flops, bytes_accessed=10**7, transcendentals=10**5),
    )(*args)


def exchange(a):
    return lax.all_to_all(a, SEQ, 0, 0, tiled=True)


AXES = DP + SEQ


def device(x, y, z, core):
    ylo, yhi = y % 2, (y % 8) // 2
    return ((((x % 4) * 2 + ylo) * 4 + yhi) * 8 + z % 8) * 2 + core


def receive(a, source):
    pairs = []
    for x in range(4):
        for y in range(8):
            for z in range(8):
                for core in range(2):
                    pairs.append((device(*source(x, y, z, core), core), device(x, y, z, core)))
    return lax.ppermute(a, AXES, pairs)


def swap_cores(a):
    return lax.ppermute(a, "core", [(0, 1), (1, 0)])


OFFSETS = ((1, 0, 2, 3), (-1, 4, -2, -3))


def class_source(x, y, z, core):
    ylo, yhi = y % 2, y // 2
    cls = (x % 2) * 2 + ylo
    return (x // 2) * 2 + yhi // 2, cls * 2 + yhi % 2, z


def line_source(step):
    return lambda x, y, z, core: (x, y, z + OFFSETS[core][step])


def near_source(dx, dy):
    def source(x, y, z, core):
        sign = 1 - 2 * core
        return x + sign * dx, y + sign * dy, z

    return source


def gather_weights(w_so, w_qkv, w_out, place, sent):
    shard = receive(jnp.concatenate([w_so, w_out, w_qkv.T], 0), class_source)
    shards = lax.all_gather(shard, "core", axis=0)
    shards, sent = lax.optimization_barrier((shards, sent))
    mine = jnp.stack([receive(shards, line_source(i)) for i in range(4)])
    sent = exchange(sent).reshape(ROWS, 2 * D + ATT)
    other = swap_cores(mine)
    rows = lambda n: ((n, D), BF)
    own_so, own_out, own_qkv, part = call(
        compact_kernel, [rows(144), rows(144), rows(432), rows(384)], place, mine, other, scalars=1,
        scratch=[
            pltpu.VMEM((8, 2, 45, D), BF),
            pltpu.VMEM((144, D), F32),
            pltpu.VMEM((144, D), F32),
            pltpu.VMEM((432, D), F32),
        ],
    )
    part, sent = lax.optimization_barrier((part, sent))
    near = [receive(part, near_source(dx, dy)) for dx, dy in ((1, 0), (0, 1), (1, 1))]
    return [own_qkv, own_so, own_out] + near + [swap_cores(a) for a in near], sent


def body(tokens, qkv, w_so, w_qkv, w_out, factors, cotangent):
    tokens, qkv, cotangent, factors = tokens[0, 0], qkv[0, 0], cotangent[0, 0], factors[0]
    core = lax.axis_index("core")
    cls = (lax.axis_index("x") % 2) * 2 + lax.axis_index("ylo")
    place = jnp.stack([core, cls, lax.axis_index("z")]).astype(jnp.int32)

    (mixed_s,) = call(spatial_forward_kernel, [((ROWS, ATT), BF)], qkv)
    sent = jnp.concatenate([tokens, cotangent, mixed_s], 1).reshape(64, 2, 2 * D + ATT)
    weights, sent = gather_weights(w_so, w_qkv, w_out, place, sent)

    rows = lambda n, kind=BF: ((ROWS, n), kind)
    out_keep, out_send, *saved = call(
        temporal_forward_kernel,
        [
            ((ATT, ATT), F32), ((ATT, ATT), BF), ((ATT, D), BF), ((ATT, D), BF), ((3 * ATT, D), BF),
            rows(ATT), rows(ATT), rows(ATT), ((HEADS * ROWS, ROWS), F32), rows(ATT),
            rows(D, F32), rows(128, F32), rows(D, F32),
        ],
        place, sent, factors, *weights,
        scalars=1, remote=len(weights), flops=4 * 10**9,
        scratch=[pltpu.SemaphoreType.DMA((24,))],
    )
    w_so = saved[0]
    out_other = swap_cores(out_send)
    (packed,) = call(temporal_backward_kernel, [rows(2 * D)], sent, factors, *saved, flops=4 * 10**9)

    half = 9 * ATT // 2
    out_part = (out_keep + out_other.astype(F32)).astype(BF).reshape(64, 2, half)
    back = exchange(jnp.concatenate([packed.reshape(64, 2, 2 * D), out_part], 2))

    out_part = back[:, :, 2 * D :].astype(F32).reshape(32, 2, 2, half)
    out_part = jnp.sum(out_part, 0).reshape(1, 2, 9 * ATT)
    out_part = jnp.broadcast_to(out_part, (8, 2, 9 * ATT))
    out_part = jnp.sum(lax.all_to_all(out_part, DP, 0, 0, tiled=True), 0)
    out_grad = out_part.reshape(2, 9, ATT).transpose(1, 0, 2).reshape(9, D)

    token_grad = back[:, :, :D].reshape(ROWS, D)
    (qkv_grad,) = call(
        spatial_backward_kernel, [((ROWS, 3 * ATT), BF)], qkv, token_grad, factors, w_so
    )

    mine = jnp.sum(back[:, :, D : 2 * D].astype(F32), 0)
    other = swap_cores(mine)
    factor_grad = jnp.where(core == 0, jnp.concatenate([mine, other]), jnp.concatenate([other, mine]))
    return token_grad[None, None], qkv_grad[None, None], factor_grad[None], out_grad


def solution(mesh):
    fine = Mesh(mesh.devices.reshape(4, 2, 4, 8, 2), DP + SEQ)
    frames = P(DP, SEQ, None, None)
    return jax.shard_map(
        body,
        mesh=fine,
        in_specs=(
            frames,
            frames,
            P(SEQ, None),
            P(None, SEQ),
            P(SEQ, None),
            P(DP, None, None),
            frames,
        ),
        out_specs=(frames, frames, P(DP, None, None), P(SEQ, None)),
        check_vma=False,
    )
```

```python
import math

import jax
import jax.numpy as jnp
from jax import lax
from jax.experimental import pallas as pl
from jax.experimental.pallas import tpu as pltpu
from jax.sharding import Mesh
from jax.sharding import PartitionSpec as P

D = 1152
HEADS = 8
HS = 72
ATT = 576
ROWS = 128
SCALE = 1.0 / math.sqrt(HS)
SEQ = ("yhi", "z", "core")
CHIPS = ("yhi", "z")
DP = ("x", "ylo")
BF = jnp.bfloat16
F32 = jnp.float32


def nn(a, b):
    return lax.dot_general(a, b, (((1,), (0,)), ((), ())), preferred_element_type=F32)


def nt(a, b):
    return lax.dot_general(a, b, (((1,), (1,)), ((), ())), preferred_element_type=F32)


def tn(a, b):
    return lax.dot_general(a, b, (((0,), (0,)), ((), ())), preferred_element_type=F32)


def head_masks():
    head = lax.broadcasted_iota(jnp.int32, (ROWS, ATT), 1) // HS
    return [head == h for h in range(HEADS)]


def stack_heads(masks, a):
    zero = jnp.zeros_like(a)
    return jnp.concatenate([jnp.where(m, a, zero) for m in masks], 0)


def pick_heads(masks, a):
    out = a[:ROWS]
    for h in range(1, HEADS):
        out = jnp.where(masks[h], a[h * ROWS : (h + 1) * ROWS], out)
    return out


def softmax_rows(scores):
    top = jnp.max(scores, -1, keepdims=True)
    weights = jnp.exp(scores - top)
    return weights / jnp.sum(weights, -1, keepdims=True)


def attend(masks, q, k, v, same):
    q_stack = stack_heads(masks, q)
    scores = nt(q_stack, k) * SCALE
    if same is not None:
        scores = jnp.where(same, scores, -1e30)
    probs = softmax_rows(scores)
    probs_b = probs.astype(BF)
    mixed = pick_heads(masks, nn(probs_b, v)).astype(BF)
    return q_stack, probs, probs_b, mixed


def attend_back(masks, q_stack, k, v, probs, probs_b, d_mixed):
    d_stack = stack_heads(masks, d_mixed)
    d_probs = nt(d_stack, v).astype(BF).astype(F32)
    d_v = tn(probs_b, d_stack)
    d_scores = probs * (d_probs - jnp.sum(d_probs * probs, -1, keepdims=True)) * SCALE
    d_scores = d_scores.astype(BF)
    d_q = pick_heads(masks, nn(d_scores, k))
    d_k = tn(d_scores, q_stack)
    return d_q.astype(BF), d_k.astype(BF), d_v.astype(BF)


def spatial_forward_kernel(qkv, mixed):
    q, k, v = qkv[:, :ATT], qkv[:, ATT : 2 * ATT], qkv[:, 2 * ATT :]
    mixed[...] = attend(head_masks(), q, k, v, None)[3]


def spatial_backward_kernel(qkv, hidden_grad, factors, w_so, out):
    q, k, v = qkv[:, :ATT], qkv[:, ATT : 2 * ATT], qkv[:, 2 * ATT :]
    masks = head_masks()
    gated = (hidden_grad[...].astype(F32) * factors[0:1, :]).astype(BF)
    d_mixed = nt(gated, w_so[...]).astype(BF)
    q_stack, probs, probs_b, _ = attend(masks, q, k, v, None)
    d_q, d_k, d_v = attend_back(masks, q_stack, k, v, probs, probs_b, d_mixed)
    out[:, :ATT] = d_q
    out[:, ATT : 2 * ATT] = d_k
    out[:, 2 * ATT :] = d_v


def compact_kernel(place, shards, own_so, own_out, own_qkv, part, so, out, qkv):
    core = place[0]
    for i in range(16):
        shard = shards[i].astype(F32)
        so[9 * i : 9 * i + 9, :] = shard[:9]
        out[9 * i : 9 * i + 9, :] = shard[9:18]
        qkv[27 * i : 27 * i + 27, :] = shard[18:45]
    own_so[...] = so[...].astype(BF)
    own_out[...] = out[...].astype(BF)
    own_qkv[...] = qkv[...].astype(BF)
    at_qkv = pl.multiple_of(core * 208, 16)
    at = pl.multiple_of(core * 64, 16)
    part[0:224, :] = own_qkv[pl.ds(at_qkv, 224), :]
    part[224:304, :] = own_so[pl.ds(at, 80), :]
    part[304:384, :] = own_out[pl.ds(at, 80), :]


SECTIONS = ((0, 0, 224), (1, 224, 304), (2, 304, 384))
BLOCK = (432, 144, 144)
STEP = (208, 64, 64)


def part_copies(ref, half, block, targets):
    copies = []
    for section, first, last in SECTIONS:
        first = first + 16 * half
        row = first - SECTIONS[section][1] + STEP[section] * half
        to = pl.multiple_of(block * BLOCK[section] + row, 16)
        rows = last - first
        copies.append((ref.at[pl.ds(first, rows)], targets[section].at[pl.ds(to, rows)]))
    return copies


def assemble(place, own, near, swapped, targets, sems):
    for me in range(2):

        @pl.when(place[0] == me)
        def _():
            cls = place[1]
            pairs = []
            for section, ref in enumerate(own):
                to = pl.multiple_of(cls * BLOCK[section], 16)
                pairs.append((ref, targets[section].at[pl.ds(to, BLOCK[section])]))
            for flip, ref, other in zip((2, 1, 3), near, swapped):
                pairs += part_copies(ref, me, cls ^ flip, targets)
                pairs += part_copies(other, 1 - me, cls ^ flip, targets)
            copies = [pltpu.make_async_copy(a, z, sems.at[i]) for i, (a, z) in enumerate(pairs)]
            for copy in copies:
                copy.start()
            for copy in copies:
                copy.wait()


def temporal_forward_kernel(
    place, sent, factors, own_qkv, own_so, own_out, b, c, d, other_b, other_c, other_d,
    out_keep, out_send, w_so, w_out, w_qkv, q_out, k_out, v_out, probs_out, mixed_out,
    unit_out, inverse_out, project_out, sems,
):
    assemble(
        place, (own_qkv, own_so, own_out), (b, c, d), (other_b, other_c, other_d),
        (w_qkv, w_so, w_out), sems,
    )
    tokens, cotangent, mixed_s = sent[:, :D], sent[:, D : 2 * D], sent[:, 2 * D :]
    gate_s, shift, scale, gate_t = (factors[i : i + 1, :] for i in range(4))
    project = nn(mixed_s, w_so[...])
    project_out[...] = project
    hidden = (tokens.astype(F32) + gate_s * project).astype(BF).astype(F32)
    centered = hidden - jnp.mean(hidden, -1, keepdims=True)
    inverse = lax.rsqrt(jnp.mean(centered * centered, -1, keepdims=True) + 1e-06)
    inverse_out[...] = jnp.broadcast_to(inverse, (ROWS, 128))
    unit = centered * inverse
    unit_out[...] = unit
    normed = (unit * (1.0 + scale) + shift).astype(BF)
    q, k, v = (nt(normed, w_qkv[i * ATT : (i + 1) * ATT, :]).astype(BF) for i in range(3))
    q_out[...], k_out[...], v_out[...] = q, k, v

    row = lax.broadcasted_iota(jnp.int32, (HEADS * ROWS, ROWS), 0)
    col = lax.broadcasted_iota(jnp.int32, (HEADS * ROWS, ROWS), 1)
    same = ((row ^ col) & 1) == 0
    _, probs, _, mixed = attend(head_masks(), q, k, v, same)
    probs_out[...] = probs
    mixed_out[...] = mixed

    scaled = (cotangent.astype(F32) * gate_t).astype(BF)
    left, right = scaled[:, :ATT], scaled[:, ATT:]
    first = place[0] == 0
    out_keep[...] = tn(mixed, jnp.where(first, left, right))
    out_send[...] = tn(mixed, jnp.where(first, right, left)).astype(BF)


def temporal_backward_kernel(
    sent, factors, w_so, w_out, w_qkv, q, k, v, probs, mixed, unit, inverse, project, packed
):
    scale, gate_t = factors[2:3, :], factors[3:4, :]
    cot = sent[:, D : 2 * D].astype(F32)
    scaled = (cot * gate_t).astype(BF)
    masks = head_masks()
    q, k, v, probs = q[...], k[...], v[...], probs[...]
    d_mixed = nt(scaled, w_out[...]).astype(BF)
    q_stack = stack_heads(masks, q)
    d_q, d_k, d_v = attend_back(masks, q_stack, k, v, probs, probs.astype(BF), d_mixed)
    wq, wk, wv = (w_qkv[i * ATT : (i + 1) * ATT, :] for i in range(3))
    d_normed = (nn(d_q, wq) + nn(d_k, wk) + nn(d_v, wv)).astype(BF).astype(F32)
    unit = unit[...]
    d_unit = d_normed * (1.0 + scale)
    d_hidden = inverse[:, 0:1] * (
        d_unit
        - jnp.mean(d_unit, -1, keepdims=True)
        - unit * jnp.mean(d_unit * unit, -1, keepdims=True)
    )
    grad = (cot + d_hidden).astype(BF)
    packed[:, :D] = grad
    project_t = nn(mixed[...], w_out[...])
    factor_grads = (
        jnp.sum(grad.astype(F32) * project[...], 0, keepdims=True),
        jnp.sum(d_normed, 0, keepdims=True),
        jnp.sum(d_normed * unit, 0, keepdims=True),
        jnp.sum(cot * project_t, 0, keepdims=True),
    )
    tile = jnp.concatenate(factor_grads * 4, 0).astype(BF)
    for i in range(8):
        packed[16 * i : 16 * i + 16, D:] = tile


def call(kernel, outs, *args, scalars=0, remote=0, scratch=(), flops=10**9):
    vmem = pl.BlockSpec(memory_space=pltpu.VMEM)
    specs = [pl.BlockSpec(memory_space=pltpu.SMEM)] * scalars
    specs += [vmem] * (len(args) - scalars - remote)
    specs += [pl.BlockSpec(memory_space=pl.ANY)] * remote
    return pl.pallas_call(
        kernel,
        out_shape=[jax.ShapeDtypeStruct(s, d) for s, d in outs],
        in_specs=specs,
        out_specs=[vmem] * len(outs),
        scratch_shapes=list(scratch),
        compiler_params=pltpu.CompilerParams(vmem_limit_bytes=32 * 2**20),
        cost_estimate=pl.CostEstimate(flops=flops, bytes_accessed=10**7, transcendentals=10**5),
    )(*args)


def exchange(a):
    return lax.all_to_all(a, SEQ, 0, 0, tiled=True)


AXES = DP + SEQ


def device(x, y, z, core):
    ylo, yhi = y % 2, (y % 8) // 2
    return ((((x % 4) * 2 + ylo) * 4 + yhi) * 8 + z % 8) * 2 + core


def receive(a, source):
    pairs = []
    for x in range(4):
        for y in range(8):
            for z in range(8):
                for core in range(2):
                    pairs.append((device(*source(x, y, z, core), core), device(x, y, z, core)))
    return lax.ppermute(a, AXES, pairs)


def swap_cores(a):
    return lax.ppermute(a, "core", [(0, 1), (1, 0)])


def class_source(x, y, z, core):
    ylo, yhi = y % 2, y // 2
    cls = (x % 2) * 2 + ylo
    return (x // 2) * 2 + yhi // 2, cls * 2 + yhi % 2, z


def near_source(dx, dy):
    def source(x, y, z, core):
        sign = 1 - 2 * core
        return x + sign * dx, y + sign * dy, z

    return source


def gather_weights(w_so, w_qkv, w_out, place, sent):
    shard = jnp.concatenate([w_so, w_out, w_qkv.T, jnp.zeros((3, D), BF)], 0)
    shard = receive(shard, class_source)
    shards = lax.all_gather(shard, "core", axis=0, tiled=True)
    shards, sent = lax.optimization_barrier((shards, sent))
    shards = lax.all_gather(shards, "z", axis=0, tiled=True).reshape(16, 48, D)
    sent = exchange(sent).reshape(ROWS, 2 * D + ATT)
    shards, sent = lax.optimization_barrier((shards, sent))
    rows = lambda n: ((n, D), BF)
    own_so, own_out, own_qkv, part = call(
        compact_kernel, [rows(144), rows(144), rows(432), rows(384)], place, shards, scalars=1,
        scratch=[pltpu.VMEM((144, D), F32), pltpu.VMEM((144, D), F32), pltpu.VMEM((432, D), F32)],
    )
    near = [receive(part, near_source(dx, dy)) for dx, dy in ((1, 0), (0, 1), (1, 1))]
    return [own_qkv, own_so, own_out] + near + [swap_cores(a) for a in near], sent


def body(tokens, qkv, w_so, w_qkv, w_out, factors, cotangent):
    tokens, qkv, cotangent, factors = tokens[0, 0], qkv[0, 0], cotangent[0, 0], factors[0]
    core = lax.axis_index("core")
    cls = (lax.axis_index("x") % 2) * 2 + lax.axis_index("ylo")
    place = jnp.stack([core, cls]).astype(jnp.int32)

    (mixed_s,) = call(spatial_forward_kernel, [((ROWS, ATT), BF)], qkv)
    sent = jnp.concatenate([tokens, cotangent, mixed_s], 1).reshape(64, 2, 2 * D + ATT)
    weights, sent = gather_weights(w_so, w_qkv, w_out, place, sent)

    rows = lambda n, kind=BF: ((ROWS, n), kind)
    out_keep, out_send, *saved = call(
        temporal_forward_kernel,
        [
            ((ATT, ATT), F32), ((ATT, ATT), BF), ((ATT, D), BF), ((ATT, D), BF), ((3 * ATT, D), BF),
            rows(ATT), rows(ATT), rows(ATT), ((HEADS * ROWS, ROWS), F32), rows(ATT),
            rows(D, F32), rows(128, F32), rows(D, F32),
        ],
        place, sent, factors, *weights,
        scalars=1, remote=len(weights), flops=4 * 10**9,
        scratch=[pltpu.SemaphoreType.DMA((24,))],
    )
    w_so = saved[0]
    out_other = swap_cores(out_send)
    (packed,) = call(temporal_backward_kernel, [rows(2 * D)], sent, factors, *saved, flops=4 * 10**9)

    half = 9 * ATT // 2
    out_part = (out_keep + out_other.astype(F32)).astype(BF).reshape(64, 2, half)
    back = exchange(jnp.concatenate([packed.reshape(64, 2, 2 * D), out_part], 2))

    out_part = back[:, :, 2 * D :].astype(F32).reshape(32, 2, 2, half)
    out_part = jnp.sum(out_part, 0).reshape(1, 2, 9 * ATT)
    out_part = jnp.broadcast_to(out_part, (8, 2, 9 * ATT))
    out_part = jnp.sum(lax.all_to_all(out_part, DP, 0, 0, tiled=True), 0)
    out_grad = out_part.reshape(2, 9, ATT).transpose(1, 0, 2).reshape(9, D)

    token_grad = back[:, :, :D].reshape(ROWS, D)
    (qkv_grad,) = call(
        spatial_backward_kernel, [((ROWS, 3 * ATT), BF)], qkv, token_grad, factors, w_so
    )

    mine = jnp.sum(back[:, :, D : 2 * D].astype(F32), 0)
    other = swap_cores(mine)
    factor_grad = jnp.where(core == 0, jnp.concatenate([mine, other]), jnp.concatenate([other, mine]))
    return token_grad[None, None], qkv_grad[None, None], factor_grad[None], out_grad


def solution(mesh):
    fine = Mesh(mesh.devices.reshape(4, 2, 4, 8, 2), DP + SEQ)
    frames = P(DP, SEQ, None, None)
    return jax.shard_map(
        body,
        mesh=fine,
        in_specs=(
            frames,
            frames,
            P(SEQ, None),
            P(None, SEQ),
            P(SEQ, None),
            P(DP, None, None),
            frames,
        ),
        out_specs=(frames, frames, P(DP, None, None), P(SEQ, None)),
        check_vma=False,
    )
```

```python
import math

import jax
import jax.numpy as jnp
from jax import lax
from jax.experimental import pallas as pl
from jax.experimental.pallas import tpu as pltpu
from jax.sharding import Mesh
from jax.sharding import PartitionSpec as P

D = 1152
HEADS = 8
HS = 72
ATT = 576
ROWS = 128
SCALE = 1.0 / math.sqrt(HS)
SEQ = ("yhi", "z", "core")
CHIPS = ("yhi", "z")
DP = ("x", "ylo")
BF = jnp.bfloat16
F32 = jnp.float32


def nn(a, b):
    return lax.dot_general(a, b, (((1,), (0,)), ((), ())), preferred_element_type=F32)


def nt(a, b):
    return lax.dot_general(a, b, (((1,), (1,)), ((), ())), preferred_element_type=F32)


def tn(a, b):
    return lax.dot_general(a, b, (((0,), (0,)), ((), ())), preferred_element_type=F32)


def head_masks():
    head = lax.broadcasted_iota(jnp.int32, (ROWS, ATT), 1) // HS
    return [head == h for h in range(HEADS)]


def stack_heads(masks, a):
    zero = jnp.zeros_like(a)
    return jnp.concatenate([jnp.where(m, a, zero) for m in masks], 0)


def pick_heads(masks, a):
    out = a[:ROWS]
    for h in range(1, HEADS):
        out = jnp.where(masks[h], a[h * ROWS : (h + 1) * ROWS], out)
    return out


def softmax_rows(scores):
    top = jnp.max(scores, -1, keepdims=True)
    weights = jnp.exp(scores - top)
    return weights / jnp.sum(weights, -1, keepdims=True)


def attend(masks, q, k, v, same):
    q_stack = stack_heads(masks, q)
    scores = nt(q_stack, k) * SCALE
    if same is not None:
        scores = jnp.where(same, scores, -1e30)
    probs = softmax_rows(scores)
    probs_b = probs.astype(BF)
    mixed = pick_heads(masks, nn(probs_b, v)).astype(BF)
    return q_stack, probs, probs_b, mixed


def attend_back(masks, q_stack, k, v, probs, probs_b, d_mixed):
    d_stack = stack_heads(masks, d_mixed)
    d_probs = nt(d_stack, v).astype(BF).astype(F32)
    d_v = tn(probs_b, d_stack)
    d_scores = probs * (d_probs - jnp.sum(d_probs * probs, -1, keepdims=True)) * SCALE
    d_scores = d_scores.astype(BF)
    d_q = pick_heads(masks, nn(d_scores, k))
    d_k = tn(d_scores, q_stack)
    return d_q.astype(BF), d_k.astype(BF), d_v.astype(BF)


def spatial_forward_kernel(qkv, mixed):
    q, k, v = qkv[:, :ATT], qkv[:, ATT : 2 * ATT], qkv[:, 2 * ATT :]
    mixed[...] = attend(head_masks(), q, k, v, None)[3]


def spatial_backward_kernel(qkv, hidden_grad, factors, w_so, out):
    q, k, v = qkv[:, :ATT], qkv[:, ATT : 2 * ATT], qkv[:, 2 * ATT :]
    masks = head_masks()
    gated = (hidden_grad[...].astype(F32) * factors[0:1, :]).astype(BF)
    d_mixed = nt(gated, w_so[...]).astype(BF)
    q_stack, probs, probs_b, _ = attend(masks, q, k, v, None)
    d_q, d_k, d_v = attend_back(masks, q_stack, k, v, probs, probs_b, d_mixed)
    out[:, :ATT] = d_q
    out[:, ATT : 2 * ATT] = d_k
    out[:, 2 * ATT :] = d_v


def compact_kernel(place, mine, other, own_so, own_out, own_qkv, part, both, so, out, qkv):
    core = place[0]
    both[core] = mine[...]
    both[1 - core] = other[...]
    for i in range(16):
        shard = both[i % 2, 48 * (i // 2) : 48 * (i // 2) + 48, :].astype(F32)
        so[9 * i : 9 * i + 9, :] = shard[:9]
        out[9 * i : 9 * i + 9, :] = shard[9:18]
        qkv[27 * i : 27 * i + 27, :] = shard[18:45]
    own_so[...] = so[...].astype(BF)
    own_out[...] = out[...].astype(BF)
    own_qkv[...] = qkv[...].astype(BF)
    at_qkv = pl.multiple_of(core * 208, 16)
    at = pl.multiple_of(core * 64, 16)
    part[0:224, :] = own_qkv[pl.ds(at_qkv, 224), :]
    part[224:304, :] = own_so[pl.ds(at, 80), :]
    part[304:384, :] = own_out[pl.ds(at, 80), :]


SECTIONS = ((0, 0, 224), (1, 224, 304), (2, 304, 384))
BLOCK = (432, 144, 144)
STEP = (208, 64, 64)


def part_copies(ref, half, block, targets):
    copies = []
    for section, first, last in SECTIONS:
        first = first + 16 * half
        row = first - SECTIONS[section][1] + STEP[section] * half
        to = pl.multiple_of(block * BLOCK[section] + row, 16)
        rows = last - first
        copies.append((ref.at[pl.ds(first, rows)], targets[section].at[pl.ds(to, rows)]))
    return copies


COPIES = 7


def start_copies(place, own, near, swapped, targets, sems):
    for me in range(2):

        @pl.when(place[0] == me)
        def _():
            cls = place[1]
            pairs = [[] for _ in SECTIONS]
            for section, ref in enumerate(own):
                to = pl.multiple_of(cls * BLOCK[section], 16)
                pairs[section].append((ref, targets[section].at[pl.ds(to, BLOCK[section])]))
            for flip, ref, other in zip((2, 1, 3), near, swapped):
                for half in range(2):
                    source = ref if half == me else other
                    for section, pair in enumerate(part_copies(source, half, cls ^ flip, targets)):
                        pairs[section].append(pair)
            for section in (1, 0, 2):
                for i, (a, z) in enumerate(pairs[section]):
                    pltpu.make_async_copy(a, z, sems.at[section * COPIES + i]).start()


def wait_copies(section, own, targets, sems):
    first, last = SECTIONS[section][1:]
    sizes = [BLOCK[section]] + [last - first, last - first - 16] * 3
    for i, n in enumerate(sizes):
        a, z = own[section].at[pl.ds(0, n)], targets[section].at[pl.ds(0, n)]
        pltpu.make_async_copy(a, z, sems.at[section * COPIES + i]).wait()


def temporal_forward_kernel(
    place, sent, factors, own_qkv, own_so, own_out, b, c, d, other_b, other_c, other_d,
    out_keep, out_send, w_so, w_out, w_qkv, q_out, k_out, v_out, probs_out, mixed_out,
    unit_out, inverse_out, project_out, sems,
):
    own, targets = (own_qkv, own_so, own_out), (w_qkv, w_so, w_out)
    start_copies(place, own, (b, c, d), (other_b, other_c, other_d), targets, sems)
    tokens, cotangent, mixed_s = sent[:, :D], sent[:, D : 2 * D], sent[:, 2 * D :]
    gate_s, shift, scale, gate_t = (factors[i : i + 1, :] for i in range(4))
    wait_copies(1, own, targets, sems)
    project = nn(mixed_s, w_so[...])
    project_out[...] = project
    hidden = (tokens.astype(F32) + gate_s * project).astype(BF).astype(F32)
    centered = hidden - jnp.mean(hidden, -1, keepdims=True)
    inverse = lax.rsqrt(jnp.mean(centered * centered, -1, keepdims=True) + 1e-06)
    inverse_out[...] = jnp.broadcast_to(inverse, (ROWS, 128))
    unit = centered * inverse
    unit_out[...] = unit
    normed = (unit * (1.0 + scale) + shift).astype(BF)
    wait_copies(0, own, targets, sems)
    q, k, v = (nt(normed, w_qkv[i * ATT : (i + 1) * ATT, :]).astype(BF) for i in range(3))
    q_out[...], k_out[...], v_out[...] = q, k, v

    row = lax.broadcasted_iota(jnp.int32, (HEADS * ROWS, ROWS), 0)
    col = lax.broadcasted_iota(jnp.int32, (HEADS * ROWS, ROWS), 1)
    same = ((row ^ col) & 1) == 0
    _, probs, _, mixed = attend(head_masks(), q, k, v, same)
    probs_out[...] = probs
    mixed_out[...] = mixed

    scaled = (cotangent.astype(F32) * gate_t).astype(BF)
    left, right = scaled[:, :ATT], scaled[:, ATT:]
    first = place[0] == 0
    out_keep[...] = tn(mixed, jnp.where(first, left, right))
    out_send[...] = tn(mixed, jnp.where(first, right, left)).astype(BF)
    wait_copies(2, own, targets, sems)


def temporal_backward_kernel(
    sent, factors, w_so, w_out, w_qkv, q, k, v, probs, mixed, unit, inverse, project, packed
):
    scale, gate_t = factors[2:3, :], factors[3:4, :]
    cot = sent[:, D : 2 * D].astype(F32)
    scaled = (cot * gate_t).astype(BF)
    masks = head_masks()
    q, k, v, probs = q[...], k[...], v[...], probs[...]
    d_mixed = nt(scaled, w_out[...]).astype(BF)
    q_stack = stack_heads(masks, q)
    d_q, d_k, d_v = attend_back(masks, q_stack, k, v, probs, probs.astype(BF), d_mixed)
    wq, wk, wv = (w_qkv[i * ATT : (i + 1) * ATT, :] for i in range(3))
    d_normed = (nn(d_q, wq) + nn(d_k, wk) + nn(d_v, wv)).astype(BF).astype(F32)
    unit = unit[...]
    d_unit = d_normed * (1.0 + scale)
    d_hidden = inverse[:, 0:1] * (
        d_unit
        - jnp.mean(d_unit, -1, keepdims=True)
        - unit * jnp.mean(d_unit * unit, -1, keepdims=True)
    )
    grad = (cot + d_hidden).astype(BF)
    packed[:, :D] = grad
    project_t = nn(mixed[...], w_out[...])
    factor_grads = (
        jnp.sum(grad.astype(F32) * project[...], 0, keepdims=True),
        jnp.sum(d_normed, 0, keepdims=True),
        jnp.sum(d_normed * unit, 0, keepdims=True),
        jnp.sum(cot * project_t, 0, keepdims=True),
    )
    zeros = jnp.zeros((16, 64), BF)
    for parity in range(2):
        rows = [
            factor_grads[2 * parity + core][:, part * ATT : part * ATT + ATT]
            for core in range(2)
            for part in range(2)
        ]
        tile = jnp.concatenate([jnp.concatenate(rows * 4, 0).astype(BF), zeros], 1)
        for yhi in (parity, parity + 2):
            packed[32 * yhi : 32 * yhi + 16, D:] = tile
            packed[32 * yhi + 16 : 32 * yhi + 32, D:] = tile


def call(kernel, outs, *args, scalars=0, remote=0, scratch=(), flops=10**9):
    vmem = pl.BlockSpec(memory_space=pltpu.VMEM)
    specs = [pl.BlockSpec(memory_space=pltpu.SMEM)] * scalars
    specs += [vmem] * (len(args) - scalars - remote)
    specs += [pl.BlockSpec(memory_space=pl.ANY)] * remote
    return pl.pallas_call(
        kernel,
        out_shape=[jax.ShapeDtypeStruct(s, d) for s, d in outs],
        in_specs=specs,
        out_specs=[vmem] * len(outs),
        scratch_shapes=list(scratch),
        compiler_params=pltpu.CompilerParams(vmem_limit_bytes=32 * 2**20),
        cost_estimate=pl.CostEstimate(flops=flops, bytes_accessed=10**7, transcendentals=10**5),
    )(*args)


def exchange(a):
    return lax.all_to_all(a, SEQ, 0, 0, tiled=True)


AXES = DP + SEQ


def device(x, y, z, core):
    ylo, yhi = y % 2, (y % 8) // 2
    return ((((x % 4) * 2 + ylo) * 4 + yhi) * 8 + z % 8) * 2 + core


def receive(a, source):
    pairs = []
    for x in range(4):
        for y in range(8):
            for z in range(8):
                for core in range(2):
                    pairs.append((device(*source(x, y, z, core), core), device(x, y, z, core)))
    return lax.ppermute(a, AXES, pairs)


def swap_cores(a):
    return lax.ppermute(a, "core", [(0, 1), (1, 0)])


def class_source(x, y, z, core):
    ylo, yhi = y % 2, y // 2
    cls = (x % 2) * 2 + ylo
    return (x // 2) * 2 + yhi // 2, cls * 2 + yhi % 2, z


def near_source(dx, dy):
    def source(x, y, z, core):
        sign = 1 - 2 * core
        return x + sign * dx, y + sign * dy, z

    return source


def gather_weights(w_so, w_qkv, w_out, place, sent):
    shard = jnp.concatenate([w_so, w_out, w_qkv.T, jnp.zeros((3, D), BF)], 0)
    shard, sent = lax.optimization_barrier((receive(shard, class_source), sent))
    sent = exchange(sent).reshape(ROWS, 2 * D + ATT)
    mine = lax.all_gather(shard, "z", axis=0, tiled=True)
    other = swap_cores(mine)
    rows = lambda n: ((n, D), BF)
    own_so, own_out, own_qkv, part = call(
        compact_kernel, [rows(144), rows(144), rows(432), rows(384)], place, mine, other, scalars=1,
        scratch=[
            pltpu.VMEM((2, 384, D), BF),
            pltpu.VMEM((144, D), F32),
            pltpu.VMEM((144, D), F32),
            pltpu.VMEM((432, D), F32),
        ],
    )
    part, sent = lax.optimization_barrier((part, sent))
    near = [receive(part, near_source(dx, dy)) for dx, dy in ((1, 0), (0, 1), (1, 1))]
    return [own_qkv, own_so, own_out] + near + [swap_cores(a) for a in near], sent


def body(tokens, qkv, w_so, w_qkv, w_out, factors, cotangent):
    tokens, qkv, cotangent, factors = tokens[0, 0], qkv[0, 0], cotangent[0, 0], factors[0]
    core = lax.axis_index("core")
    cls = (lax.axis_index("x") % 2) * 2 + lax.axis_index("ylo")
    place = jnp.stack([core, cls]).astype(jnp.int32)

    (mixed_s,) = call(spatial_forward_kernel, [((ROWS, ATT), BF)], qkv)
    sent = jnp.concatenate([tokens, cotangent, mixed_s], 1).reshape(64, 2, 2 * D + ATT)
    weights, sent = gather_weights(w_so, w_qkv, w_out, place, sent)

    rows = lambda n, kind=BF: ((ROWS, n), kind)
    out_keep, out_send, *saved = call(
        temporal_forward_kernel,
        [
            ((ATT, ATT), F32), ((ATT, ATT), BF), ((ATT, D), BF), ((ATT, D), BF), ((3 * ATT, D), BF),
            rows(ATT), rows(ATT), rows(ATT), ((HEADS * ROWS, ROWS), F32), rows(ATT),
            rows(D, F32), rows(128, F32), rows(D, F32),
        ],
        place, sent, factors, *weights,
        scalars=1, remote=len(weights), flops=4 * 10**9,
        scratch=[pltpu.SemaphoreType.DMA((24,))],
    )
    w_so = saved[0]
    out_other = swap_cores(out_send)
    (packed,) = call(temporal_backward_kernel, [rows(D + 640)], sent, factors, *saved, flops=4 * 10**9)

    half = 9 * ATT // 2
    out_part = (out_keep + out_other.astype(F32)).astype(BF).reshape(64, 2, half)
    back = exchange(jnp.concatenate([packed.reshape(64, 2, D + 640), out_part], 2))

    out_part = back[:, :, D + 640 :].astype(F32).reshape(32, 2, 2, half)
    out_part = jnp.sum(out_part, 0).astype(BF).reshape(1, 2, 9 * ATT)
    out_part = jnp.broadcast_to(out_part, (8, 2, 9 * ATT))
    out_part = jnp.sum(lax.all_to_all(out_part, DP, 0, 0, tiled=True).astype(F32), 0)
    out_grad = out_part.reshape(2, 9, ATT).transpose(1, 0, 2).reshape(9, D)

    token_grad = back[:, :, :D].reshape(ROWS, D)
    mine = jnp.sum(back[:, :, D : D + ATT].astype(F32), 0).reshape(1, D)
    other = swap_cores(mine)
    rows = jnp.where(core == 0, jnp.concatenate([mine, other]), jnp.concatenate([other, mine]))
    rows, token_grad = lax.optimization_barrier((rows, token_grad))
    other = lax.ppermute(rows, "yhi", [(0, 1), (1, 0), (2, 3), (3, 2)])
    (qkv_grad,) = call(
        spatial_backward_kernel, [((ROWS, 3 * ATT), BF)], qkv, token_grad, factors, w_so
    )
    low = lax.axis_index("yhi") % 2 == 0
    factor_grad = jnp.where(low, jnp.concatenate([rows, other]), jnp.concatenate([other, rows]))
    return token_grad[None, None], qkv_grad[None, None], factor_grad[None], out_grad


def solution(mesh):
    fine = Mesh(mesh.devices.reshape(4, 2, 4, 8, 2), DP + SEQ)
    frames = P(DP, SEQ, None, None)
    return jax.shard_map(
        body,
        mesh=fine,
        in_specs=(
            frames,
            frames,
            P(SEQ, None),
            P(None, SEQ),
            P(SEQ, None),
            P(DP, None, None),
            frames,
        ),
        out_specs=(frames, frames, P(DP, None, None), P(SEQ, None)),
        check_vma=False,
    )
```

```python
import math

import jax
import jax.numpy as jnp
from jax import lax
from jax.experimental import pallas as pl
from jax.experimental.pallas import tpu as pltpu
from jax.sharding import Mesh
from jax.sharding import PartitionSpec as P

D = 1152
HEADS = 8
HS = 72
ATT = 576
ROWS = 128
SCALE = 1.0 / math.sqrt(HS)
SEQ = ("yhi", "z", "core")
CHIPS = ("yhi", "z")
DP = ("x", "ylo")
BF = jnp.bfloat16
F32 = jnp.float32


def nn(a, b):
    return lax.dot_general(a, b, (((1,), (0,)), ((), ())), preferred_element_type=F32)


def nt(a, b):
    return lax.dot_general(a, b, (((1,), (1,)), ((), ())), preferred_element_type=F32)


def tn(a, b):
    return lax.dot_general(a, b, (((0,), (0,)), ((), ())), preferred_element_type=F32)


def head_masks():
    head = lax.broadcasted_iota(jnp.int32, (ROWS, ATT), 1) // HS
    return [head == h for h in range(HEADS)]


def stack_heads(masks, a):
    zero = jnp.zeros_like(a)
    return jnp.concatenate([jnp.where(m, a, zero) for m in masks], 0)


def pick_heads(masks, a):
    out = a[:ROWS]
    for h in range(1, HEADS):
        out = jnp.where(masks[h], a[h * ROWS : (h + 1) * ROWS], out)
    return out


def softmax_rows(scores):
    top = jnp.max(scores, -1, keepdims=True)
    weights = jnp.exp(scores - top)
    return weights / jnp.sum(weights, -1, keepdims=True)


def attend(masks, q, k, v, same):
    q_stack = stack_heads(masks, q)
    scores = nt(q_stack, k) * SCALE
    if same is not None:
        scores = jnp.where(same, scores, -1e30)
    probs = softmax_rows(scores)
    probs_b = probs.astype(BF)
    mixed = pick_heads(masks, nn(probs_b, v)).astype(BF)
    return q_stack, probs, probs_b, mixed


def attend_back(masks, q_stack, k, v, probs, probs_b, d_mixed):
    d_stack = stack_heads(masks, d_mixed)
    d_probs = nt(d_stack, v).astype(BF).astype(F32)
    d_v = tn(probs_b, d_stack)
    d_scores = probs * (d_probs - jnp.sum(d_probs * probs, -1, keepdims=True)) * SCALE
    d_scores = d_scores.astype(BF)
    d_q = pick_heads(masks, nn(d_scores, k))
    d_k = tn(d_scores, q_stack)
    return d_q.astype(BF), d_k.astype(BF), d_v.astype(BF)


def spatial_forward_kernel(qkv, mixed):
    q, k, v = qkv[:, :ATT], qkv[:, ATT : 2 * ATT], qkv[:, 2 * ATT :]
    mixed[...] = attend(head_masks(), q, k, v, None)[3]


def spatial_backward_kernel(qkv, hidden_grad, factors, w_so, out):
    q, k, v = qkv[:, :ATT], qkv[:, ATT : 2 * ATT], qkv[:, 2 * ATT :]
    masks = head_masks()
    gated = (hidden_grad[...].astype(F32) * factors[0:1, :]).astype(BF)
    d_mixed = nt(gated, w_so[...]).astype(BF)
    q_stack, probs, probs_b, _ = attend(masks, q, k, v, None)
    d_q, d_k, d_v = attend_back(masks, q_stack, k, v, probs, probs_b, d_mixed)
    out[:, :ATT] = d_q
    out[:, ATT : 2 * ATT] = d_k
    out[:, 2 * ATT :] = d_v


def compact_kernel(place, mine, other, own_so, own_out, own_qkv, part, both, so, out, qkv):
    core = place[0]
    both[core] = mine[...]
    both[1 - core] = other[...]
    for i in range(16):
        shard = both[i % 2, 48 * (i // 2) : 48 * (i // 2) + 48, :].astype(F32)
        so[9 * i : 9 * i + 9, :] = shard[:9]
        out[9 * i : 9 * i + 9, :] = shard[9:18]
        qkv[27 * i : 27 * i + 27, :] = shard[18:45]
    own_so[...] = so[...].astype(BF)
    own_out[...] = out[...].astype(BF)
    own_qkv[...] = qkv[...].astype(BF)
    at_qkv = pl.multiple_of(core * 208, 16)
    at = pl.multiple_of(core * 64, 16)
    part[0:224, :] = own_qkv[pl.ds(at_qkv, 224), :]
    part[224:304, :] = own_so[pl.ds(at, 80), :]
    part[304:384, :] = own_out[pl.ds(at, 80), :]


SECTIONS = ((0, 0, 224), (1, 224, 304), (2, 304, 384))
BLOCK = (432, 144, 144)
STEP = (208, 64, 64)


def assemble(place, own, near, swapped, targets):
    for me in range(2):

        @pl.when(place[0] == me)
        def _():
            cls = place[1]
            for section, ref in enumerate(own):
                to = pl.multiple_of(cls * BLOCK[section], 16)
                targets[section][pl.ds(to, BLOCK[section]), :] = ref[...]
            for flip, ref, other in zip((2, 1, 3), near, swapped):
                for half in range(2):
                    source = ref if half == me else other
                    for section, first, last in SECTIONS:
                        skip = 16 * half
                        row = skip + STEP[section] * half
                        to = pl.multiple_of((cls ^ flip) * BLOCK[section] + row, 16)
                        rows = last - first - skip
                        targets[section][pl.ds(to, rows), :] = source[first + skip : last, :]


def temporal_forward_kernel(
    place, sent, factors, own_qkv, own_so, own_out, b, c, d, other_b, other_c, other_d,
    out_keep, out_send, w_so, w_out, w_qkv, q_out, k_out, v_out, probs_out, mixed_out,
    unit_out, inverse_out, project_out,
):
    assemble(
        place, (own_qkv, own_so, own_out), (b, c, d), (other_b, other_c, other_d),
        (w_qkv, w_so, w_out),
    )
    tokens, cotangent, mixed_s = sent[:, :D], sent[:, D : 2 * D], sent[:, 2 * D :]
    gate_s, shift, scale, gate_t = (factors[i : i + 1, :] for i in range(4))
    project = nn(mixed_s, w_so[...])
    project_out[...] = project
    hidden = (tokens.astype(F32) + gate_s * project).astype(BF).astype(F32)
    centered = hidden - jnp.mean(hidden, -1, keepdims=True)
    inverse = lax.rsqrt(jnp.mean(centered * centered, -1, keepdims=True) + 1e-06)
    inverse_out[...] = jnp.broadcast_to(inverse, (ROWS, 128))
    unit = centered * inverse
    unit_out[...] = unit
    normed = (unit * (1.0 + scale) + shift).astype(BF)
    q, k, v = (nt(normed, w_qkv[i * ATT : (i + 1) * ATT, :]).astype(BF) for i in range(3))
    q_out[...], k_out[...], v_out[...] = q, k, v

    row = lax.broadcasted_iota(jnp.int32, (HEADS * ROWS, ROWS), 0)
    col = lax.broadcasted_iota(jnp.int32, (HEADS * ROWS, ROWS), 1)
    same = ((row ^ col) & 1) == 0
    _, probs, _, mixed = attend(head_masks(), q, k, v, same)
    probs_out[...] = probs
    mixed_out[...] = mixed

    scaled = (cotangent.astype(F32) * gate_t).astype(BF)
    left, right = scaled[:, :ATT], scaled[:, ATT:]
    first = place[0] == 0
    out_keep[...] = tn(mixed, jnp.where(first, left, right))
    out_send[...] = tn(mixed, jnp.where(first, right, left)).astype(BF)


def temporal_backward_kernel(
    sent, factors, w_so, w_out, w_qkv, q, k, v, probs, mixed, unit, inverse, project, packed
):
    scale, gate_t = factors[2:3, :], factors[3:4, :]
    cot = sent[:, D : 2 * D].astype(F32)
    scaled = (cot * gate_t).astype(BF)
    masks = head_masks()
    q, k, v, probs = q[...], k[...], v[...], probs[...]
    d_mixed = nt(scaled, w_out[...]).astype(BF)
    q_stack = stack_heads(masks, q)
    d_q, d_k, d_v = attend_back(masks, q_stack, k, v, probs, probs.astype(BF), d_mixed)
    wq, wk, wv = (w_qkv[i * ATT : (i + 1) * ATT, :] for i in range(3))
    d_normed = (nn(d_q, wq) + nn(d_k, wk) + nn(d_v, wv)).astype(BF).astype(F32)
    unit = unit[...]
    d_unit = d_normed * (1.0 + scale)
    d_hidden = inverse[:, 0:1] * (
        d_unit
        - jnp.mean(d_unit, -1, keepdims=True)
        - unit * jnp.mean(d_unit * unit, -1, keepdims=True)
    )
    grad = (cot + d_hidden).astype(BF)
    packed[:, :D] = grad
    project_t = nn(mixed[...], w_out[...])
    factor_grads = (
        jnp.sum(grad.astype(F32) * project[...], 0, keepdims=True),
        jnp.sum(d_normed, 0, keepdims=True),
        jnp.sum(d_normed * unit, 0, keepdims=True),
        jnp.sum(cot * project_t, 0, keepdims=True),
    )
    zeros = jnp.zeros((16, 64), BF)
    for parity in range(2):
        rows = [
            factor_grads[2 * parity + core][:, part * ATT : part * ATT + ATT]
            for core in range(2)
            for part in range(2)
        ]
        tile = jnp.concatenate([jnp.concatenate(rows * 4, 0).astype(BF), zeros], 1)
        for yhi in (parity, parity + 2):
            packed[32 * yhi : 32 * yhi + 16, D:] = tile
            packed[32 * yhi + 16 : 32 * yhi + 32, D:] = tile


def call(kernel, outs, *args, scalars=0, scratch=(), flops=10**9):
    vmem = pl.BlockSpec(memory_space=pltpu.VMEM)
    return pl.pallas_call(
        kernel,
        out_shape=[jax.ShapeDtypeStruct(s, d) for s, d in outs],
        in_specs=[pl.BlockSpec(memory_space=pltpu.SMEM)] * scalars + [vmem] * (len(args) - scalars),
        out_specs=[vmem] * len(outs),
        scratch_shapes=list(scratch),
        compiler_params=pltpu.CompilerParams(vmem_limit_bytes=32 * 2**20),
        cost_estimate=pl.CostEstimate(flops=flops, bytes_accessed=10**7, transcendentals=10**5),
    )(*args)


def exchange(a):
    return lax.all_to_all(a, SEQ, 0, 0, tiled=True)


AXES = DP + SEQ


def device(x, y, z, core):
    ylo, yhi = y % 2, (y % 8) // 2
    return ((((x % 4) * 2 + ylo) * 4 + yhi) * 8 + z % 8) * 2 + core


def receive(a, source):
    pairs = []
    for x in range(4):
        for y in range(8):
            for z in range(8):
                for core in range(2):
                    pairs.append((device(*source(x, y, z, core), core), device(x, y, z, core)))
    return lax.ppermute(a, AXES, pairs)


def swap_cores(a):
    return lax.ppermute(a, "core", [(0, 1), (1, 0)])


def class_source(x, y, z, core):
    ylo, yhi = y % 2, y // 2
    cls = (x % 2) * 2 + ylo
    return (x // 2) * 2 + yhi // 2, cls * 2 + yhi % 2, z


def near_source(dx, dy):
    def source(x, y, z, core):
        sign = 1 - 2 * core
        return x + sign * dx, y + sign * dy, z

    return source


def gather_weights(w_so, w_qkv, w_out, place, sent):
    shard = jnp.concatenate([w_so, w_out, w_qkv.T, jnp.zeros((3, D), BF)], 0)
    mine = lax.all_gather(receive(shard, class_source), "z", axis=0, tiled=True)
    mine, sent = lax.optimization_barrier((mine, sent))
    sent = exchange(sent).reshape(ROWS, 2 * D + ATT)
    other = swap_cores(mine)
    rows = lambda n: ((n, D), BF)
    own_so, own_out, own_qkv, part = call(
        compact_kernel, [rows(144), rows(144), rows(432), rows(384)], place, mine, other, scalars=1,
        scratch=[
            pltpu.VMEM((2, 384, D), BF),
            pltpu.VMEM((144, D), F32),
            pltpu.VMEM((144, D), F32),
            pltpu.VMEM((432, D), F32),
        ],
    )
    near = [receive(part, near_source(dx, dy)) for dx, dy in ((1, 0), (0, 1), (1, 1))]
    near[2], sent = lax.optimization_barrier((near[2], sent))
    return [own_qkv, own_so, own_out] + near + [swap_cores(a) for a in near], sent


def body(tokens, qkv, w_so, w_qkv, w_out, factors, cotangent):
    tokens, qkv, cotangent, factors = tokens[0, 0], qkv[0, 0], cotangent[0, 0], factors[0]
    core = lax.axis_index("core")
    cls = (lax.axis_index("x") % 2) * 2 + lax.axis_index("ylo")
    place = jnp.stack([core, cls]).astype(jnp.int32)

    (mixed_s,) = call(spatial_forward_kernel, [((ROWS, ATT), BF)], qkv)
    sent = jnp.concatenate([tokens, cotangent, mixed_s], 1).reshape(64, 2, 2 * D + ATT)
    weights, sent = gather_weights(w_so, w_qkv, w_out, place, sent)

    rows = lambda n, kind=BF: ((ROWS, n), kind)
    out_keep, out_send, *saved = call(
        temporal_forward_kernel,
        [
            ((ATT, ATT), F32), ((ATT, ATT), BF), ((ATT, D), BF), ((ATT, D), BF), ((3 * ATT, D), BF),
            rows(ATT), rows(ATT), rows(ATT), ((HEADS * ROWS, ROWS), F32), rows(ATT),
            rows(D, F32), rows(128, F32), rows(D, F32),
        ],
        place, sent, factors, *weights,
        scalars=1, flops=4 * 10**9,
    )
    w_so = saved[0]
    out_other = swap_cores(out_send)
    (packed,) = call(temporal_backward_kernel, [rows(D + 640)], sent, factors, *saved, flops=4 * 10**9)

    half = 9 * ATT // 2
    out_part = (out_keep + out_other.astype(F32)).astype(BF).reshape(64, 2, half)
    back = exchange(jnp.concatenate([packed.reshape(64, 2, D + 640), out_part], 2))

    out_part = back[:, :, D + 640 :].astype(F32).reshape(32, 2, 2, half)
    out_part = jnp.sum(out_part, 0).astype(BF).reshape(1, 2, 9 * ATT)
    out_part = jnp.broadcast_to(out_part, (8, 2, 9 * ATT))
    out_part, back = lax.optimization_barrier((out_part, back))
    out_part = jnp.sum(lax.all_to_all(out_part, DP, 0, 0, tiled=True).astype(F32), 0)
    out_grad = out_part.reshape(2, 9, ATT).transpose(1, 0, 2).reshape(9, D)

    token_grad = back[:, :, :D].reshape(ROWS, D)
    mine = jnp.sum(back[:, :, D : D + ATT].astype(F32), 0).reshape(1, D)
    other = swap_cores(mine)
    rows = jnp.where(core == 0, jnp.concatenate([mine, other]), jnp.concatenate([other, mine]))
    rows, token_grad = lax.optimization_barrier((rows, token_grad))
    other = lax.ppermute(rows, "yhi", [(0, 1), (1, 0), (2, 3), (3, 2)])
    (qkv_grad,) = call(
        spatial_backward_kernel, [((ROWS, 3 * ATT), BF)], qkv, token_grad, factors, w_so
    )
    low = lax.axis_index("yhi") % 2 == 0
    factor_grad = jnp.where(low, jnp.concatenate([rows, other]), jnp.concatenate([other, rows]))
    return token_grad[None, None], qkv_grad[None, None], factor_grad[None], out_grad


def solution(mesh):
    fine = Mesh(mesh.devices.reshape(4, 2, 4, 8, 2), DP + SEQ)
    frames = P(DP, SEQ, None, None)
    return jax.shard_map(
        body,
        mesh=fine,
        in_specs=(
            frames,
            frames,
            P(SEQ, None),
            P(None, SEQ),
            P(SEQ, None),
            P(DP, None, None),
            frames,
        ),
        out_specs=(frames, frames, P(DP, None, None), P(SEQ, None)),
        check_vma=False,
    )
```

```python
import math

import jax
import jax.numpy as jnp
from jax import lax
from jax.experimental import pallas as pl
from jax.experimental.pallas import tpu as pltpu
from jax.sharding import Mesh
from jax.sharding import PartitionSpec as P

D = 1152
HEADS = 8
HS = 72
ATT = 576
ROWS = 128
SCALE = 1.0 / math.sqrt(HS)
SEQ = ("yhi", "z", "core")
CHIPS = ("yhi", "z")
DP = ("x", "ylo")
BF = jnp.bfloat16
F32 = jnp.float32


def nn(a, b):
    return lax.dot_general(a, b, (((1,), (0,)), ((), ())), preferred_element_type=F32)


def nt(a, b):
    return lax.dot_general(a, b, (((1,), (1,)), ((), ())), preferred_element_type=F32)


def tn(a, b):
    return lax.dot_general(a, b, (((0,), (0,)), ((), ())), preferred_element_type=F32)


def head_masks():
    head = lax.broadcasted_iota(jnp.int32, (ROWS, ATT), 1) // HS
    return [head == h for h in range(HEADS)]


def stack_heads(masks, a):
    zero = jnp.zeros_like(a)
    return jnp.concatenate([jnp.where(m, a, zero) for m in masks], 0)


def pick_heads(masks, a):
    out = a[:ROWS]
    for h in range(1, HEADS):
        out = jnp.where(masks[h], a[h * ROWS : (h + 1) * ROWS], out)
    return out


def softmax_rows(scores):
    top = jnp.max(scores, -1, keepdims=True)
    weights = jnp.exp(scores - top)
    return weights / jnp.sum(weights, -1, keepdims=True)


def attend(masks, q, k, v, same):
    q_stack = stack_heads(masks, q)
    scores = nt(q_stack, k) * SCALE
    if same is not None:
        scores = jnp.where(same, scores, -1e30)
    probs = softmax_rows(scores)
    probs_b = probs.astype(BF)
    mixed = pick_heads(masks, nn(probs_b, v)).astype(BF)
    return q_stack, probs, probs_b, mixed


def attend_back(masks, q_stack, k, v, probs, probs_b, d_mixed):
    d_stack = stack_heads(masks, d_mixed)
    d_probs = nt(d_stack, v).astype(BF).astype(F32)
    d_v = tn(probs_b, d_stack)
    d_scores = probs * (d_probs - jnp.sum(d_probs * probs, -1, keepdims=True)) * SCALE
    d_scores = d_scores.astype(BF)
    d_q = pick_heads(masks, nn(d_scores, k))
    d_k = tn(d_scores, q_stack)
    return d_q.astype(BF), d_k.astype(BF), d_v.astype(BF)


def spatial_forward_kernel(qkv, mixed):
    q, k, v = qkv[:, :ATT], qkv[:, ATT : 2 * ATT], qkv[:, 2 * ATT :]
    mixed[...] = attend(head_masks(), q, k, v, None)[3]


def spatial_backward_kernel(qkv, hidden_grad, factors, w_so, out):
    q, k, v = qkv[:, :ATT], qkv[:, ATT : 2 * ATT], qkv[:, 2 * ATT :]
    masks = head_masks()
    gated = (hidden_grad[...].astype(F32) * factors[0:1, :]).astype(BF)
    d_mixed = nt(gated, w_so[...]).astype(BF)
    q_stack, probs, probs_b, _ = attend(masks, q, k, v, None)
    d_q, d_k, d_v = attend_back(masks, q_stack, k, v, probs, probs_b, d_mixed)
    out[:, :ATT] = d_q
    out[:, ATT : 2 * ATT] = d_k
    out[:, 2 * ATT :] = d_v


def compact_kernel(place, mine, other, own_so, own_out, own_qkv, part, both, so, out, qkv):
    core = place[0]
    both[core] = mine[...]
    both[1 - core] = other[...]
    for i in range(16):
        shard = both[i % 2, 48 * (i // 2) : 48 * (i // 2) + 48, :].astype(F32)
        so[9 * i : 9 * i + 9, :] = shard[:9]
        out[9 * i : 9 * i + 9, :] = shard[9:18]
        qkv[27 * i : 27 * i + 27, :] = shard[18:45]
    own_so[...] = so[...].astype(BF)
    own_out[...] = out[...].astype(BF)
    own_qkv[...] = qkv[...].astype(BF)
    at_qkv = pl.multiple_of(core * 208, 16)
    at = pl.multiple_of(core * 64, 16)
    part[0:224, :] = own_qkv[pl.ds(at_qkv, 224), :]
    part[224:304, :] = own_so[pl.ds(at, 80), :]
    part[304:384, :] = own_out[pl.ds(at, 80), :]


SECTIONS = ((0, 0, 224), (1, 224, 304), (2, 304, 384))
BLOCK = (432, 144, 144)
STEP = (208, 64, 64)


def assemble(place, own, near, swapped, targets):
    for me in range(2):

        @pl.when(place[0] == me)
        def _():
            cls = place[1]
            for section, ref in enumerate(own):
                to = pl.multiple_of(cls * BLOCK[section], 16)
                targets[section][pl.ds(to, BLOCK[section]), :] = ref[...]
            for flip, ref, other in zip((2, 1, 3), near, swapped):
                for half in range(2):
                    source = ref if half == me else other
                    for section, first, last in SECTIONS:
                        skip = 16 * half
                        row = skip + STEP[section] * half
                        to = pl.multiple_of((cls ^ flip) * BLOCK[section] + row, 16)
                        rows = last - first - skip
                        targets[section][pl.ds(to, rows), :] = source[first + skip : last, :]


def temporal_forward_kernel(
    place, sent, factors, own_qkv, own_so, own_out, b, c, d, other_b, other_c, other_d,
    out_keep, out_send, w_so, w_out, w_qkv, q_out, k_out, v_out, probs_out, mixed_out,
    unit_out, inverse_out, project_out,
):
    assemble(
        place, (own_qkv, own_so, own_out), (b, c, d), (other_b, other_c, other_d),
        (w_qkv, w_so, w_out),
    )
    tokens, cotangent, mixed_s = sent[:, :D], sent[:, D : 2 * D], sent[:, 2 * D :]
    gate_s, shift, scale, gate_t = (factors[i : i + 1, :] for i in range(4))
    project = nn(mixed_s, w_so[...])
    project_out[...] = project
    hidden = (tokens.astype(F32) + gate_s * project).astype(BF).astype(F32)
    centered = hidden - jnp.mean(hidden, -1, keepdims=True)
    inverse = lax.rsqrt(jnp.mean(centered * centered, -1, keepdims=True) + 1e-06)
    inverse_out[...] = jnp.broadcast_to(inverse, (ROWS, 128))
    unit = centered * inverse
    unit_out[...] = unit
    normed = (unit * (1.0 + scale) + shift).astype(BF)
    q, k, v = (nt(normed, w_qkv[i * ATT : (i + 1) * ATT, :]).astype(BF) for i in range(3))
    q_out[...], k_out[...], v_out[...] = q, k, v

    row = lax.broadcasted_iota(jnp.int32, (HEADS * ROWS, ROWS), 0)
    col = lax.broadcasted_iota(jnp.int32, (HEADS * ROWS, ROWS), 1)
    same = ((row ^ col) & 1) == 0
    _, probs, _, mixed = attend(head_masks(), q, k, v, same)
    probs_out[...] = probs
    mixed_out[...] = mixed

    scaled = (cotangent.astype(F32) * gate_t).astype(BF)
    left, right = scaled[:, :ATT], scaled[:, ATT:]
    first = place[0] == 0
    out_keep[...] = tn(mixed, jnp.where(first, left, right))
    out_send[...] = tn(mixed, jnp.where(first, right, left)).astype(BF)


def temporal_backward_kernel(
    sent, factors, w_so, w_out, w_qkv, q, k, v, probs, mixed, unit, inverse, project, packed
):
    scale, gate_t = factors[2:3, :], factors[3:4, :]
    cot = sent[:, D : 2 * D].astype(F32)
    scaled = (cot * gate_t).astype(BF)
    masks = head_masks()
    q, k, v, probs = q[...], k[...], v[...], probs[...]
    d_mixed = nt(scaled, w_out[...]).astype(BF)
    q_stack = stack_heads(masks, q)
    d_q, d_k, d_v = attend_back(masks, q_stack, k, v, probs, probs.astype(BF), d_mixed)
    wq, wk, wv = (w_qkv[i * ATT : (i + 1) * ATT, :] for i in range(3))
    d_normed = (nn(d_q, wq) + nn(d_k, wk) + nn(d_v, wv)).astype(BF).astype(F32)
    unit = unit[...]
    d_unit = d_normed * (1.0 + scale)
    d_hidden = inverse[:, 0:1] * (
        d_unit
        - jnp.mean(d_unit, -1, keepdims=True)
        - unit * jnp.mean(d_unit * unit, -1, keepdims=True)
    )
    grad = (cot + d_hidden).astype(BF)
    packed[:, :D] = grad
    project_t = nn(mixed[...], w_out[...])
    factor_grads = (
        jnp.sum(grad.astype(F32) * project[...], 0, keepdims=True),
        jnp.sum(d_normed, 0, keepdims=True),
        jnp.sum(d_normed * unit, 0, keepdims=True),
        jnp.sum(cot * project_t, 0, keepdims=True),
    )
    tile = jnp.concatenate(factor_grads * 4, 0).astype(BF)
    for i in range(8):
        packed[16 * i : 16 * i + 16, D:] = tile


def call(kernel, outs, *args, scalars=0, scratch=(), flops=10**9):
    vmem = pl.BlockSpec(memory_space=pltpu.VMEM)
    return pl.pallas_call(
        kernel,
        out_shape=[jax.ShapeDtypeStruct(s, d) for s, d in outs],
        in_specs=[pl.BlockSpec(memory_space=pltpu.SMEM)] * scalars + [vmem] * (len(args) - scalars),
        out_specs=[vmem] * len(outs),
        scratch_shapes=list(scratch),
        compiler_params=pltpu.CompilerParams(vmem_limit_bytes=20 * 2**20),
        cost_estimate=pl.CostEstimate(flops=flops, bytes_accessed=10**7, transcendentals=10**5),
    )(*args)


def exchange(a):
    return lax.all_to_all(a, SEQ, 0, 0, tiled=True)


AXES = DP + SEQ


def device(x, y, z, core):
    ylo, yhi = y % 2, (y % 8) // 2
    return ((((x % 4) * 2 + ylo) * 4 + yhi) * 8 + z % 8) * 2 + core


def receive(a, source):
    pairs = []
    for x in range(4):
        for y in range(8):
            for z in range(8):
                for core in range(2):
                    pairs.append((device(*source(x, y, z, core), core), device(x, y, z, core)))
    return lax.ppermute(a, AXES, pairs)


def swap_cores(a):
    return lax.ppermute(a, "core", [(0, 1), (1, 0)])


def class_source(x, y, z, core):
    ylo, yhi = y % 2, y // 2
    cls = (x % 2) * 2 + ylo
    return (x // 2) * 2 + yhi // 2, cls * 2 + yhi % 2, z


def near_source(dx, dy):
    def source(x, y, z, core):
        sign = 1 - 2 * core
        return x + sign * dx, y + sign * dy, z

    return source


def gather_weights(w_so, w_qkv, w_out, place, sent):
    shard = jnp.concatenate([w_so, w_out, w_qkv.T, jnp.zeros((3, D), BF)], 0)
    mine = lax.all_gather(receive(shard, class_source), "z", axis=0, tiled=True)
    other = swap_cores(mine)
    rows = lambda n: ((n, D), BF)
    own_so, own_out, own_qkv, part = call(
        compact_kernel, [rows(144), rows(144), rows(432), rows(384)], place, mine, other, scalars=1,
        scratch=[
            pltpu.VMEM((2, 384, D), BF),
            pltpu.VMEM((144, D), F32),
            pltpu.VMEM((144, D), F32),
            pltpu.VMEM((432, D), F32),
        ],
    )
    near = [receive(part, near_source(dx, dy)) for dx, dy in ((1, 0), (0, 1), (1, 1))]
    sent = exchange(lax.optimization_barrier((part, sent))[1]).reshape(ROWS, 2 * D + ATT)
    near[1], sent = lax.optimization_barrier((near[1], sent))
    return [own_qkv, own_so, own_out] + near + [swap_cores(a) for a in near], sent


def body(tokens, qkv, w_so, w_qkv, w_out, factors, cotangent):
    tokens, qkv, cotangent, factors = tokens[0, 0], qkv[0, 0], cotangent[0, 0], factors[0]
    core = lax.axis_index("core")
    cls = (lax.axis_index("x") % 2) * 2 + lax.axis_index("ylo")
    place = jnp.stack([core, cls]).astype(jnp.int32)

    (mixed_s,) = call(spatial_forward_kernel, [((ROWS, ATT), BF)], qkv)
    sent = jnp.concatenate([tokens, cotangent, mixed_s], 1).reshape(64, 2, 2 * D + ATT)
    weights, sent = gather_weights(w_so, w_qkv, w_out, place, sent)

    rows = lambda n, kind=BF: ((ROWS, n), kind)
    out_keep, out_send, *saved = call(
        temporal_forward_kernel,
        [
            ((ATT, ATT), F32), ((ATT, ATT), BF), ((ATT, D), BF), ((ATT, D), BF), ((3 * ATT, D), BF),
            rows(ATT), rows(ATT), rows(ATT), ((HEADS * ROWS, ROWS), F32), rows(ATT),
            rows(D, F32), rows(128, F32), rows(D, F32),
        ],
        place, sent, factors, *weights,
        scalars=1, flops=4 * 10**9,
    )
    w_so = saved[0]
    out_other = swap_cores(out_send)
    (packed,) = call(temporal_backward_kernel, [rows(2 * D)], sent, factors, *saved, flops=4 * 10**9)

    half = 9 * ATT // 2
    out_part = (out_keep + out_other.astype(F32)).astype(BF).reshape(64, 2, half)
    back = exchange(jnp.concatenate([packed.reshape(64, 2, 2 * D), out_part], 2))

    out_part = back[:, :, 2 * D :].astype(F32).reshape(32, 2, 2, half)
    out_part = jnp.sum(out_part, 0).astype(BF).reshape(1, 2, 9 * ATT)
    out_part = jnp.broadcast_to(out_part, (8, 2, 9 * ATT))
    out_part = jnp.sum(lax.all_to_all(out_part, DP, 0, 0, tiled=True).astype(F32), 0)
    out_grad = out_part.reshape(2, 9, ATT).transpose(1, 0, 2).reshape(9, D)

    token_grad = back[:, :, :D].reshape(ROWS, D)
    (qkv_grad,) = call(
        spatial_backward_kernel, [((ROWS, 3 * ATT), BF)], qkv, token_grad, factors, w_so
    )
    mine = jnp.sum(back[:, :, D : 2 * D].astype(F32), 0)
    other = swap_cores(mine)
    factor_grad = jnp.where(core == 0, jnp.concatenate([mine, other]), jnp.concatenate([other, mine]))
    return token_grad[None, None], qkv_grad[None, None], factor_grad[None], out_grad


def solution(mesh):
    fine = Mesh(mesh.devices.reshape(4, 2, 4, 8, 2), DP + SEQ)
    frames = P(DP, SEQ, None, None)
    return jax.shard_map(
        body,
        mesh=fine,
        in_specs=(
            frames,
            frames,
            P(SEQ, None),
            P(None, SEQ),
            P(SEQ, None),
            P(DP, None, None),
            frames,
        ),
        out_specs=(frames, frames, P(DP, None, None), P(SEQ, None)),
        check_vma=False,
    )
```

```python
import math

import jax
import jax.numpy as jnp
from jax import lax
from jax.experimental import pallas as pl
from jax.experimental.pallas import tpu as pltpu
from jax.sharding import Mesh
from jax.sharding import PartitionSpec as P

D = 1152
HEADS = 8
HS = 72
ATT = 576
ROWS = 128
SCALE = 1.0 / math.sqrt(HS)
SEQ = ("yhi", "z", "core")
CHIPS = ("yhi", "z")
DP = ("x", "ylo")
BF = jnp.bfloat16
F32 = jnp.float32


def nn(a, b):
    return lax.dot_general(a, b, (((1,), (0,)), ((), ())), preferred_element_type=F32)


def nt(a, b):
    return lax.dot_general(a, b, (((1,), (1,)), ((), ())), preferred_element_type=F32)


def tn(a, b):
    return lax.dot_general(a, b, (((0,), (0,)), ((), ())), preferred_element_type=F32)


def head_masks():
    head = lax.broadcasted_iota(jnp.int32, (ROWS, ATT), 1) // HS
    return [head == h for h in range(HEADS)]


def stack_heads(masks, a):
    zero = jnp.zeros_like(a)
    return jnp.concatenate([jnp.where(m, a, zero) for m in masks], 0)


def pick_heads(masks, a):
    out = a[:ROWS]
    for h in range(1, HEADS):
        out = jnp.where(masks[h], a[h * ROWS : (h + 1) * ROWS], out)
    return out


def softmax_rows(scores):
    top = jnp.max(scores, -1, keepdims=True)
    weights = jnp.exp(scores - top)
    return weights / jnp.sum(weights, -1, keepdims=True)


def attend(masks, q, k, v, same):
    q_stack = stack_heads(masks, q)
    scores = nt(q_stack, k) * SCALE
    if same is not None:
        scores = jnp.where(same, scores, -1e30)
    probs = softmax_rows(scores)
    probs_b = probs.astype(BF)
    mixed = pick_heads(masks, nn(probs_b, v)).astype(BF)
    return q_stack, probs, probs_b, mixed


def attend_back(masks, q_stack, k, v, probs, probs_b, d_mixed):
    d_stack = stack_heads(masks, d_mixed)
    d_probs = nt(d_stack, v).astype(BF).astype(F32)
    d_v = tn(probs_b, d_stack)
    d_scores = probs * (d_probs - jnp.sum(d_probs * probs, -1, keepdims=True)) * SCALE
    d_scores = d_scores.astype(BF)
    d_q = pick_heads(masks, nn(d_scores, k))
    d_k = tn(d_scores, q_stack)
    return d_q.astype(BF), d_k.astype(BF), d_v.astype(BF)


def spatial_forward_kernel(qkv, mixed):
    q, k, v = qkv[:, :ATT], qkv[:, ATT : 2 * ATT], qkv[:, 2 * ATT :]
    mixed[...] = attend(head_masks(), q, k, v, None)[3]


def spatial_backward_kernel(qkv, hidden_grad, factors, w_so, out):
    q, k, v = qkv[:, :ATT], qkv[:, ATT : 2 * ATT], qkv[:, 2 * ATT :]
    masks = head_masks()
    gated = (hidden_grad[...].astype(F32) * factors[0:1, :]).astype(BF)
    d_mixed = nt(gated, w_so[...]).astype(BF)
    q_stack, probs, probs_b, _ = attend(masks, q, k, v, None)
    d_q, d_k, d_v = attend_back(masks, q_stack, k, v, probs, probs_b, d_mixed)
    out[:, :ATT] = d_q
    out[:, ATT : 2 * ATT] = d_k
    out[:, 2 * ATT :] = d_v


def compact_kernel(place, mine, other, own_so, own_out, own_qkv, part, both, so, out, qkv):
    core = place[0]
    both[core] = mine[...]
    both[1 - core] = other[...]
    for i in range(16):
        shard = both[i % 2, 48 * (i // 2) : 48 * (i // 2) + 48, :].astype(F32)
        so[9 * i : 9 * i + 9, :] = shard[:9]
        out[9 * i : 9 * i + 9, :] = shard[9:18]
        qkv[27 * i : 27 * i + 27, :] = shard[18:45]
    own_so[...] = so[...].astype(BF)
    own_out[...] = out[...].astype(BF)
    own_qkv[...] = qkv[...].astype(BF)
    at_qkv = pl.multiple_of(core * 208, 16)
    at = pl.multiple_of(core * 64, 16)
    part[0:224, :] = own_qkv[pl.ds(at_qkv, 224), :]
    part[224:304, :] = own_so[pl.ds(at, 80), :]
    part[304:384, :] = own_out[pl.ds(at, 80), :]


SECTIONS = ((0, 0, 224), (1, 224, 304), (2, 304, 384))
BLOCK = (432, 144, 144)
STEP = (208, 64, 64)


def assemble(place, own, near, swapped, targets):
    for me in range(2):

        @pl.when(place[0] == me)
        def _():
            cls = place[1]
            for section, ref in enumerate(own):
                to = pl.multiple_of(cls * BLOCK[section], 16)
                targets[section][pl.ds(to, BLOCK[section]), :] = ref[...]
            for flip, ref, other in zip((2, 1, 3), near, swapped):
                for half in range(2):
                    source = ref if half == me else other
                    for section, first, last in SECTIONS:
                        skip = 16 * half
                        row = skip + STEP[section] * half
                        to = pl.multiple_of((cls ^ flip) * BLOCK[section] + row, 16)
                        rows = last - first - skip
                        targets[section][pl.ds(to, rows), :] = source[first + skip : last, :]


def temporal_forward_kernel(
    place, sent, factors, own_qkv, own_so, own_out, b, c, d, other_b, other_c, other_d,
    out_keep, out_send, w_so, w_out, w_qkv, q_out, k_out, v_out, probs_out, mixed_out,
    unit_out, inverse_out, project_out,
):
    assemble(
        place, (own_qkv, own_so, own_out), (b, c, d), (other_b, other_c, other_d),
        (w_qkv, w_so, w_out),
    )
    tokens, cotangent, mixed_s = sent[:, :D], sent[:, D : 2 * D], sent[:, 2 * D :]
    gate_s, shift, scale, gate_t = (factors[i : i + 1, :] for i in range(4))
    project = nn(mixed_s, w_so[...])
    project_out[...] = project
    hidden = (tokens.astype(F32) + gate_s * project).astype(BF).astype(F32)
    centered = hidden - jnp.mean(hidden, -1, keepdims=True)
    inverse = lax.rsqrt(jnp.mean(centered * centered, -1, keepdims=True) + 1e-06)
    inverse_out[...] = jnp.broadcast_to(inverse, (ROWS, 128))
    unit = centered * inverse
    unit_out[...] = unit
    normed = (unit * (1.0 + scale) + shift).astype(BF)
    q, k, v = (nt(normed, w_qkv[i * ATT : (i + 1) * ATT, :]).astype(BF) for i in range(3))
    q_out[...], k_out[...], v_out[...] = q, k, v

    row = lax.broadcasted_iota(jnp.int32, (HEADS * ROWS, ROWS), 0)
    col = lax.broadcasted_iota(jnp.int32, (HEADS * ROWS, ROWS), 1)
    same = ((row ^ col) & 1) == 0
    _, probs, _, mixed = attend(head_masks(), q, k, v, same)
    probs_out[...] = probs
    mixed_out[...] = mixed

    scaled = (cotangent.astype(F32) * gate_t).astype(BF)
    left, right = scaled[:, :ATT], scaled[:, ATT:]
    first = place[0] == 0
    out_keep[...] = tn(mixed, jnp.where(first, left, right))
    out_send[...] = tn(mixed, jnp.where(first, right, left)).astype(BF)


def temporal_backward_kernel(
    sent, factors, w_so, w_out, w_qkv, q, k, v, probs, mixed, unit, inverse, project, packed
):
    scale, gate_t = factors[2:3, :], factors[3:4, :]
    cot = sent[:, D : 2 * D].astype(F32)
    scaled = (cot * gate_t).astype(BF)
    masks = head_masks()
    q, k, v, probs = q[...], k[...], v[...], probs[...]
    d_mixed = nt(scaled, w_out[...]).astype(BF)
    q_stack = stack_heads(masks, q)
    d_q, d_k, d_v = attend_back(masks, q_stack, k, v, probs, probs.astype(BF), d_mixed)
    wq, wk, wv = (w_qkv[i * ATT : (i + 1) * ATT, :] for i in range(3))
    d_normed = (nn(d_q, wq) + nn(d_k, wk) + nn(d_v, wv)).astype(BF).astype(F32)
    unit = unit[...]
    d_unit = d_normed * (1.0 + scale)
    d_hidden = inverse[:, 0:1] * (
        d_unit
        - jnp.mean(d_unit, -1, keepdims=True)
        - unit * jnp.mean(d_unit * unit, -1, keepdims=True)
    )
    grad = (cot + d_hidden).astype(BF)
    packed[:, :D] = grad
    project_t = nn(mixed[...], w_out[...])
    factor_grads = (
        jnp.sum(grad.astype(F32) * project[...], 0, keepdims=True),
        jnp.sum(d_normed, 0, keepdims=True),
        jnp.sum(d_normed * unit, 0, keepdims=True),
        jnp.sum(cot * project_t, 0, keepdims=True),
    )
    tile = jnp.concatenate(factor_grads * 4, 0).astype(BF)
    for i in range(8):
        packed[16 * i : 16 * i + 16, D:] = tile


def call(kernel, outs, *args, scalars=0, scratch=(), flops=10**9):
    vmem = pl.BlockSpec(memory_space=pltpu.VMEM)
    return pl.pallas_call(
        kernel,
        out_shape=[jax.ShapeDtypeStruct(s, d) for s, d in outs],
        in_specs=[pl.BlockSpec(memory_space=pltpu.SMEM)] * scalars + [vmem] * (len(args) - scalars),
        out_specs=[vmem] * len(outs),
        scratch_shapes=list(scratch),
        compiler_params=pltpu.CompilerParams(vmem_limit_bytes=32 * 2**20),
        cost_estimate=pl.CostEstimate(flops=flops, bytes_accessed=10**7, transcendentals=10**5),
    )(*args)


def exchange(a):
    return lax.all_to_all(a, SEQ, 0, 0, tiled=True)


AXES = DP + SEQ


def device(x, y, z, core):
    ylo, yhi = y % 2, (y % 8) // 2
    return ((((x % 4) * 2 + ylo) * 4 + yhi) * 8 + z % 8) * 2 + core


def receive(a, source):
    pairs = []
    for x in range(4):
        for y in range(8):
            for z in range(8):
                for core in range(2):
                    pairs.append((device(*source(x, y, z, core), core), device(x, y, z, core)))
    return lax.ppermute(a, AXES, pairs)


def swap_cores(a):
    return lax.ppermute(a, "core", [(0, 1), (1, 0)])


def class_source(x, y, z, core):
    ylo, yhi = y % 2, y // 2
    cls = (x % 2) * 2 + ylo
    return (x // 2) * 2 + yhi // 2, cls * 2 + yhi % 2, z


def near_source(dx, dy):
    def source(x, y, z, core):
        sign = 1 - 2 * core
        return x + sign * dx, y + sign * dy, z

    return source


def gather_weights(w_so, w_qkv, w_out, place, sent):
    shard = jnp.concatenate([w_so, w_out, w_qkv.T, jnp.zeros((3, D), BF)], 0)
    shard, sent = lax.optimization_barrier((receive(shard, class_source), sent))
    mine = lax.all_gather(shard, "z", axis=0, tiled=True)
    other = swap_cores(mine)
    rows = lambda n: ((n, D), BF)
    own_so, own_out, own_qkv, part = call(
        compact_kernel, [rows(144), rows(144), rows(432), rows(384)], place, mine, other, scalars=1,
        scratch=[
            pltpu.VMEM((2, 384, D), BF),
            pltpu.VMEM((144, D), F32),
            pltpu.VMEM((144, D), F32),
            pltpu.VMEM((432, D), F32),
        ],
    )
    part, sent = lax.optimization_barrier((part, sent))
    near = [receive(part, near_source(dx, dy)) for dx, dy in ((1, 0), (0, 1), (1, 1))]
    sent = exchange(sent).reshape(ROWS, 2 * D + ATT)
    return [own_qkv, own_so, own_out] + near + [swap_cores(a) for a in near], sent


def body(tokens, qkv, w_so, w_qkv, w_out, factors, cotangent):
    tokens, qkv, cotangent, factors = tokens[0, 0], qkv[0, 0], cotangent[0, 0], factors[0]
    core = lax.axis_index("core")
    cls = (lax.axis_index("x") % 2) * 2 + lax.axis_index("ylo")
    place = jnp.stack([core, cls]).astype(jnp.int32)

    (mixed_s,) = call(spatial_forward_kernel, [((ROWS, ATT), BF)], qkv)
    sent = jnp.concatenate([tokens, cotangent, mixed_s], 1).reshape(64, 2, 2 * D + ATT)
    weights, sent = gather_weights(w_so, w_qkv, w_out, place, sent)

    rows = lambda n, kind=BF: ((ROWS, n), kind)
    out_keep, out_send, *saved = call(
        temporal_forward_kernel,
        [
            ((ATT, ATT), F32), ((ATT, ATT), BF), ((ATT, D), BF), ((ATT, D), BF), ((3 * ATT, D), BF),
            rows(ATT), rows(ATT), rows(ATT), ((HEADS * ROWS, ROWS), F32), rows(ATT),
            rows(D, F32), rows(128, F32), rows(D, F32),
        ],
        place, sent, factors, *weights,
        scalars=1, flops=4 * 10**9,
    )
    w_so = saved[0]
    out_other = swap_cores(out_send)
    (packed,) = call(temporal_backward_kernel, [rows(2 * D)], sent, factors, *saved, flops=4 * 10**9)

    half = 9 * ATT // 2
    out_part = (out_keep + out_other.astype(F32)).astype(BF).reshape(64, 2, half)
    back = exchange(jnp.concatenate([packed.reshape(64, 2, 2 * D), out_part], 2))

    out_part = back[:, :, 2 * D :].astype(F32).reshape(32, 2, 2, half)
    out_part = jnp.sum(out_part, 0).astype(BF).reshape(1, 2, 9 * ATT)
    out_part = jnp.broadcast_to(out_part, (8, 2, 9 * ATT))
    out_part = jnp.sum(lax.all_to_all(out_part, DP, 0, 0, tiled=True).astype(F32), 0)
    out_grad = out_part.reshape(2, 9, ATT).transpose(1, 0, 2).reshape(9, D)

    token_grad = back[:, :, :D].reshape(ROWS, D)
    (qkv_grad,) = call(
        spatial_backward_kernel, [((ROWS, 3 * ATT), BF)], qkv, token_grad, factors, w_so
    )
    mine = jnp.sum(back[:, :, D : 2 * D].astype(F32), 0)
    other = swap_cores(mine)
    factor_grad = jnp.where(core == 0, jnp.concatenate([mine, other]), jnp.concatenate([other, mine]))
    return token_grad[None, None], qkv_grad[None, None], factor_grad[None], out_grad


def solution(mesh):
    fine = Mesh(mesh.devices.reshape(4, 2, 4, 8, 2), DP + SEQ)
    frames = P(DP, SEQ, None, None)
    return jax.shard_map(
        body,
        mesh=fine,
        in_specs=(
            frames,
            frames,
            P(SEQ, None),
            P(None, SEQ),
            P(SEQ, None),
            P(DP, None, None),
            frames,
        ),
        out_specs=(frames, frames, P(DP, None, None), P(SEQ, None)),
        check_vma=False,
    )
```

```python
import math

import jax
import jax.numpy as jnp
from jax import lax
from jax.experimental import pallas as pl
from jax.experimental.pallas import tpu as pltpu
from jax.sharding import Mesh
from jax.sharding import PartitionSpec as P

D = 1152
HEADS = 8
HS = 72
ATT = 576
ROWS = 128
SCALE = 1.0 / math.sqrt(HS)
SEQ = ("yhi", "z", "core")
CHIPS = ("yhi", "z")
DP = ("x", "ylo")
BF = jnp.bfloat16
F32 = jnp.float32


def nn(a, b):
    return lax.dot_general(a, b, (((1,), (0,)), ((), ())), preferred_element_type=F32)


def nt(a, b):
    return lax.dot_general(a, b, (((1,), (1,)), ((), ())), preferred_element_type=F32)


def tn(a, b):
    return lax.dot_general(a, b, (((0,), (0,)), ((), ())), preferred_element_type=F32)


def head_masks():
    head = lax.broadcasted_iota(jnp.int32, (ROWS, ATT), 1) // HS
    return [head == h for h in range(HEADS)]


def stack_heads(masks, a):
    zero = jnp.zeros_like(a)
    return jnp.concatenate([jnp.where(m, a, zero) for m in masks], 0)


def pick_heads(masks, a):
    out = a[:ROWS]
    for h in range(1, HEADS):
        out = jnp.where(masks[h], a[h * ROWS : (h + 1) * ROWS], out)
    return out


def softmax_rows(scores):
    top = jnp.max(scores, -1, keepdims=True)
    weights = jnp.exp(scores - top)
    return weights / jnp.sum(weights, -1, keepdims=True)


def attend(masks, q, k, v, same):
    q_stack = stack_heads(masks, q)
    scores = nt(q_stack, k) * SCALE
    if same is not None:
        scores = jnp.where(same, scores, -1e30)
    probs = softmax_rows(scores)
    probs_b = probs.astype(BF)
    mixed = pick_heads(masks, nn(probs_b, v)).astype(BF)
    return q_stack, probs, probs_b, mixed


def attend_back(masks, q_stack, k, v, probs, probs_b, d_mixed):
    d_stack = stack_heads(masks, d_mixed)
    d_probs = nt(d_stack, v).astype(BF).astype(F32)
    d_v = tn(probs_b, d_stack)
    d_scores = probs * (d_probs - jnp.sum(d_probs * probs, -1, keepdims=True)) * SCALE
    d_scores = d_scores.astype(BF)
    d_q = pick_heads(masks, nn(d_scores, k))
    d_k = tn(d_scores, q_stack)
    return d_q.astype(BF), d_k.astype(BF), d_v.astype(BF)


def spatial_forward_kernel(qkv, mixed):
    q, k, v = qkv[:, :ATT], qkv[:, ATT : 2 * ATT], qkv[:, 2 * ATT :]
    mixed[...] = attend(head_masks(), q, k, v, None)[3]


def spatial_backward_kernel(qkv, hidden_grad, factors, w_so, out):
    q, k, v = qkv[:, :ATT], qkv[:, ATT : 2 * ATT], qkv[:, 2 * ATT :]
    masks = head_masks()
    gated = (hidden_grad[...].astype(F32) * factors[0:1, :]).astype(BF)
    d_mixed = nt(gated, w_so[...]).astype(BF)
    q_stack, probs, probs_b, _ = attend(masks, q, k, v, None)
    d_q, d_k, d_v = attend_back(masks, q_stack, k, v, probs, probs_b, d_mixed)
    out[:, :ATT] = d_q
    out[:, ATT : 2 * ATT] = d_k
    out[:, 2 * ATT :] = d_v


def compact_kernel(place, mine, other, own_so, own_out, own_qkv, part, both, so, out, qkv):
    core = place[0]
    both[core] = mine[...]
    both[1 - core] = other[...]
    for i in range(16):
        shard = both[i % 2, 48 * (i // 2) : 48 * (i // 2) + 48, :].astype(F32)
        so[9 * i : 9 * i + 9, :] = shard[:9]
        out[9 * i : 9 * i + 9, :] = shard[9:18]
        qkv[27 * i : 27 * i + 27, :] = shard[18:45]
    own_so[...] = so[...].astype(BF)
    own_out[...] = out[...].astype(BF)
    own_qkv[...] = qkv[...].astype(BF)
    at_qkv = pl.multiple_of(core * 208, 16)
    at = pl.multiple_of(core * 64, 16)
    part[0:224, :] = own_qkv[pl.ds(at_qkv, 224), :]
    part[224:304, :] = own_so[pl.ds(at, 80), :]
    part[304:384, :] = own_out[pl.ds(at, 80), :]


SECTIONS = ((0, 0, 224), (1, 224, 304), (2, 304, 384))
BLOCK = (432, 144, 144)
STEP = (208, 64, 64)


COPIES = 6


def start_copies(place, near, swapped, targets, sems):
    for me in range(2):

        @pl.when(place[0] == me)
        def _():
            for section, first, last in (SECTIONS[1], SECTIONS[0], SECTIONS[2]):
                for i, (flip, ref, other) in enumerate(zip((2, 1, 3), near, swapped)):
                    for half in range(2):
                        source = ref if half == me else other
                        skip = 16 * half
                        row = skip + STEP[section] * half
                        to = pl.multiple_of((place[1] ^ flip) * BLOCK[section] + row, 16)
                        rows = last - first - skip
                        pltpu.make_async_copy(
                            source.at[pl.ds(first + skip, rows)],
                            targets[section].at[pl.ds(to, rows)],
                            sems.at[section * COPIES + 2 * i + half],
                        ).start()


def wait_copies(section, near, targets, sems):
    first, last = SECTIONS[section][1:]
    for i in range(3):
        for half in range(2):
            rows = pl.ds(0, last - first - 16 * half)
            sem = sems.at[section * COPIES + 2 * i + half]
            pltpu.make_async_copy(near[i].at[rows], targets[section].at[rows], sem).wait()


def temporal_forward_kernel(
    place, sent, factors, own_qkv, own_so, own_out, b, c, d, other_b, other_c, other_d,
    out_keep, out_send, w_so, w_out, w_qkv, q_out, k_out, v_out, probs_out, mixed_out,
    unit_out, inverse_out, project_out, cot_out, sems,
):
    near, targets = (b, c, d), (w_qkv, w_so, w_out)
    start_copies(place, near, (other_b, other_c, other_d), targets, sems)
    for section, ref in enumerate((own_qkv, own_so, own_out)):
        to = pl.multiple_of(place[1] * BLOCK[section], 16)
        targets[section][pl.ds(to, BLOCK[section]), :] = ref[...]
    received = sent[...].reshape(ROWS, 2 * D + ATT)
    tokens, cotangent, mixed_s = received[:, :D], received[:, D : 2 * D], received[:, 2 * D :]
    cot_out[...] = cotangent
    wait_copies(1, near, targets, sems)
    gate_s, shift, scale, gate_t = (factors[i : i + 1, :] for i in range(4))
    project = nn(mixed_s, w_so[...])
    project_out[...] = project
    hidden = (tokens.astype(F32) + gate_s * project).astype(BF).astype(F32)
    centered = hidden - jnp.mean(hidden, -1, keepdims=True)
    inverse = lax.rsqrt(jnp.mean(centered * centered, -1, keepdims=True) + 1e-06)
    inverse_out[...] = jnp.broadcast_to(inverse, (ROWS, 128))
    unit = centered * inverse
    unit_out[...] = unit
    normed = (unit * (1.0 + scale) + shift).astype(BF)
    wait_copies(0, near, targets, sems)
    q, k, v = (nt(normed, w_qkv[i * ATT : (i + 1) * ATT, :]).astype(BF) for i in range(3))
    q_out[...], k_out[...], v_out[...] = q, k, v

    row = lax.broadcasted_iota(jnp.int32, (HEADS * ROWS, ROWS), 0)
    col = lax.broadcasted_iota(jnp.int32, (HEADS * ROWS, ROWS), 1)
    same = ((row ^ col) & 1) == 0
    _, probs, _, mixed = attend(head_masks(), q, k, v, same)
    probs_out[...] = probs
    mixed_out[...] = mixed

    scaled = (cotangent.astype(F32) * gate_t).astype(BF)
    source = lax.broadcasted_iota(jnp.int32, (ATT, ATT), 0)
    target = lax.broadcasted_iota(jnp.int32, (ATT, ATT), 1)
    order = jnp.where(source == (target & 63) * 9 + (target >> 6), 1.0, 0.0).astype(BF)
    ordered = nn(mixed, order).astype(BF)
    left, right = scaled[:, :ATT], scaled[:, ATT:]
    first = place[0] == 0
    keep = tn(ordered, jnp.where(first, left, right))
    send = tn(ordered, jnp.where(first, right, left)).astype(BF)
    for j in range(9):
        out_keep[:, ATT * j : ATT * j + ATT] = keep[64 * j : 64 * j + 64]
        out_send[:, ATT * j : ATT * j + ATT] = send[64 * j : 64 * j + 64]
    wait_copies(2, near, targets, sems)


def temporal_backward_kernel(
    factors, w_so, w_out, w_qkv, q, k, v, probs, mixed, unit, inverse, project, cotangent, packed
):
    scale, gate_t = factors[2:3, :], factors[3:4, :]
    cot = cotangent[...].astype(F32)
    scaled = (cot * gate_t).astype(BF)
    masks = head_masks()
    q, k, v, probs = q[...], k[...], v[...], probs[...]
    d_mixed = nt(scaled, w_out[...]).astype(BF)
    q_stack = stack_heads(masks, q)
    d_q, d_k, d_v = attend_back(masks, q_stack, k, v, probs, probs.astype(BF), d_mixed)
    wq, wk, wv = (w_qkv[i * ATT : (i + 1) * ATT, :] for i in range(3))
    d_normed = (nn(d_q, wq) + nn(d_k, wk) + nn(d_v, wv)).astype(BF).astype(F32)
    unit = unit[...]
    d_unit = d_normed * (1.0 + scale)
    d_hidden = inverse[:, 0:1] * (
        d_unit
        - jnp.mean(d_unit, -1, keepdims=True)
        - unit * jnp.mean(d_unit * unit, -1, keepdims=True)
    )
    grad = (cot + d_hidden).astype(BF)
    packed[:, :D] = grad
    project_t = nn(mixed[...], w_out[...])
    factor_grads = (
        jnp.sum(grad.astype(F32) * project[...], 0, keepdims=True),
        jnp.sum(d_normed, 0, keepdims=True),
        jnp.sum(d_normed * unit, 0, keepdims=True),
        jnp.sum(cot * project_t, 0, keepdims=True),
    )
    tile = jnp.concatenate(factor_grads * 4, 0).astype(BF)
    for i in range(8):
        packed[16 * i : 16 * i + 16, D:] = tile


HALF = 9 * ATT // 2


def pack_kernel(packed, out_keep, out_other, out):
    out[:, :, : 2 * D] = packed[...].reshape(64, 2, 2 * D)
    pair = (out_keep[...] + out_other[...].astype(F32)).astype(BF)
    out[:, 0, 2 * D :] = pair[:, :HALF]
    out[:, 1, 2 * D :] = pair[:, HALF:]


def unpack_kernel(back, token_grad, out_part, factor_part):
    token_grad[...] = back[:, :, :D].reshape(ROWS, D)
    first = lax.broadcasted_iota(jnp.int32, (64, HALF), 0) & 1 == 0
    for r in range(2):
        factor_part[r : r + 1, :] = jnp.sum(back[:, r, D : 2 * D].astype(F32), 0, keepdims=True)
        rows = back[:, r, 2 * D :].astype(F32)
        for core in range(2):
            total = jnp.sum(jnp.where(first == (core == 0), rows, 0.0), 0, keepdims=True)
            for copy in range(8):
                out_part[copy, core : core + 1, HALF * r : HALF * r + HALF] = total


def call(kernel, outs, *args, scalars=0, hbm=0, scratch=(), flops=10**9):
    vmem = pl.BlockSpec(memory_space=pltpu.VMEM)
    specs = [pl.BlockSpec(memory_space=pltpu.SMEM)] * scalars
    specs += [vmem] * (len(args) - scalars - hbm) + [pl.BlockSpec(memory_space=pltpu.HBM)] * hbm
    return pl.pallas_call(
        kernel,
        out_shape=[jax.ShapeDtypeStruct(s, d) for s, d in outs],
        in_specs=specs,
        out_specs=[vmem] * len(outs),
        scratch_shapes=list(scratch),
        compiler_params=pltpu.CompilerParams(vmem_limit_bytes=32 * 2**20),
        cost_estimate=pl.CostEstimate(flops=flops, bytes_accessed=10**7, transcendentals=10**5),
    )(*args)


def exchange(a):
    return lax.all_to_all(a, SEQ, 0, 0, tiled=True)


AXES = DP + SEQ


def device(x, y, z, core):
    ylo, yhi = y % 2, (y % 8) // 2
    return ((((x % 4) * 2 + ylo) * 4 + yhi) * 8 + z % 8) * 2 + core


def receive(a, source):
    pairs = []
    for x in range(4):
        for y in range(8):
            for z in range(8):
                for core in range(2):
                    pairs.append((device(*source(x, y, z, core), core), device(x, y, z, core)))
    return lax.ppermute(a, AXES, pairs)


def swap_cores(a):
    return lax.ppermute(a, "core", [(0, 1), (1, 0)])


def class_source(x, y, z, core):
    ylo, yhi = y % 2, y // 2
    cls = (x % 2) * 2 + ylo
    return (x // 2) * 2 + yhi // 2, cls * 2 + yhi % 2, z


def near_source(dx, dy):
    def source(x, y, z, core):
        sign = 1 - 2 * core
        return x + sign * dx, y + sign * dy, z

    return source


def gather_weights(w_so, w_qkv, w_out, place, sent):
    shard = jnp.concatenate([w_so, w_out, w_qkv.T, jnp.zeros((3, D), BF)], 0)
    shard, sent = lax.optimization_barrier((receive(shard, class_source), sent))
    mine = lax.all_gather(shard, "z", axis=0, tiled=True)
    other = swap_cores(mine)
    rows = lambda n: ((n, D), BF)
    own_so, own_out, own_qkv, part = call(
        compact_kernel, [rows(144), rows(144), rows(432), rows(384)], place, mine, other, scalars=1,
        scratch=[
            pltpu.VMEM((2, 384, D), BF),
            pltpu.VMEM((144, D), F32),
            pltpu.VMEM((144, D), F32),
            pltpu.VMEM((432, D), F32),
        ],
    )
    part, sent = lax.optimization_barrier((part, sent))
    near = [receive(part, near_source(dx, dy)) for dx, dy in ((1, 0), (0, 1), (1, 1))]
    sent = exchange(sent)
    return [own_qkv, own_so, own_out] + near + [swap_cores(a) for a in near], sent


def body(tokens, qkv, w_so, w_qkv, w_out, factors, cotangent):
    tokens, qkv, cotangent, factors = tokens[0, 0], qkv[0, 0], cotangent[0, 0], factors[0]
    core = lax.axis_index("core")
    cls = (lax.axis_index("x") % 2) * 2 + lax.axis_index("ylo")
    place = jnp.stack([core, cls]).astype(jnp.int32)

    (mixed_s,) = call(spatial_forward_kernel, [((ROWS, ATT), BF)], qkv)
    sent = jnp.concatenate([tokens, cotangent, mixed_s], 1).reshape(64, 2, 2 * D + ATT)
    weights, sent = gather_weights(w_so, w_qkv, w_out, place, sent)

    rows = lambda n, kind=BF: ((ROWS, n), kind)
    out_keep, out_send, *saved = call(
        temporal_forward_kernel,
        [
            ((64, 2 * HALF), F32), ((64, 2 * HALF), BF),
            ((ATT, D), BF), ((ATT, D), BF), ((3 * ATT, D), BF),
            rows(ATT), rows(ATT), rows(ATT), ((HEADS * ROWS, ROWS), F32), rows(ATT),
            rows(D, F32), rows(128, F32), rows(D, F32), rows(D),
        ],
        place, sent, factors, *weights,
        scalars=1, hbm=6, flops=4 * 10**9,
        scratch=[pltpu.SemaphoreType.DMA((3 * COPIES,))],
    )
    w_so = saved[0]
    out_other = swap_cores(out_send)
    (packed,) = call(temporal_backward_kernel, [rows(2 * D)], factors, *saved, flops=4 * 10**9)

    (packed,) = call(
        pack_kernel, [((64, 2, 2 * D + HALF), BF)], packed, out_keep, out_other, flops=10**8
    )
    token_grad, out_part, mine = call(
        unpack_kernel,
        [rows(D), ((8, 2, 2 * HALF), F32), ((2, D), F32)],
        exchange(packed), flops=10**8,
    )
    out_part = jnp.sum(lax.all_to_all(out_part, DP, 0, 0, tiled=True), 0)
    out_grad = out_part.reshape(2, 9, ATT).transpose(1, 0, 2).reshape(9, D)

    (qkv_grad,) = call(
        spatial_backward_kernel, [((ROWS, 3 * ATT), BF)], qkv, token_grad, factors, w_so
    )
    other = swap_cores(mine)
    factor_grad = jnp.where(core == 0, jnp.concatenate([mine, other]), jnp.concatenate([other, mine]))
    return token_grad[None, None], qkv_grad[None, None], factor_grad[None], out_grad


def solution(mesh):
    fine = Mesh(mesh.devices.reshape(4, 2, 4, 8, 2), DP + SEQ)
    frames = P(DP, SEQ, None, None)
    return jax.shard_map(
        body,
        mesh=fine,
        in_specs=(
            frames,
            frames,
            P(SEQ, None),
            P(None, SEQ),
            P(SEQ, None),
            P(DP, None, None),
            frames,
        ),
        out_specs=(frames, frames, P(DP, None, None), P(SEQ, None)),
        check_vma=False,
    )
```

```python
import math

import jax
import jax.numpy as jnp
from jax import lax
from jax.experimental import pallas as pl
from jax.experimental.pallas import tpu as pltpu
from jax.sharding import Mesh
from jax.sharding import PartitionSpec as P

D = 1152
HEADS = 8
HS = 72
ATT = 576
ROWS = 128
SCALE = 1.0 / math.sqrt(HS)
SEQ = ("yhi", "z", "core")
CHIPS = ("yhi", "z")
DP = ("x", "ylo")
BF = jnp.bfloat16
F32 = jnp.float32


def nn(a, b):
    return lax.dot_general(a, b, (((1,), (0,)), ((), ())), preferred_element_type=F32)


def nt(a, b):
    return lax.dot_general(a, b, (((1,), (1,)), ((), ())), preferred_element_type=F32)


def tn(a, b):
    return lax.dot_general(a, b, (((0,), (0,)), ((), ())), preferred_element_type=F32)


def head_masks():
    head = lax.broadcasted_iota(jnp.int32, (ROWS, ATT), 1) // HS
    return [head == h for h in range(HEADS)]


def stack_heads(masks, a):
    zero = jnp.zeros_like(a)
    return jnp.concatenate([jnp.where(m, a, zero) for m in masks], 0)


def pick_heads(masks, a):
    out = a[:ROWS]
    for h in range(1, HEADS):
        out = jnp.where(masks[h], a[h * ROWS : (h + 1) * ROWS], out)
    return out


def softmax_rows(scores):
    top = jnp.max(scores, -1, keepdims=True)
    weights = jnp.exp(scores - top)
    return weights / jnp.sum(weights, -1, keepdims=True)


def attend(masks, q, k, v, same):
    q_stack = stack_heads(masks, q)
    scores = nt(q_stack, k) * SCALE
    if same is not None:
        scores = jnp.where(same, scores, -1e30)
    probs = softmax_rows(scores)
    probs_b = probs.astype(BF)
    mixed = pick_heads(masks, nn(probs_b, v)).astype(BF)
    return q_stack, probs, probs_b, mixed


def attend_back(masks, q_stack, k, v, probs, probs_b, d_mixed):
    d_stack = stack_heads(masks, d_mixed)
    d_probs = nt(d_stack, v).astype(BF).astype(F32)
    d_v = tn(probs_b, d_stack)
    d_scores = probs * (d_probs - jnp.sum(d_probs * probs, -1, keepdims=True)) * SCALE
    d_scores = d_scores.astype(BF)
    d_q = pick_heads(masks, nn(d_scores, k))
    d_k = tn(d_scores, q_stack)
    return d_q.astype(BF), d_k.astype(BF), d_v.astype(BF)


def spatial_forward_kernel(qkv, mixed):
    q, k, v = qkv[:, :ATT], qkv[:, ATT : 2 * ATT], qkv[:, 2 * ATT :]
    mixed[...] = attend(head_masks(), q, k, v, None)[3]


def spatial_backward_kernel(qkv, hidden_grad, factors, w_so, out):
    q, k, v = qkv[:, :ATT], qkv[:, ATT : 2 * ATT], qkv[:, 2 * ATT :]
    masks = head_masks()
    gated = (hidden_grad[...].astype(F32) * factors[0:1, :]).astype(BF)
    d_mixed = nt(gated, w_so[...]).astype(BF)
    q_stack, probs, probs_b, _ = attend(masks, q, k, v, None)
    d_q, d_k, d_v = attend_back(masks, q_stack, k, v, probs, probs_b, d_mixed)
    out[:, :ATT] = d_q
    out[:, ATT : 2 * ATT] = d_k
    out[:, 2 * ATT :] = d_v


def compact_kernel(place, mine, other, own_so, own_out, own_qkv, part, both, so, out, qkv):
    core = place[0]
    both[core] = mine[...]
    both[1 - core] = other[...]
    for i in range(16):
        shard = both[i % 2, 48 * (i // 2) : 48 * (i // 2) + 48, :].astype(F32)
        so[9 * i : 9 * i + 9, :] = shard[:9]
        out[9 * i : 9 * i + 9, :] = shard[9:18]
        qkv[27 * i : 27 * i + 27, :] = shard[18:45]
    own_so[...] = so[...].astype(BF)
    own_out[...] = out[...].astype(BF)
    own_qkv[...] = qkv[...].astype(BF)
    at_qkv = pl.multiple_of(core * 208, 16)
    at = pl.multiple_of(core * 64, 16)
    part[0:224, :] = own_qkv[pl.ds(at_qkv, 224), :]
    part[224:304, :] = own_so[pl.ds(at, 80), :]
    part[304:384, :] = own_out[pl.ds(at, 80), :]


SECTIONS = ((0, 0, 224), (1, 224, 304), (2, 304, 384))
BLOCK = (432, 144, 144)
STEP = (208, 64, 64)


COPIES = 7


def start_copies(place, own, near, swapped, targets, sems):
    for section in (1, 0, 2):
        to = pl.multiple_of(place[1] * BLOCK[section], 16)
        pltpu.make_async_copy(
            own[section],
            targets[section].at[pl.ds(to, BLOCK[section])],
            sems.at[section * COPIES + 6],
        ).start()
    for me in range(2):

        @pl.when(place[0] == me)
        def _():
            for section, first, last in (SECTIONS[1], SECTIONS[0], SECTIONS[2]):
                for i, (flip, ref, other) in enumerate(zip((2, 1, 3), near, swapped)):
                    for half in range(2):
                        source = ref if half == me else other
                        skip = 16 * half
                        row = skip + STEP[section] * half
                        to = pl.multiple_of((place[1] ^ flip) * BLOCK[section] + row, 16)
                        rows = last - first - skip
                        pltpu.make_async_copy(
                            source.at[pl.ds(first + skip, rows)],
                            targets[section].at[pl.ds(to, rows)],
                            sems.at[section * COPIES + 2 * i + half],
                        ).start()


def wait_copies(section, own, near, targets, sems):
    first, last = SECTIONS[section][1:]
    for i in range(3):
        for half in range(2):
            rows = pl.ds(0, last - first - 16 * half)
            sem = sems.at[section * COPIES + 2 * i + half]
            pltpu.make_async_copy(near[i].at[rows], targets[section].at[rows], sem).wait()
    rows, sem = pl.ds(0, BLOCK[section]), sems.at[section * COPIES + 6]
    pltpu.make_async_copy(own[section], targets[section].at[rows], sem).wait()


def temporal_forward_kernel(
    place, sent, factors, own_qkv, own_so, own_out, b, c, d, other_b, other_c, other_d,
    out_keep, out_send, w_so, w_out, w_qkv, q_out, k_out, v_out, probs_out, mixed_out,
    unit_out, inverse_out, project_out, cot_out, sems,
):
    own, near, targets = (own_qkv, own_so, own_out), (b, c, d), (w_qkv, w_so, w_out)
    start_copies(place, own, near, (other_b, other_c, other_d), targets, sems)
    received = sent[...].reshape(ROWS, 2 * D + ATT)
    tokens, cotangent, mixed_s = received[:, :D], received[:, D : 2 * D], received[:, 2 * D :]
    cot_out[...] = cotangent
    wait_copies(1, own, near, targets, sems)
    gate_s, shift, scale, gate_t = (factors[i : i + 1, :] for i in range(4))
    project = nn(mixed_s, w_so[...])
    project_out[...] = project
    hidden = (tokens.astype(F32) + gate_s * project).astype(BF).astype(F32)
    centered = hidden - jnp.mean(hidden, -1, keepdims=True)
    inverse = lax.rsqrt(jnp.mean(centered * centered, -1, keepdims=True) + 1e-06)
    inverse_out[...] = jnp.broadcast_to(inverse, (ROWS, 128))
    unit = centered * inverse
    unit_out[...] = unit
    normed = (unit * (1.0 + scale) + shift).astype(BF)
    wait_copies(0, own, near, targets, sems)
    q, k, v = (nt(normed, w_qkv[i * ATT : (i + 1) * ATT, :]).astype(BF) for i in range(3))
    q_out[...], k_out[...], v_out[...] = q, k, v

    row = lax.broadcasted_iota(jnp.int32, (HEADS * ROWS, ROWS), 0)
    col = lax.broadcasted_iota(jnp.int32, (HEADS * ROWS, ROWS), 1)
    same = ((row ^ col) & 1) == 0
    _, probs, _, mixed = attend(head_masks(), q, k, v, same)
    probs_out[...] = probs
    mixed_out[...] = mixed

    scaled = (cotangent.astype(F32) * gate_t).astype(BF)
    source = lax.broadcasted_iota(jnp.int32, (ATT, ATT), 0)
    target = lax.broadcasted_iota(jnp.int32, (ATT, ATT), 1)
    order = jnp.where(source == (target & 63) * 9 + (target >> 6), 1.0, 0.0).astype(BF)
    ordered = nn(mixed, order).astype(BF)
    left, right = scaled[:, :ATT], scaled[:, ATT:]
    first = place[0] == 0
    keep = tn(ordered, jnp.where(first, left, right))
    send = tn(ordered, jnp.where(first, right, left)).astype(BF)
    for j in range(9):
        out_keep[:, ATT * j : ATT * j + ATT] = keep[64 * j : 64 * j + 64]
        out_send[:, ATT * j : ATT * j + ATT] = send[64 * j : 64 * j + 64]
    wait_copies(2, own, near, targets, sems)


def temporal_backward_kernel(
    factors, w_so, w_out, w_qkv, q, k, v, probs, mixed, unit, inverse, project, cotangent, packed
):
    scale, gate_t = factors[2:3, :], factors[3:4, :]
    cot = cotangent[...].astype(F32)
    scaled = (cot * gate_t).astype(BF)
    masks = head_masks()
    q, k, v, probs = q[...], k[...], v[...], probs[...]
    d_mixed = nt(scaled, w_out[...]).astype(BF)
    q_stack = stack_heads(masks, q)
    d_q, d_k, d_v = attend_back(masks, q_stack, k, v, probs, probs.astype(BF), d_mixed)
    wq, wk, wv = (w_qkv[i * ATT : (i + 1) * ATT, :] for i in range(3))
    d_normed = (nn(d_q, wq) + nn(d_k, wk) + nn(d_v, wv)).astype(BF).astype(F32)
    unit = unit[...]
    d_unit = d_normed * (1.0 + scale)
    d_hidden = inverse[:, 0:1] * (
        d_unit
        - jnp.mean(d_unit, -1, keepdims=True)
        - unit * jnp.mean(d_unit * unit, -1, keepdims=True)
    )
    grad = (cot + d_hidden).astype(BF)
    packed[:, :D] = grad
    project_t = nn(mixed[...], w_out[...])
    factor_grads = (
        jnp.sum(grad.astype(F32) * project[...], 0, keepdims=True),
        jnp.sum(d_normed, 0, keepdims=True),
        jnp.sum(d_normed * unit, 0, keepdims=True),
        jnp.sum(cot * project_t, 0, keepdims=True),
    )
    zeros = jnp.zeros((16, 64), BF)
    for parity in range(2):
        rows = [
            factor_grads[2 * parity + core][:, part * ATT : part * ATT + ATT]
            for core in range(2)
            for part in range(2)
        ]
        tile = jnp.concatenate([jnp.concatenate(rows * 4, 0).astype(BF), zeros], 1)
        for yhi in (parity, parity + 2):
            packed[32 * yhi : 32 * yhi + 16, D:] = tile
            packed[32 * yhi + 16 : 32 * yhi + 32, D:] = tile


HALF = 9 * ATT // 2
HEAD = D + 640


def pack_kernel(packed, out_keep, out_other, out):
    out[:, :, :HEAD] = packed[...].reshape(64, 2, HEAD)
    pair = (out_keep[...] + out_other[...].astype(F32)).astype(BF)
    out[:, 0, HEAD:] = pair[:, :HALF]
    out[:, 1, HEAD:] = pair[:, HALF:]


def unpack_kernel(back, token_grad, out_part, factor_part):
    token_grad[...] = back[:, :, :D].reshape(ROWS, D)
    first = lax.broadcasted_iota(jnp.int32, (64, HALF), 0) & 1 == 0
    for r in range(2):
        half_row = jnp.sum(back[:, r, D : D + ATT].astype(F32), 0, keepdims=True)
        factor_part[:, ATT * r : ATT * r + ATT] = half_row
        rows = back[:, r, HEAD:].astype(F32)
        for core in range(2):
            total = jnp.sum(jnp.where(first == (core == 0), rows, 0.0), 0, keepdims=True)
            for copy in range(8):
                out_part[copy, core : core + 1, HALF * r : HALF * r + HALF] = total


def call(kernel, outs, *args, scalars=0, hbm=0, scratch=(), flops=10**9):
    vmem = pl.BlockSpec(memory_space=pltpu.VMEM)
    specs = [pl.BlockSpec(memory_space=pltpu.SMEM)] * scalars
    specs += [vmem] * (len(args) - scalars - hbm) + [pl.BlockSpec(memory_space=pltpu.HBM)] * hbm
    return pl.pallas_call(
        kernel,
        out_shape=[jax.ShapeDtypeStruct(s, d) for s, d in outs],
        in_specs=specs,
        out_specs=[vmem] * len(outs),
        scratch_shapes=list(scratch),
        compiler_params=pltpu.CompilerParams(vmem_limit_bytes=32 * 2**20),
        cost_estimate=pl.CostEstimate(flops=flops, bytes_accessed=10**7, transcendentals=10**5),
    )(*args)


def exchange(a):
    return lax.all_to_all(a, SEQ, 0, 0, tiled=True)


AXES = DP + SEQ


def device(x, y, z, core):
    ylo, yhi = y % 2, (y % 8) // 2
    return ((((x % 4) * 2 + ylo) * 4 + yhi) * 8 + z % 8) * 2 + core


def receive(a, source):
    pairs = []
    for x in range(4):
        for y in range(8):
            for z in range(8):
                for core in range(2):
                    pairs.append((device(*source(x, y, z, core), core), device(x, y, z, core)))
    return lax.ppermute(a, AXES, pairs)


def swap_cores(a):
    return lax.ppermute(a, "core", [(0, 1), (1, 0)])


SENDERS = (
    ((0, 0), (1, 2), (0, 1), (3, 3), (1, 1), (0, 3), (3, 0), (0, 2)),
    ((0, 5), (1, 7), (0, 4), (1, 6), (1, 4), (2, 6), (1, 5), (2, 7)),
    ((1, 0), (2, 2), (3, 1), (1, 3), (2, 1), (2, 3), (2, 0), (3, 2)),
    ((3, 5), (0, 7), (2, 4), (0, 6), (3, 4), (3, 6), (2, 5), (3, 7)),
)


def class_source(x, y, z, core):
    return *SENDERS[x][y], z


def near_source(dx, dy):
    def source(x, y, z, core):
        sign = 1 - 2 * core
        return x + sign * dx, y + sign * dy, z

    return source


def gather_weights(w_so, w_qkv, w_out, place, sent):
    shard = jnp.concatenate([w_so, w_out, w_qkv.T, jnp.zeros((3, D), BF)], 0)
    shard, sent = lax.optimization_barrier((receive(shard, class_source), sent))
    mine = lax.all_gather(shard, "z", axis=0, tiled=True)
    other = swap_cores(mine)
    rows = lambda n: ((n, D), BF)
    own_so, own_out, own_qkv, part = call(
        compact_kernel, [rows(144), rows(144), rows(432), rows(384)], place, mine, other, scalars=1,
        scratch=[
            pltpu.VMEM((2, 384, D), BF),
            pltpu.VMEM((144, D), F32),
            pltpu.VMEM((144, D), F32),
            pltpu.VMEM((432, D), F32),
        ],
    )
    part, sent = lax.optimization_barrier((part, sent))
    near = [receive(part, near_source(dx, dy)) for dx, dy in ((1, 0), (0, 1), (1, 1))]
    sent = exchange(sent)
    return [own_qkv, own_so, own_out] + near + [swap_cores(a) for a in near], sent


def body(tokens, qkv, w_so, w_qkv, w_out, factors, cotangent):
    tokens, qkv, cotangent, factors = tokens[0, 0], qkv[0, 0], cotangent[0, 0], factors[0]
    core = lax.axis_index("core")
    cls = (lax.axis_index("x") % 2) * 2 + lax.axis_index("ylo")
    place = jnp.stack([core, cls]).astype(jnp.int32)

    (mixed_s,) = call(spatial_forward_kernel, [((ROWS, ATT), BF)], qkv)
    sent = jnp.concatenate([tokens, cotangent, mixed_s], 1).reshape(64, 2, 2 * D + ATT)
    weights, sent = gather_weights(w_so, w_qkv, w_out, place, sent)

    rows = lambda n, kind=BF: ((ROWS, n), kind)
    out_keep, out_send, *saved = call(
        temporal_forward_kernel,
        [
            ((64, 2 * HALF), F32), ((64, 2 * HALF), BF),
            ((ATT, D), BF), ((ATT, D), BF), ((3 * ATT, D), BF),
            rows(ATT), rows(ATT), rows(ATT), ((HEADS * ROWS, ROWS), F32), rows(ATT),
            rows(D, F32), rows(128, F32), rows(D, F32), rows(D),
        ],
        place, sent, factors, *weights,
        scalars=1, hbm=9, flops=4 * 10**9,
        scratch=[pltpu.SemaphoreType.DMA((3 * COPIES,))],
    )
    w_so = saved[0]
    out_other = swap_cores(out_send)
    (packed,) = call(temporal_backward_kernel, [rows(HEAD)], factors, *saved, flops=4 * 10**9)

    (packed,) = call(
        pack_kernel, [((64, 2, HEAD + HALF), BF)], packed, out_keep, out_other, flops=10**8
    )
    token_grad, out_part, mine = call(
        unpack_kernel,
        [rows(D), ((8, 2, 2 * HALF), F32), ((1, D), F32)],
        exchange(packed), flops=10**8,
    )
    out_part = jnp.sum(lax.all_to_all(out_part, DP, 0, 0, tiled=True), 0)
    out_grad = out_part.reshape(2, 9, ATT).transpose(1, 0, 2).reshape(9, D)

    (qkv_grad,) = call(
        spatial_backward_kernel, [((ROWS, 3 * ATT), BF)], qkv, token_grad, factors, w_so
    )
    other = swap_cores(mine)
    mine = jnp.where(core == 0, jnp.concatenate([mine, other]), jnp.concatenate([other, mine]))
    other = lax.ppermute(mine, "yhi", [(0, 1), (1, 0), (2, 3), (3, 2)])
    low = lax.axis_index("yhi") % 2 == 0
    factor_grad = jnp.where(low, jnp.concatenate([mine, other]), jnp.concatenate([other, mine]))
    return token_grad[None, None], qkv_grad[None, None], factor_grad[None], out_grad


def solution(mesh):
    fine = Mesh(mesh.devices.reshape(4, 2, 4, 8, 2), DP + SEQ)
    frames = P(DP, SEQ, None, None)
    return jax.shard_map(
        body,
        mesh=fine,
        in_specs=(
            frames,
            frames,
            P(SEQ, None),
            P(None, SEQ),
            P(SEQ, None),
            P(DP, None, None),
            frames,
        ),
        out_specs=(frames, frames, P(DP, None, None), P(SEQ, None)),
        check_vma=False,
    )
```

```python
import math

import jax
import jax.numpy as jnp
from jax import lax
from jax.experimental import pallas as pl
from jax.experimental.pallas import tpu as pltpu
from jax.sharding import Mesh
from jax.sharding import PartitionSpec as P

D = 1152
HEADS = 8
HS = 72
ATT = 576
ROWS = 128
SCALE = 1.0 / math.sqrt(HS)
SEQ = ("yhi", "z", "core")
CHIPS = ("yhi", "z")
DP = ("x", "ylo")
BF = jnp.bfloat16
F32 = jnp.float32


def nn(a, b):
    return lax.dot_general(a, b, (((1,), (0,)), ((), ())), preferred_element_type=F32)


def nt(a, b):
    return lax.dot_general(a, b, (((1,), (1,)), ((), ())), preferred_element_type=F32)


def tn(a, b):
    return lax.dot_general(a, b, (((0,), (0,)), ((), ())), preferred_element_type=F32)


def head_masks():
    head = lax.broadcasted_iota(jnp.int32, (ROWS, ATT), 1) // HS
    return [head == h for h in range(HEADS)]


def stack_heads(masks, a):
    zero = jnp.zeros_like(a)
    return jnp.concatenate([jnp.where(m, a, zero) for m in masks], 0)


def pick_heads(masks, a):
    out = a[:ROWS]
    for h in range(1, HEADS):
        out = jnp.where(masks[h], a[h * ROWS : (h + 1) * ROWS], out)
    return out


def softmax_rows(scores):
    top = jnp.max(scores, -1, keepdims=True)
    weights = jnp.exp(scores - top)
    return weights / jnp.sum(weights, -1, keepdims=True)


def attend(masks, q, k, v, same):
    q_stack = stack_heads(masks, q)
    scores = nt(q_stack, k) * SCALE
    if same is not None:
        scores = jnp.where(same, scores, -1e30)
    probs = softmax_rows(scores)
    probs_b = probs.astype(BF)
    mixed = pick_heads(masks, nn(probs_b, v)).astype(BF)
    return q_stack, probs, probs_b, mixed


def attend_back(masks, q_stack, k, v, probs, probs_b, d_mixed):
    d_stack = stack_heads(masks, d_mixed)
    d_probs = nt(d_stack, v).astype(BF).astype(F32)
    d_v = tn(probs_b, d_stack)
    d_scores = probs * (d_probs - jnp.sum(d_probs * probs, -1, keepdims=True)) * SCALE
    d_scores = d_scores.astype(BF)
    d_q = pick_heads(masks, nn(d_scores, k))
    d_k = tn(d_scores, q_stack)
    return d_q.astype(BF), d_k.astype(BF), d_v.astype(BF)


def spatial_forward_kernel(qkv, mixed):
    q, k, v = qkv[:, :ATT], qkv[:, ATT : 2 * ATT], qkv[:, 2 * ATT :]
    mixed[...] = attend(head_masks(), q, k, v, None)[3]


def spatial_backward_kernel(qkv, hidden_grad, factors, w_so, out):
    q, k, v = qkv[:, :ATT], qkv[:, ATT : 2 * ATT], qkv[:, 2 * ATT :]
    masks = head_masks()
    gated = (hidden_grad[...].astype(F32) * factors[0:1, :]).astype(BF)
    d_mixed = nt(gated, w_so[...]).astype(BF)
    q_stack, probs, probs_b, _ = attend(masks, q, k, v, None)
    d_q, d_k, d_v = attend_back(masks, q_stack, k, v, probs, probs_b, d_mixed)
    out[:, :ATT] = d_q
    out[:, ATT : 2 * ATT] = d_k
    out[:, 2 * ATT :] = d_v


def compact_kernel(place, mine, other, own, part, both, so, out, qkv):
    core = place[0]
    both[core] = mine[...]
    both[1 - core] = other[...]
    for i in range(16):
        shard = both[i % 2, 48 * (i // 2) : 48 * (i // 2) + 48, :].astype(F32)
        so[9 * i : 9 * i + 9, :] = shard[:9]
        out[9 * i : 9 * i + 9, :] = shard[9:18]
        qkv[27 * i : 27 * i + 27, :] = shard[18:45]
    own[OWN[1] : OWN[1] + 144, :] = so[...].astype(BF)
    own[OWN[2] : OWN[2] + 144, :] = out[...].astype(BF)
    own[OWN[0] : OWN[0] + 432, :] = qkv[...].astype(BF)
    at_qkv = pl.multiple_of(core * 208, 16)
    at = pl.multiple_of(core * 64, 16)
    part[0:224, :] = own[pl.ds(OWN[0] + at_qkv, 224), :]
    part[224:304, :] = own[pl.ds(OWN[1] + at, 80), :]
    part[304:384, :] = own[pl.ds(OWN[2] + at, 80), :]


SECTIONS = ((0, 0, 224), (1, 224, 304), (2, 304, 384))
BLOCK = (432, 144, 144)
OWN = (288, 0, 144)
STEP = (208, 64, 64)


COPIES = 6


def start_copies(place, near, swapped, targets, sems):
    for me in range(2):

        @pl.when(place[0] == me)
        def _():
            for section, first, last in (SECTIONS[1], SECTIONS[0], SECTIONS[2]):
                for i, (flip, ref, other) in enumerate(zip((2, 1, 3), near, swapped)):
                    for half in range(2):
                        source = ref if half == me else other
                        skip = 16 * half
                        row = skip + STEP[section] * half
                        to = pl.multiple_of((place[1] ^ flip) * BLOCK[section] + row, 16)
                        rows = last - first - skip
                        pltpu.make_async_copy(
                            source.at[pl.ds(first + skip, rows)],
                            targets[section].at[pl.ds(to, rows)],
                            sems.at[section * COPIES + 2 * i + half],
                        ).start()


def wait_copies(section, near, targets, sems):
    first, last = SECTIONS[section][1:]
    for i in range(3):
        for half in range(2):
            rows = pl.ds(0, last - first - 16 * half)
            sem = sems.at[section * COPIES + 2 * i + half]
            pltpu.make_async_copy(near[i].at[rows], targets[section].at[rows], sem).wait()


def temporal_forward_kernel(
    place, sent, factors, own, b, c, d, other_b, other_c, other_d,
    out_keep, out_send, w_so, w_out, w_qkv, q_out, k_out, v_out, probs_out, mixed_out,
    unit_out, inverse_out, project_out, cot_out, sems,
):
    near, targets = (b, c, d), (w_qkv, w_so, w_out)
    start_copies(place, near, (other_b, other_c, other_d), targets, sems)
    for section, rows in enumerate(BLOCK):
        to = pl.multiple_of(place[1] * rows, 16)
        targets[section][pl.ds(to, rows), :] = own[OWN[section] : OWN[section] + rows, :]
    received = sent[...].reshape(ROWS, 2 * D + ATT)
    tokens, cotangent, mixed_s = received[:, :D], received[:, D : 2 * D], received[:, 2 * D :]
    cot_out[...] = cotangent
    wait_copies(1, near, targets, sems)
    gate_s, shift, scale, gate_t = (factors[i : i + 1, :] for i in range(4))
    project = nn(mixed_s, w_so[...])
    project_out[...] = project
    hidden = (tokens.astype(F32) + gate_s * project).astype(BF).astype(F32)
    centered = hidden - jnp.mean(hidden, -1, keepdims=True)
    inverse = lax.rsqrt(jnp.mean(centered * centered, -1, keepdims=True) + 1e-06)
    inverse_out[...] = jnp.broadcast_to(inverse, (ROWS, 128))
    unit = centered * inverse
    unit_out[...] = unit
    normed = (unit * (1.0 + scale) + shift).astype(BF)
    wait_copies(0, near, targets, sems)
    q, k, v = (nt(normed, w_qkv[i * ATT : (i + 1) * ATT, :]).astype(BF) for i in range(3))
    q_out[...], k_out[...], v_out[...] = q, k, v

    row = lax.broadcasted_iota(jnp.int32, (HEADS * ROWS, ROWS), 0)
    col = lax.broadcasted_iota(jnp.int32, (HEADS * ROWS, ROWS), 1)
    same = ((row ^ col) & 1) == 0
    _, probs, _, mixed = attend(head_masks(), q, k, v, same)
    probs_out[...] = probs
    mixed_out[...] = mixed

    scaled = (cotangent.astype(F32) * gate_t).astype(BF)
    source = lax.broadcasted_iota(jnp.int32, (ATT, ATT), 0)
    target = lax.broadcasted_iota(jnp.int32, (ATT, ATT), 1)
    order = jnp.where(source == (target & 63) * 9 + (target >> 6), 1.0, 0.0).astype(BF)
    ordered = nn(mixed, order).astype(BF)
    left, right = scaled[:, :ATT], scaled[:, ATT:]
    first = place[0] == 0
    keep = tn(ordered, jnp.where(first, left, right))
    send = tn(ordered, jnp.where(first, right, left)).astype(BF)
    for j in range(9):
        out_keep[:, ATT * j : ATT * j + ATT] = keep[64 * j : 64 * j + 64]
        out_send[:, ATT * j : ATT * j + ATT] = send[64 * j : 64 * j + 64]
    wait_copies(2, near, targets, sems)


def temporal_backward_kernel(
    factors, w_so, w_out, w_qkv, q, k, v, probs, mixed, unit, inverse, project, cotangent, packed
):
    scale, gate_t = factors[2:3, :], factors[3:4, :]
    cot = cotangent[...].astype(F32)
    scaled = (cot * gate_t).astype(BF)
    masks = head_masks()
    q, k, v, probs = q[...], k[...], v[...], probs[...]
    d_mixed = nt(scaled, w_out[...]).astype(BF)
    q_stack = stack_heads(masks, q)
    d_q, d_k, d_v = attend_back(masks, q_stack, k, v, probs, probs.astype(BF), d_mixed)
    wq, wk, wv = (w_qkv[i * ATT : (i + 1) * ATT, :] for i in range(3))
    d_normed = (nn(d_q, wq) + nn(d_k, wk) + nn(d_v, wv)).astype(BF).astype(F32)
    unit = unit[...]
    d_unit = d_normed * (1.0 + scale)
    d_hidden = inverse[:, 0:1] * (
        d_unit
        - jnp.mean(d_unit, -1, keepdims=True)
        - unit * jnp.mean(d_unit * unit, -1, keepdims=True)
    )
    grad = (cot + d_hidden).astype(BF)
    packed[:, :D] = grad
    project_t = nn(mixed[...], w_out[...])
    factor_grads = (
        jnp.sum(grad.astype(F32) * project[...], 0, keepdims=True),
        jnp.sum(d_normed, 0, keepdims=True),
        jnp.sum(d_normed * unit, 0, keepdims=True),
        jnp.sum(cot * project_t, 0, keepdims=True),
    )
    tile = jnp.concatenate(factor_grads * 4, 0).astype(BF)
    for i in range(8):
        packed[16 * i : 16 * i + 16, D:] = tile


HALF = 9 * ATT // 2


def pack_kernel(packed, out_keep, out_other, out):
    out[:, :, : 2 * D] = packed[...].reshape(64, 2, 2 * D)
    pair = (out_keep[...] + out_other[...].astype(F32)).astype(BF)
    out[:, 0, 2 * D :] = pair[:, :HALF]
    out[:, 1, 2 * D :] = pair[:, HALF:]


def unpack_kernel(back, token_grad, out_part, factor_part):
    token_grad[...] = back[:, :, :D].reshape(ROWS, D)
    first = lax.broadcasted_iota(jnp.int32, (64, HALF), 0) & 1 == 0
    for r in range(2):
        factor_part[r : r + 1, :] = jnp.sum(back[:, r, D : 2 * D].astype(F32), 0, keepdims=True)
        rows = back[:, r, 2 * D :].astype(F32)
        for core in range(2):
            total = jnp.sum(jnp.where(first == (core == 0), rows, 0.0), 0, keepdims=True)
            for copy in range(8):
                out_part[copy, core : core + 1, HALF * r : HALF * r + HALF] = total


def call(kernel, outs, *args, scalars=0, hbm=0, scratch=(), flops=10**9):
    vmem = pl.BlockSpec(memory_space=pltpu.VMEM)
    specs = [pl.BlockSpec(memory_space=pltpu.SMEM)] * scalars
    specs += [vmem] * (len(args) - scalars - hbm) + [pl.BlockSpec(memory_space=pltpu.HBM)] * hbm
    return pl.pallas_call(
        kernel,
        out_shape=[jax.ShapeDtypeStruct(s, d) for s, d in outs],
        in_specs=specs,
        out_specs=[vmem] * len(outs),
        scratch_shapes=list(scratch),
        compiler_params=pltpu.CompilerParams(vmem_limit_bytes=32 * 2**20),
        cost_estimate=pl.CostEstimate(flops=flops, bytes_accessed=10**7, transcendentals=10**5),
    )(*args)


def exchange(a):
    return lax.all_to_all(a, SEQ, 0, 0, tiled=True)


AXES = DP + SEQ


def device(x, y, z, core):
    ylo, yhi = y % 2, (y % 8) // 2
    return ((((x % 4) * 2 + ylo) * 4 + yhi) * 8 + z % 8) * 2 + core


def receive(a, source):
    pairs = []
    for x in range(4):
        for y in range(8):
            for z in range(8):
                for core in range(2):
                    pairs.append((device(*source(x, y, z, core), core), device(x, y, z, core)))
    return lax.ppermute(a, AXES, pairs)


def swap_cores(a):
    return lax.ppermute(a, "core", [(0, 1), (1, 0)])


SENDERS = (
    ((0, 0), (1, 2), (0, 1), (3, 3), (1, 1), (0, 3), (3, 0), (0, 2)),
    ((0, 5), (1, 7), (0, 4), (1, 6), (1, 4), (2, 6), (1, 5), (2, 7)),
    ((1, 0), (2, 2), (3, 1), (1, 3), (2, 1), (2, 3), (2, 0), (3, 2)),
    ((3, 5), (0, 7), (2, 4), (0, 6), (3, 4), (3, 6), (2, 5), (3, 7)),
)


def class_source(x, y, z, core):
    return *SENDERS[x][y], z


def near_source(dx, dy):
    def source(x, y, z, core):
        sign = 1 - 2 * core
        return x + sign * dx, y + sign * dy, z

    return source


def gather_weights(w_so, w_qkv, w_out, place, sent):
    shard = jnp.concatenate([w_so, w_out, w_qkv.T, jnp.zeros((3, D), BF)], 0)
    shard, sent = lax.optimization_barrier((receive(shard, class_source), sent))
    mine = lax.all_gather(shard, "z", axis=0, tiled=True)
    other = swap_cores(mine)
    rows = lambda n: ((n, D), BF)
    own, part = call(
        compact_kernel, [rows(720), rows(384)], place, mine, other, scalars=1,
        scratch=[
            pltpu.VMEM((2, 384, D), BF),
            pltpu.VMEM((144, D), F32),
            pltpu.VMEM((144, D), F32),
            pltpu.VMEM((432, D), F32),
        ],
    )
    part, sent = lax.optimization_barrier((part, sent))
    near = [receive(part, near_source(1, 0)), receive(part, near_source(0, 1))]
    near.append(receive(near[1], near_source(1, 0)))
    sent = exchange(sent)
    return [own] + near + [swap_cores(a) for a in near], sent


def body(tokens, qkv, w_so, w_qkv, w_out, factors, cotangent):
    tokens, qkv, cotangent, factors = tokens[0, 0], qkv[0, 0], cotangent[0, 0], factors[0]
    core = lax.axis_index("core")
    cls = (lax.axis_index("x") % 2) * 2 + lax.axis_index("ylo")
    place = jnp.stack([core, cls]).astype(jnp.int32)

    (mixed_s,) = call(spatial_forward_kernel, [((ROWS, ATT), BF)], qkv)
    sent = jnp.concatenate([tokens, cotangent, mixed_s], 1).reshape(64, 2, 2 * D + ATT)
    weights, sent = gather_weights(w_so, w_qkv, w_out, place, sent)

    rows = lambda n, kind=BF: ((ROWS, n), kind)
    out_keep, out_send, *saved = call(
        temporal_forward_kernel,
        [
            ((64, 2 * HALF), F32), ((64, 2 * HALF), BF),
            ((ATT, D), BF), ((ATT, D), BF), ((3 * ATT, D), BF),
            rows(ATT), rows(ATT), rows(ATT), ((HEADS * ROWS, ROWS), F32), rows(ATT),
            rows(D, F32), rows(128, F32), rows(D, F32), rows(D),
        ],
        place, sent, factors, *weights,
        scalars=1, hbm=6, flops=4 * 10**9,
        scratch=[pltpu.SemaphoreType.DMA((3 * COPIES,))],
    )
    w_so = saved[0]
    out_other = swap_cores(out_send)
    (packed,) = call(temporal_backward_kernel, [rows(2 * D)], factors, *saved, flops=4 * 10**9)

    (packed,) = call(
        pack_kernel, [((64, 2, 2 * D + HALF), BF)], packed, out_keep, out_other, flops=10**8
    )
    token_grad, out_part, mine = call(
        unpack_kernel,
        [rows(D), ((8, 2, 2 * HALF), F32), ((2, D), F32)],
        exchange(packed), flops=10**8,
    )
    out_part = jnp.sum(lax.all_to_all(out_part, DP, 0, 0, tiled=True), 0)
    out_grad = out_part.reshape(2, 9, ATT).transpose(1, 0, 2).reshape(9, D)

    (qkv_grad,) = call(
        spatial_backward_kernel, [((ROWS, 3 * ATT), BF)], qkv, token_grad, factors, w_so
    )
    other = swap_cores(mine)
    factor_grad = jnp.where(core == 0, jnp.concatenate([mine, other]), jnp.concatenate([other, mine]))
    return token_grad[None, None], qkv_grad[None, None], factor_grad[None], out_grad


def solution(mesh):
    fine = Mesh(mesh.devices.reshape(4, 2, 4, 8, 2), DP + SEQ)
    frames = P(DP, SEQ, None, None)
    return jax.shard_map(
        body,
        mesh=fine,
        in_specs=(
            frames,
            frames,
            P(SEQ, None),
            P(None, SEQ),
            P(SEQ, None),
            P(DP, None, None),
            frames,
        ),
        out_specs=(frames, frames, P(DP, None, None), P(SEQ, None)),
        check_vma=False,
    )
```

```python
import math

import jax
import jax.numpy as jnp
from jax import lax
from jax.experimental import pallas as pl
from jax.experimental.pallas import tpu as pltpu
from jax.sharding import Mesh
from jax.sharding import PartitionSpec as P

D = 1152
HEADS = 8
HS = 72
ATT = 576
ROWS = 128
SCALE = 1.0 / math.sqrt(HS)
SEQ = ("yhi", "z", "core")
CHIPS = ("yhi", "z")
DP = ("x", "ylo")
BF = jnp.bfloat16
F32 = jnp.float32


def nn(a, b):
    return lax.dot_general(a, b, (((1,), (0,)), ((), ())), preferred_element_type=F32)


def nt(a, b):
    return lax.dot_general(a, b, (((1,), (1,)), ((), ())), preferred_element_type=F32)


def tn(a, b):
    return lax.dot_general(a, b, (((0,), (0,)), ((), ())), preferred_element_type=F32)


def head_masks():
    head = lax.broadcasted_iota(jnp.int32, (ROWS, ATT), 1) // HS
    return [head == h for h in range(HEADS)]


def stack_heads(masks, a):
    zero = jnp.zeros_like(a)
    return jnp.concatenate([jnp.where(m, a, zero) for m in masks], 0)


def pick_heads(masks, a):
    out = a[:ROWS]
    for h in range(1, HEADS):
        out = jnp.where(masks[h], a[h * ROWS : (h + 1) * ROWS], out)
    return out


def softmax_rows(scores):
    top = jnp.max(scores, -1, keepdims=True)
    weights = jnp.exp(scores - top)
    return weights / jnp.sum(weights, -1, keepdims=True)


def attend(masks, q, k, v, same):
    q_stack = stack_heads(masks, q)
    scores = nt(q_stack, k) * SCALE
    if same is not None:
        scores = jnp.where(same, scores, -1e30)
    probs = softmax_rows(scores)
    probs_b = probs.astype(BF)
    mixed = pick_heads(masks, nn(probs_b, v)).astype(BF)
    return q_stack, probs, probs_b, mixed


def attend_back(masks, q_stack, k, v, probs, probs_b, d_mixed):
    d_stack = stack_heads(masks, d_mixed)
    d_probs = nt(d_stack, v).astype(BF).astype(F32)
    d_v = tn(probs_b, d_stack)
    d_scores = probs * (d_probs - jnp.sum(d_probs * probs, -1, keepdims=True)) * SCALE
    d_scores = d_scores.astype(BF)
    d_q = pick_heads(masks, nn(d_scores, k))
    d_k = tn(d_scores, q_stack)
    return d_q.astype(BF), d_k.astype(BF), d_v.astype(BF)


def spatial_forward_kernel(qkv, mixed):
    q, k, v = qkv[:, :ATT], qkv[:, ATT : 2 * ATT], qkv[:, 2 * ATT :]
    mixed[...] = attend(head_masks(), q, k, v, None)[3]


def spatial_backward_kernel(qkv, hidden_grad, factors, w_so, out):
    q, k, v = qkv[:, :ATT], qkv[:, ATT : 2 * ATT], qkv[:, 2 * ATT :]
    masks = head_masks()
    gated = (hidden_grad[...].astype(F32) * factors[0:1, :]).astype(BF)
    d_mixed = nt(gated, w_so[...]).astype(BF)
    q_stack, probs, probs_b, _ = attend(masks, q, k, v, None)
    d_q, d_k, d_v = attend_back(masks, q_stack, k, v, probs, probs_b, d_mixed)
    out[:, :ATT] = d_q
    out[:, ATT : 2 * ATT] = d_k
    out[:, 2 * ATT :] = d_v


def compact_kernel(place, mine, other, own, part, both, so, out, qkv):
    core = place[0]
    both[core] = mine[...]
    both[1 - core] = other[...]
    for i in range(16):
        shard = both[i % 2, 48 * (i // 2) : 48 * (i // 2) + 48, :].astype(F32)
        so[9 * i : 9 * i + 9, :] = shard[:9]
        out[9 * i : 9 * i + 9, :] = shard[9:18]
        qkv[27 * i : 27 * i + 27, :] = shard[18:45]
    own[OWN[1] : OWN[1] + 144, :] = so[...].astype(BF)
    own[OWN[2] : OWN[2] + 144, :] = out[...].astype(BF)
    own[OWN[0] : OWN[0] + 432, :] = qkv[...].astype(BF)
    at_qkv = pl.multiple_of(core * 208, 16)
    at = pl.multiple_of(core * 64, 16)
    part[0:224, :] = own[pl.ds(OWN[0] + at_qkv, 224), :]
    part[224:304, :] = own[pl.ds(OWN[1] + at, 80), :]
    part[304:384, :] = own[pl.ds(OWN[2] + at, 80), :]


SECTIONS = ((0, 0, 224), (1, 224, 304), (2, 304, 384))
BLOCK = (432, 144, 144)
OWN = (288, 0, 144)
STEP = (208, 64, 64)


COPIES = 6


def start_copies(place, near, swapped, targets, sems):
    for me in range(2):

        @pl.when(place[0] == me)
        def _():
            for section, first, last in (SECTIONS[1], SECTIONS[0], SECTIONS[2]):
                for i, (flip, ref, other) in enumerate(zip((2, 1, 3), near, swapped)):
                    for half in range(2):
                        source = ref if half == me else other
                        skip = 16 * half
                        row = skip + STEP[section] * half
                        to = pl.multiple_of((place[1] ^ flip) * BLOCK[section] + row, 16)
                        rows = last - first - skip
                        pltpu.make_async_copy(
                            source.at[pl.ds(first + skip, rows)],
                            targets[section].at[pl.ds(to, rows)],
                            sems.at[section * COPIES + 2 * i + half],
                        ).start()


def wait_copies(section, near, targets, sems):
    first, last = SECTIONS[section][1:]
    for i in range(3):
        for half in range(2):
            rows = pl.ds(0, last - first - 16 * half)
            sem = sems.at[section * COPIES + 2 * i + half]
            pltpu.make_async_copy(near[i].at[rows], targets[section].at[rows], sem).wait()


def temporal_forward_kernel(
    place, sent, factors, own, b, c, d, other_b, other_c, other_d,
    out_keep, out_send, w_so, w_out, w_qkv, q_out, k_out, v_out, probs_out, mixed_out,
    unit_out, inverse_out, project_out, cot_out, sems,
):
    near, targets = (b, c, d), (w_qkv, w_so, w_out)
    start_copies(place, near, (other_b, other_c, other_d), targets, sems)
    for section, rows in enumerate(BLOCK):
        to = pl.multiple_of(place[1] * rows, 16)
        targets[section][pl.ds(to, rows), :] = own[OWN[section] : OWN[section] + rows, :]
    received = sent[...].reshape(ROWS, 2 * D + ATT)
    tokens, cotangent, mixed_s = received[:, :D], received[:, D : 2 * D], received[:, 2 * D :]
    cot_out[...] = cotangent
    wait_copies(1, near, targets, sems)
    gate_s, shift, scale, gate_t = (factors[i : i + 1, :] for i in range(4))
    project = nn(mixed_s, w_so[...])
    project_out[...] = project
    hidden = (tokens.astype(F32) + gate_s * project).astype(BF).astype(F32)
    centered = hidden - jnp.mean(hidden, -1, keepdims=True)
    inverse = lax.rsqrt(jnp.mean(centered * centered, -1, keepdims=True) + 1e-06)
    inverse_out[...] = jnp.broadcast_to(inverse, (ROWS, 128))
    unit = centered * inverse
    unit_out[...] = unit
    normed = (unit * (1.0 + scale) + shift).astype(BF)
    wait_copies(0, near, targets, sems)
    q, k, v = (nt(normed, w_qkv[i * ATT : (i + 1) * ATT, :]).astype(BF) for i in range(3))
    q_out[...], k_out[...], v_out[...] = q, k, v

    row = lax.broadcasted_iota(jnp.int32, (HEADS * ROWS, ROWS), 0)
    col = lax.broadcasted_iota(jnp.int32, (HEADS * ROWS, ROWS), 1)
    same = ((row ^ col) & 1) == 0
    _, probs, _, mixed = attend(head_masks(), q, k, v, same)
    probs_out[...] = probs
    mixed_out[...] = mixed

    scaled = (cotangent.astype(F32) * gate_t).astype(BF)
    source = lax.broadcasted_iota(jnp.int32, (ATT, ATT), 0)
    target = lax.broadcasted_iota(jnp.int32, (ATT, ATT), 1)
    order = jnp.where(source == (target & 63) * 9 + (target >> 6), 1.0, 0.0).astype(BF)
    ordered = nn(mixed, order).astype(BF)
    left, right = scaled[:, :ATT], scaled[:, ATT:]
    first = place[0] == 0
    keep = tn(ordered, jnp.where(first, left, right))
    send = tn(ordered, jnp.where(first, right, left)).astype(BF)
    for j in range(9):
        out_keep[:, ATT * j : ATT * j + ATT] = keep[64 * j : 64 * j + 64]
        out_send[:, ATT * j : ATT * j + ATT] = send[64 * j : 64 * j + 64]
    wait_copies(2, near, targets, sems)


def temporal_backward_kernel(
    factors, w_so, w_out, w_qkv, q, k, v, probs, mixed, unit, inverse, project, cotangent, packed
):
    scale, gate_t = factors[2:3, :], factors[3:4, :]
    cot = cotangent[...].astype(F32)
    scaled = (cot * gate_t).astype(BF)
    masks = head_masks()
    q, k, v, probs = q[...], k[...], v[...], probs[...]
    d_mixed = nt(scaled, w_out[...]).astype(BF)
    q_stack = stack_heads(masks, q)
    d_q, d_k, d_v = attend_back(masks, q_stack, k, v, probs, probs.astype(BF), d_mixed)
    wq, wk, wv = (w_qkv[i * ATT : (i + 1) * ATT, :] for i in range(3))
    d_normed = (nn(d_q, wq) + nn(d_k, wk) + nn(d_v, wv)).astype(BF).astype(F32)
    unit = unit[...]
    d_unit = d_normed * (1.0 + scale)
    d_hidden = inverse[:, 0:1] * (
        d_unit
        - jnp.mean(d_unit, -1, keepdims=True)
        - unit * jnp.mean(d_unit * unit, -1, keepdims=True)
    )
    grad = (cot + d_hidden).astype(BF)
    packed[:, :D] = grad
    project_t = nn(mixed[...], w_out[...])
    factor_grads = (
        jnp.sum(grad.astype(F32) * project[...], 0, keepdims=True),
        jnp.sum(d_normed, 0, keepdims=True),
        jnp.sum(d_normed * unit, 0, keepdims=True),
        jnp.sum(cot * project_t, 0, keepdims=True),
    )
    tile = jnp.concatenate(factor_grads * 4, 0).astype(BF)
    for i in range(8):
        packed[16 * i : 16 * i + 16, D:] = tile


HALF = 9 * ATT // 2


def pack_kernel(packed, out_keep, out_other, out):
    out[:, :, : 2 * D] = packed[...].reshape(64, 2, 2 * D)
    pair = (out_keep[...] + out_other[...].astype(F32)).astype(BF)
    out[:, 0, 2 * D :] = pair[:, :HALF]
    out[:, 1, 2 * D :] = pair[:, HALF:]


def unpack_kernel(back, token_grad, out_part, factor_part):
    token_grad[...] = back[:, :, :D].reshape(ROWS, D)
    first = lax.broadcasted_iota(jnp.int32, (64, HALF), 0) & 1 == 0
    for r in range(2):
        factor_part[r : r + 1, :] = jnp.sum(back[:, r, D : 2 * D].astype(F32), 0, keepdims=True)
        rows = back[:, r, 2 * D :].astype(F32)
        for core in range(2):
            total = jnp.sum(jnp.where(first == (core == 0), rows, 0.0), 0, keepdims=True)
            for copy in range(8):
                out_part[copy, core : core + 1, HALF * r : HALF * r + HALF] = total


def call(kernel, outs, *args, scalars=0, hbm=0, scratch=(), flops=10**9):
    vmem = pl.BlockSpec(memory_space=pltpu.VMEM)
    specs = [pl.BlockSpec(memory_space=pltpu.SMEM)] * scalars
    specs += [vmem] * (len(args) - scalars - hbm) + [pl.BlockSpec(memory_space=pltpu.HBM)] * hbm
    return pl.pallas_call(
        kernel,
        out_shape=[jax.ShapeDtypeStruct(s, d) for s, d in outs],
        in_specs=specs,
        out_specs=[vmem] * len(outs),
        scratch_shapes=list(scratch),
        compiler_params=pltpu.CompilerParams(vmem_limit_bytes=32 * 2**20),
        cost_estimate=pl.CostEstimate(flops=flops, bytes_accessed=10**7, transcendentals=10**5),
    )(*args)


def exchange(a):
    return lax.all_to_all(a, SEQ, 0, 0, tiled=True)


AXES = DP + SEQ


def device(x, y, z, core):
    ylo, yhi = y % 2, (y % 8) // 2
    return ((((x % 4) * 2 + ylo) * 4 + yhi) * 8 + z % 8) * 2 + core


def receive(a, source):
    pairs = []
    for x in range(4):
        for y in range(8):
            for z in range(8):
                for core in range(2):
                    pairs.append((device(*source(x, y, z, core), core), device(x, y, z, core)))
    return lax.ppermute(a, AXES, pairs)


def swap_cores(a):
    return lax.ppermute(a, "core", [(0, 1), (1, 0)])


SENDERS = (
    ((0, 0), (1, 2), (0, 1), (3, 3), (1, 1), (0, 3), (3, 0), (0, 2)),
    ((0, 5), (1, 7), (0, 4), (1, 6), (1, 4), (2, 6), (1, 5), (2, 7)),
    ((1, 0), (2, 2), (3, 1), (1, 3), (2, 1), (2, 3), (2, 0), (3, 2)),
    ((3, 5), (0, 7), (2, 4), (0, 6), (3, 4), (3, 6), (2, 5), (3, 7)),
)


def class_source(x, y, z, core):
    return *SENDERS[x][y], z


def near_source(dx, dy):
    def source(x, y, z, core):
        sign = 1 - 2 * core
        return x + sign * dx, y + sign * dy, z

    return source


def gather_weights(w_so, w_qkv, w_out, place, sent):
    shard = jnp.concatenate([w_so, w_out, w_qkv.T, jnp.zeros((3, D), BF)], 0)
    shard, sent = lax.optimization_barrier((receive(shard, class_source), sent))
    mine = lax.all_gather(shard, "z", axis=0, tiled=True)
    mine, sent = lax.optimization_barrier((mine, sent))
    sent = exchange(sent)
    other = swap_cores(mine)
    rows = lambda n: ((n, D), BF)
    own, part = call(
        compact_kernel, [rows(720), rows(384)], place, mine, other, scalars=1,
        scratch=[
            pltpu.VMEM((2, 384, D), BF),
            pltpu.VMEM((144, D), F32),
            pltpu.VMEM((144, D), F32),
            pltpu.VMEM((432, D), F32),
        ],
    )
    near = [receive(part, near_source(1, 0)), receive(part, near_source(0, 1))]
    near.append(receive(near[1], near_source(1, 0)))
    return [own] + near + [swap_cores(a) for a in near], sent


def body(tokens, qkv, w_so, w_qkv, w_out, factors, cotangent):
    tokens, qkv, cotangent, factors = tokens[0, 0], qkv[0, 0], cotangent[0, 0], factors[0]
    core = lax.axis_index("core")
    cls = (lax.axis_index("x") % 2) * 2 + lax.axis_index("ylo")
    place = jnp.stack([core, cls]).astype(jnp.int32)

    (mixed_s,) = call(spatial_forward_kernel, [((ROWS, ATT), BF)], qkv)
    sent = jnp.concatenate([tokens, cotangent, mixed_s], 1).reshape(64, 2, 2 * D + ATT)
    weights, sent = gather_weights(w_so, w_qkv, w_out, place, sent)

    rows = lambda n, kind=BF: ((ROWS, n), kind)
    out_keep, out_send, *saved = call(
        temporal_forward_kernel,
        [
            ((64, 2 * HALF), F32), ((64, 2 * HALF), BF),
            ((ATT, D), BF), ((ATT, D), BF), ((3 * ATT, D), BF),
            rows(ATT), rows(ATT), rows(ATT), ((HEADS * ROWS, ROWS), F32), rows(ATT),
            rows(D, F32), rows(128, F32), rows(D, F32), rows(D),
        ],
        place, sent, factors, *weights,
        scalars=1, hbm=6, flops=4 * 10**9,
        scratch=[pltpu.SemaphoreType.DMA((3 * COPIES,))],
    )
    w_so = saved[0]
    out_other = swap_cores(out_send)
    (packed,) = call(temporal_backward_kernel, [rows(2 * D)], factors, *saved, flops=4 * 10**9)

    (packed,) = call(
        pack_kernel, [((64, 2, 2 * D + HALF), BF)], packed, out_keep, out_other, flops=10**8
    )
    token_grad, out_part, mine = call(
        unpack_kernel,
        [rows(D), ((8, 2, 2 * HALF), F32), ((2, D), F32)],
        exchange(packed), flops=10**8,
    )
    out_part = jnp.sum(lax.all_to_all(out_part, DP, 0, 0, tiled=True), 0)
    out_grad = out_part.reshape(2, 9, ATT).transpose(1, 0, 2).reshape(9, D)

    (qkv_grad,) = call(
        spatial_backward_kernel, [((ROWS, 3 * ATT), BF)], qkv, token_grad, factors, w_so
    )
    other = swap_cores(mine)
    factor_grad = jnp.where(core == 0, jnp.concatenate([mine, other]), jnp.concatenate([other, mine]))
    return token_grad[None, None], qkv_grad[None, None], factor_grad[None], out_grad


def solution(mesh):
    fine = Mesh(mesh.devices.reshape(4, 2, 4, 8, 2), DP + SEQ)
    frames = P(DP, SEQ, None, None)
    return jax.shard_map(
        body,
        mesh=fine,
        in_specs=(
            frames,
            frames,
            P(SEQ, None),
            P(None, SEQ),
            P(SEQ, None),
            P(DP, None, None),
            frames,
        ),
        out_specs=(frames, frames, P(DP, None, None), P(SEQ, None)),
        check_vma=False,
    )
```

```python
import math

import jax
import jax.numpy as jnp
from jax import lax
from jax.experimental import pallas as pl
from jax.experimental.pallas import tpu as pltpu
from jax.sharding import Mesh
from jax.sharding import PartitionSpec as P

D = 1152
HEADS = 8
HS = 72
ATT = 576
ROWS = 128
SCALE = 1.0 / math.sqrt(HS)
SEQ = ("yhi", "z", "core")
CHIPS = ("yhi", "z")
DP = ("x", "ylo")
BF = jnp.bfloat16
F32 = jnp.float32


def nn(a, b):
    return lax.dot_general(a, b, (((1,), (0,)), ((), ())), preferred_element_type=F32)


def nt(a, b):
    return lax.dot_general(a, b, (((1,), (1,)), ((), ())), preferred_element_type=F32)


def tn(a, b):
    return lax.dot_general(a, b, (((0,), (0,)), ((), ())), preferred_element_type=F32)


def head_masks():
    head = lax.broadcasted_iota(jnp.int32, (ROWS, ATT), 1) // HS
    return [head == h for h in range(HEADS)]


def stack_heads(masks, a):
    zero = jnp.zeros_like(a)
    return jnp.concatenate([jnp.where(m, a, zero) for m in masks], 0)


def pick_heads(masks, a):
    out = a[:ROWS]
    for h in range(1, HEADS):
        out = jnp.where(masks[h], a[h * ROWS : (h + 1) * ROWS], out)
    return out


def softmax_rows(scores):
    top = jnp.max(scores, -1, keepdims=True)
    weights = jnp.exp(scores - top)
    return weights / jnp.sum(weights, -1, keepdims=True)


def attend(masks, q, k, v, same):
    q_stack = stack_heads(masks, q)
    scores = nt(q_stack, k) * SCALE
    if same is not None:
        scores = jnp.where(same, scores, -1e30)
    probs = softmax_rows(scores)
    probs_b = probs.astype(BF)
    mixed = pick_heads(masks, nn(probs_b, v)).astype(BF)
    return q_stack, probs, probs_b, mixed


def attend_back(masks, q_stack, k, v, probs, probs_b, d_mixed):
    d_stack = stack_heads(masks, d_mixed)
    d_probs = nt(d_stack, v).astype(BF).astype(F32)
    d_v = tn(probs_b, d_stack)
    d_scores = probs * (d_probs - jnp.sum(d_probs * probs, -1, keepdims=True)) * SCALE
    d_scores = d_scores.astype(BF)
    d_q = pick_heads(masks, nn(d_scores, k))
    d_k = tn(d_scores, q_stack)
    return d_q.astype(BF), d_k.astype(BF), d_v.astype(BF)


def spatial_forward_kernel(qkv, mixed):
    q, k, v = qkv[:, :ATT], qkv[:, ATT : 2 * ATT], qkv[:, 2 * ATT :]
    mixed[...] = attend(head_masks(), q, k, v, None)[3]


def spatial_backward_kernel(qkv, hidden_grad, factors, w_so, out):
    q, k, v = qkv[:, :ATT], qkv[:, ATT : 2 * ATT], qkv[:, 2 * ATT :]
    masks = head_masks()
    gated = (hidden_grad[...].astype(F32) * factors[0:1, :]).astype(BF)
    d_mixed = nt(gated, w_so[...]).astype(BF)
    q_stack, probs, probs_b, _ = attend(masks, q, k, v, None)
    d_q, d_k, d_v = attend_back(masks, q_stack, k, v, probs, probs_b, d_mixed)
    out[:, :ATT] = d_q
    out[:, ATT : 2 * ATT] = d_k
    out[:, 2 * ATT :] = d_v


def compact_kernel(place, mine, other, own, part, both, so, out, qkv):
    core = place[0]
    both[core] = mine[...]
    both[1 - core] = other[...]
    for i in range(16):
        shard = both[i % 2, 48 * (i // 2) : 48 * (i // 2) + 48, :].astype(F32)
        so[9 * i : 9 * i + 9, :] = shard[:9]
        out[9 * i : 9 * i + 9, :] = shard[9:18]
        qkv[27 * i : 27 * i + 27, :] = shard[18:45]
    own[OWN[1] : OWN[1] + 144, :] = so[...].astype(BF)
    own[OWN[2] : OWN[2] + 144, :] = out[...].astype(BF)
    own[OWN[0] : OWN[0] + 432, :] = qkv[...].astype(BF)
    at_qkv = pl.multiple_of(core * 208, 16)
    at = pl.multiple_of(core * 64, 16)
    part[0:224, :] = own[pl.ds(OWN[0] + at_qkv, 224), :]
    part[224:304, :] = own[pl.ds(OWN[1] + at, 80), :]
    part[304:384, :] = own[pl.ds(OWN[2] + at, 80), :]


SECTIONS = ((0, 0, 224), (1, 224, 304), (2, 304, 384))
BLOCK = (432, 144, 144)
OWN = (288, 0, 144)
STEP = (208, 64, 64)


COPIES = 6


def start_copies(place, near, swapped, targets, sems):
    for me in range(2):

        @pl.when(place[0] == me)
        def _():
            for section, first, last in (SECTIONS[1], SECTIONS[0], SECTIONS[2]):
                for i, (flip, ref, other) in enumerate(zip((2, 1, 3), near, swapped)):
                    for half in range(2):
                        source = ref if half == me else other
                        skip = 16 * half
                        row = skip + STEP[section] * half
                        to = pl.multiple_of((place[1] ^ flip) * BLOCK[section] + row, 16)
                        rows = last - first - skip
                        pltpu.make_async_copy(
                            source.at[pl.ds(first + skip, rows)],
                            targets[section].at[pl.ds(to, rows)],
                            sems.at[section * COPIES + 2 * i + half],
                        ).start()


def wait_copies(section, near, targets, sems):
    first, last = SECTIONS[section][1:]
    for i in range(3):
        for half in range(2):
            rows = pl.ds(0, last - first - 16 * half)
            sem = sems.at[section * COPIES + 2 * i + half]
            pltpu.make_async_copy(near[i].at[rows], targets[section].at[rows], sem).wait()


def temporal_forward_kernel(
    place, sent, factors, own, b, c, d, other_b, other_c, other_d,
    out_keep, out_send, w_so, w_out, w_qkv, q_out, k_out, v_out, probs_out, mixed_out,
    unit_out, inverse_out, project_out, cot_out, sems,
):
    near, targets = (b, c, d), (w_qkv, w_so, w_out)
    start_copies(place, near, (other_b, other_c, other_d), targets, sems)
    for section, rows in enumerate(BLOCK):
        to = pl.multiple_of(place[1] * rows, 16)
        targets[section][pl.ds(to, rows), :] = own[OWN[section] : OWN[section] + rows, :]
    received = sent[...].reshape(ROWS, 2 * D + ATT)
    tokens, cotangent, mixed_s = received[:, :D], received[:, D : 2 * D], received[:, 2 * D :]
    cot_out[...] = cotangent
    wait_copies(1, near, targets, sems)
    gate_s, shift, scale, gate_t = (factors[i : i + 1, :] for i in range(4))
    project = nn(mixed_s, w_so[...])
    project_out[...] = project
    hidden = (tokens.astype(F32) + gate_s * project).astype(BF).astype(F32)
    centered = hidden - jnp.mean(hidden, -1, keepdims=True)
    inverse = lax.rsqrt(jnp.mean(centered * centered, -1, keepdims=True) + 1e-06)
    inverse_out[...] = jnp.broadcast_to(inverse, (ROWS, 128))
    unit = centered * inverse
    unit_out[...] = unit
    normed = (unit * (1.0 + scale) + shift).astype(BF)
    wait_copies(0, near, targets, sems)
    q, k, v = (nt(normed, w_qkv[i * ATT : (i + 1) * ATT, :]).astype(BF) for i in range(3))
    q_out[...], k_out[...], v_out[...] = q, k, v

    row = lax.broadcasted_iota(jnp.int32, (HEADS * ROWS, ROWS), 0)
    col = lax.broadcasted_iota(jnp.int32, (HEADS * ROWS, ROWS), 1)
    same = ((row ^ col) & 1) == 0
    _, probs, _, mixed = attend(head_masks(), q, k, v, same)
    probs_out[...] = probs
    mixed_out[...] = mixed

    scaled = (cotangent.astype(F32) * gate_t).astype(BF)
    source = lax.broadcasted_iota(jnp.int32, (ATT, ATT), 0)
    target = lax.broadcasted_iota(jnp.int32, (ATT, ATT), 1)
    order = jnp.where(source == (target & 63) * 9 + (target >> 6), 1.0, 0.0).astype(BF)
    ordered = nn(mixed, order).astype(BF)
    left, right = scaled[:, :ATT], scaled[:, ATT:]
    first = place[0] == 0
    keep = tn(ordered, jnp.where(first, left, right))
    send = tn(ordered, jnp.where(first, right, left)).astype(BF)
    for j in range(9):
        out_keep[:, ATT * j : ATT * j + ATT] = keep[64 * j : 64 * j + 64]
        out_send[:, ATT * j : ATT * j + ATT] = send[64 * j : 64 * j + 64]
    wait_copies(2, near, targets, sems)


def temporal_backward_kernel(
    factors, w_so, w_out, w_qkv, q, k, v, probs, mixed, unit, inverse, project, cotangent, packed
):
    scale, gate_t = factors[2:3, :], factors[3:4, :]
    cot = cotangent[...].astype(F32)
    scaled = (cot * gate_t).astype(BF)
    masks = head_masks()
    q, k, v, probs = q[...], k[...], v[...], probs[...]
    d_mixed = nt(scaled, w_out[...]).astype(BF)
    q_stack = stack_heads(masks, q)
    d_q, d_k, d_v = attend_back(masks, q_stack, k, v, probs, probs.astype(BF), d_mixed)
    wq, wk, wv = (w_qkv[i * ATT : (i + 1) * ATT, :] for i in range(3))
    d_normed = (nn(d_q, wq) + nn(d_k, wk) + nn(d_v, wv)).astype(BF).astype(F32)
    unit = unit[...]
    d_unit = d_normed * (1.0 + scale)
    d_hidden = inverse[:, 0:1] * (
        d_unit
        - jnp.mean(d_unit, -1, keepdims=True)
        - unit * jnp.mean(d_unit * unit, -1, keepdims=True)
    )
    grad = (cot + d_hidden).astype(BF)
    packed[:, :D] = grad
    project_t = nn(mixed[...], w_out[...])
    factor_grads = (
        jnp.sum(grad.astype(F32) * project[...], 0, keepdims=True),
        jnp.sum(d_normed, 0, keepdims=True),
        jnp.sum(d_normed * unit, 0, keepdims=True),
        jnp.sum(cot * project_t, 0, keepdims=True),
    )
    tile = jnp.concatenate(factor_grads * 4, 0).astype(BF)
    for i in range(8):
        packed[16 * i : 16 * i + 16, D:] = tile


HALF = 9 * ATT // 2


def pack_kernel(packed, out_keep, out_other, out):
    out[:, :, : 2 * D] = packed[...].reshape(64, 2, 2 * D)
    pair = (out_keep[...] + out_other[...].astype(F32)).astype(BF)
    out[:, 0, 2 * D :] = pair[:, :HALF]
    out[:, 1, 2 * D :] = pair[:, HALF:]


def unpack_kernel(back, token_grad, out_part, factor_part):
    token_grad[...] = back[:, :, :D].reshape(ROWS, D)
    first = lax.broadcasted_iota(jnp.int32, (64, HALF), 0) & 1 == 0
    for r in range(2):
        factor_part[r : r + 1, :] = jnp.sum(back[:, r, D : 2 * D].astype(F32), 0, keepdims=True)
        rows = back[:, r, 2 * D :].astype(F32)
        for core in range(2):
            total = jnp.sum(jnp.where(first == (core == 0), rows, 0.0), 0, keepdims=True)
            for copy in range(8):
                out_part[copy, core : core + 1, HALF * r : HALF * r + HALF] = total


def call(kernel, outs, *args, scalars=0, hbm=0, scratch=(), flops=10**9):
    vmem = pl.BlockSpec(memory_space=pltpu.VMEM)
    specs = [pl.BlockSpec(memory_space=pltpu.SMEM)] * scalars
    specs += [vmem] * (len(args) - scalars - hbm) + [pl.BlockSpec(memory_space=pltpu.HBM)] * hbm
    return pl.pallas_call(
        kernel,
        out_shape=[jax.ShapeDtypeStruct(s, d) for s, d in outs],
        in_specs=specs,
        out_specs=[vmem] * len(outs),
        scratch_shapes=list(scratch),
        compiler_params=pltpu.CompilerParams(vmem_limit_bytes=32 * 2**20),
        cost_estimate=pl.CostEstimate(flops=flops, bytes_accessed=10**7, transcendentals=10**5),
    )(*args)


def exchange(a):
    return lax.all_to_all(a, SEQ, 0, 0, tiled=True)


AXES = DP + SEQ


def device(x, y, z, core):
    ylo, yhi = y % 2, (y % 8) // 2
    return ((((x % 4) * 2 + ylo) * 4 + yhi) * 8 + z % 8) * 2 + core


def receive(a, source):
    pairs = []
    for x in range(4):
        for y in range(8):
            for z in range(8):
                for core in range(2):
                    pairs.append((device(*source(x, y, z, core), core), device(x, y, z, core)))
    return lax.ppermute(a, AXES, pairs)


def swap_cores(a):
    return lax.ppermute(a, "core", [(0, 1), (1, 0)])


SENDERS = (
    ((0, 0), (1, 2), (0, 1), (3, 3), (1, 1), (0, 3), (3, 0), (0, 2)),
    ((0, 5), (1, 7), (0, 4), (1, 6), (1, 4), (2, 6), (1, 5), (2, 7)),
    ((1, 0), (2, 2), (3, 1), (1, 3), (2, 1), (2, 3), (2, 0), (3, 2)),
    ((3, 5), (0, 7), (2, 4), (0, 6), (3, 4), (3, 6), (2, 5), (3, 7)),
)


def class_source(x, y, z, core):
    return *SENDERS[x][y], z


def near_source(dx, dy):
    def source(x, y, z, core):
        sign = 1 - 2 * core
        return x + sign * dx, y + sign * dy, z

    return source


def gather_weights(w_so, w_qkv, w_out, place, sent):
    shard = jnp.concatenate([w_so, w_out, w_qkv.T, jnp.zeros((3, D), BF)], 0)
    shard, sent = lax.optimization_barrier((receive(shard, class_source), sent))
    mine = lax.all_gather(shard, "z", axis=0, tiled=True)
    mine, sent = lax.optimization_barrier((mine, sent))
    sent = exchange(sent)
    other = swap_cores(mine)
    rows = lambda n: ((n, D), BF)
    own, part = call(
        compact_kernel, [rows(720), rows(384)], place, mine, other, scalars=1,
        scratch=[
            pltpu.VMEM((2, 384, D), BF),
            pltpu.VMEM((144, D), F32),
            pltpu.VMEM((144, D), F32),
            pltpu.VMEM((432, D), F32),
        ],
    )
    near = [receive(part, near_source(1, 0)), receive(part, near_source(0, 1))]
    near[1], sent = lax.optimization_barrier((near[1], sent))
    near.append(receive(near[1], near_source(1, 0)))
    return [own] + near + [swap_cores(a) for a in near], sent


def body(tokens, qkv, w_so, w_qkv, w_out, factors, cotangent):
    tokens, qkv, cotangent, factors = tokens[0, 0], qkv[0, 0], cotangent[0, 0], factors[0]
    core = lax.axis_index("core")
    cls = (lax.axis_index("x") % 2) * 2 + lax.axis_index("ylo")
    place = jnp.stack([core, cls]).astype(jnp.int32)

    (mixed_s,) = call(spatial_forward_kernel, [((ROWS, ATT), BF)], qkv)
    sent = jnp.concatenate([tokens, cotangent, mixed_s], 1).reshape(64, 2, 2 * D + ATT)
    weights, sent = gather_weights(w_so, w_qkv, w_out, place, sent)

    rows = lambda n, kind=BF: ((ROWS, n), kind)
    out_keep, out_send, *saved = call(
        temporal_forward_kernel,
        [
            ((64, 2 * HALF), F32), ((64, 2 * HALF), BF),
            ((ATT, D), BF), ((ATT, D), BF), ((3 * ATT, D), BF),
            rows(ATT), rows(ATT), rows(ATT), ((HEADS * ROWS, ROWS), F32), rows(ATT),
            rows(D, F32), rows(128, F32), rows(D, F32), rows(D),
        ],
        place, sent, factors, *weights,
        scalars=1, hbm=6, flops=4 * 10**9,
        scratch=[pltpu.SemaphoreType.DMA((3 * COPIES,))],
    )
    w_so = saved[0]
    out_other = swap_cores(out_send)
    (packed,) = call(temporal_backward_kernel, [rows(2 * D)], factors, *saved, flops=4 * 10**9)

    (packed,) = call(
        pack_kernel, [((64, 2, 2 * D + HALF), BF)], packed, out_keep, out_other, flops=10**8
    )
    token_grad, out_part, mine = call(
        unpack_kernel,
        [rows(D), ((8, 2, 2 * HALF), F32), ((2, D), F32)],
        exchange(packed), flops=10**8,
    )
    out_part = jnp.sum(lax.all_to_all(out_part, DP, 0, 0, tiled=True), 0)
    out_grad = out_part.reshape(2, 9, ATT).transpose(1, 0, 2).reshape(9, D)

    (qkv_grad,) = call(
        spatial_backward_kernel, [((ROWS, 3 * ATT), BF)], qkv, token_grad, factors, w_so
    )
    other = swap_cores(mine)
    factor_grad = jnp.where(core == 0, jnp.concatenate([mine, other]), jnp.concatenate([other, mine]))
    return token_grad[None, None], qkv_grad[None, None], factor_grad[None], out_grad


def solution(mesh):
    fine = Mesh(mesh.devices.reshape(4, 2, 4, 8, 2), DP + SEQ)
    frames = P(DP, SEQ, None, None)
    return jax.shard_map(
        body,
        mesh=fine,
        in_specs=(
            frames,
            frames,
            P(SEQ, None),
            P(None, SEQ),
            P(SEQ, None),
            P(DP, None, None),
            frames,
        ),
        out_specs=(frames, frames, P(DP, None, None), P(SEQ, None)),
        check_vma=False,
    )
```

```python
import math

import jax
import jax.numpy as jnp
from jax import lax
from jax.experimental import pallas as pl
from jax.experimental.pallas import tpu as pltpu
from jax.sharding import Mesh
from jax.sharding import PartitionSpec as P

D = 1152
HEADS = 8
HS = 72
ATT = 576
ROWS = 128
SCALE = 1.0 / math.sqrt(HS)
SEQ = ("yhi", "z", "core")
CHIPS = ("yhi", "z")
DP = ("x", "ylo")
BF = jnp.bfloat16
F32 = jnp.float32


def nn(a, b):
    return lax.dot_general(a, b, (((1,), (0,)), ((), ())), preferred_element_type=F32)


def nt(a, b):
    return lax.dot_general(a, b, (((1,), (1,)), ((), ())), preferred_element_type=F32)


def tn(a, b):
    return lax.dot_general(a, b, (((0,), (0,)), ((), ())), preferred_element_type=F32)


def head_masks():
    head = lax.broadcasted_iota(jnp.int32, (ROWS, ATT), 1) // HS
    return [head == h for h in range(HEADS)]


def stack_heads(masks, a):
    zero = jnp.zeros_like(a)
    return jnp.concatenate([jnp.where(m, a, zero) for m in masks], 0)


def pick_heads(masks, a):
    out = a[:ROWS]
    for h in range(1, HEADS):
        out = jnp.where(masks[h], a[h * ROWS : (h + 1) * ROWS], out)
    return out


def softmax_rows(scores):
    top = jnp.max(scores, -1, keepdims=True)
    weights = jnp.exp(scores - top)
    return weights / jnp.sum(weights, -1, keepdims=True)


def attend(masks, q, k, v, same):
    q_stack = stack_heads(masks, q)
    scores = nt(q_stack, k) * SCALE
    if same is not None:
        scores = jnp.where(same, scores, -1e30)
    probs = softmax_rows(scores)
    probs_b = probs.astype(BF)
    mixed = pick_heads(masks, nn(probs_b, v)).astype(BF)
    return q_stack, probs, probs_b, mixed


def attend_back(masks, q_stack, k, v, probs, probs_b, d_mixed):
    d_stack = stack_heads(masks, d_mixed)
    d_probs = nt(d_stack, v).astype(BF).astype(F32)
    d_v = tn(probs_b, d_stack)
    d_scores = probs * (d_probs - jnp.sum(d_probs * probs, -1, keepdims=True)) * SCALE
    d_scores = d_scores.astype(BF)
    d_q = pick_heads(masks, nn(d_scores, k))
    d_k = tn(d_scores, q_stack)
    return d_q.astype(BF), d_k.astype(BF), d_v.astype(BF)


def spatial_forward_kernel(qkv, mixed):
    q, k, v = qkv[:, :ATT], qkv[:, ATT : 2 * ATT], qkv[:, 2 * ATT :]
    mixed[...] = attend(head_masks(), q, k, v, None)[3]


def spatial_backward_kernel(qkv, hidden_grad, factors, w_so, out):
    q, k, v = qkv[:, :ATT], qkv[:, ATT : 2 * ATT], qkv[:, 2 * ATT :]
    masks = head_masks()
    gated = (hidden_grad[...].astype(F32) * factors[0:1, :]).astype(BF)
    d_mixed = nt(gated, w_so[...]).astype(BF)
    q_stack, probs, probs_b, _ = attend(masks, q, k, v, None)
    d_q, d_k, d_v = attend_back(masks, q_stack, k, v, probs, probs_b, d_mixed)
    out[:, :ATT] = d_q
    out[:, ATT : 2 * ATT] = d_k
    out[:, 2 * ATT :] = d_v


def compact_kernel(place, mine, other, own, part, both, so, out, qkv):
    core = place[0]
    both[core] = mine[...]
    both[1 - core] = other[...]
    for i in range(16):
        shard = both[i % 2, 48 * (i // 2) : 48 * (i // 2) + 48, :].astype(F32)
        so[9 * i : 9 * i + 9, :] = shard[:9]
        out[9 * i : 9 * i + 9, :] = shard[9:18]
        qkv[27 * i : 27 * i + 27, :] = shard[18:45]
    own[OWN[1] : OWN[1] + 144, :] = so[...].astype(BF)
    own[OWN[2] : OWN[2] + 144, :] = out[...].astype(BF)
    own[OWN[0] : OWN[0] + 432, :] = qkv[...].astype(BF)
    at_qkv = pl.multiple_of(core * 208, 16)
    at = pl.multiple_of(core * 64, 16)
    part[0:224, :] = own[pl.ds(OWN[0] + at_qkv, 224), :]
    part[224:304, :] = own[pl.ds(OWN[1] + at, 80), :]
    part[304:384, :] = own[pl.ds(OWN[2] + at, 80), :]


SECTIONS = ((0, 0, 224), (1, 224, 304), (2, 304, 384))
BLOCK = (432, 144, 144)
OWN = (288, 0, 144)
STEP = (208, 64, 64)


COPIES = 6


def start_copies(place, near, swapped, targets, sems):
    for me in range(2):

        @pl.when(place[0] == me)
        def _():
            for section, first, last in (SECTIONS[1], SECTIONS[0], SECTIONS[2]):
                for i, (flip, ref, other) in enumerate(zip((2, 1, 3), near, swapped)):
                    for half in range(2):
                        source = ref if half == me else other
                        skip = 16 * half
                        row = skip + STEP[section] * half
                        to = pl.multiple_of((place[1] ^ flip) * BLOCK[section] + row, 16)
                        rows = last - first - skip
                        pltpu.make_async_copy(
                            source.at[pl.ds(first + skip, rows)],
                            targets[section].at[pl.ds(to, rows)],
                            sems.at[section * COPIES + 2 * i + half],
                        ).start()


def wait_copies(section, near, targets, sems):
    first, last = SECTIONS[section][1:]
    for i in range(3):
        for half in range(2):
            rows = pl.ds(0, last - first - 16 * half)
            sem = sems.at[section * COPIES + 2 * i + half]
            pltpu.make_async_copy(near[i].at[rows], targets[section].at[rows], sem).wait()


def temporal_forward_kernel(
    place, sent, factors, own, b, c, d, other_b, other_c, other_d,
    out_keep, out_send, w_so, w_out, w_qkv, q_out, k_out, v_out, probs_out, mixed_out,
    unit_out, inverse_out, project_out, cot_out, sems,
):
    near, targets = (b, c, d), (w_qkv, w_so, w_out)
    start_copies(place, near, (other_b, other_c, other_d), targets, sems)
    for section, rows in enumerate(BLOCK):
        to = pl.multiple_of(place[1] * rows, 16)
        targets[section][pl.ds(to, rows), :] = own[OWN[section] : OWN[section] + rows, :]
    received = sent[...].reshape(ROWS, 2 * D + ATT)
    tokens, cotangent, mixed_s = received[:, :D], received[:, D : 2 * D], received[:, 2 * D :]
    cot_out[...] = cotangent
    wait_copies(1, near, targets, sems)
    gate_s, shift, scale, gate_t = (factors[i : i + 1, :] for i in range(4))
    project = nn(mixed_s, w_so[...])
    project_out[...] = project
    hidden = (tokens.astype(F32) + gate_s * project).astype(BF).astype(F32)
    centered = hidden - jnp.mean(hidden, -1, keepdims=True)
    inverse = lax.rsqrt(jnp.mean(centered * centered, -1, keepdims=True) + 1e-06)
    inverse_out[...] = jnp.broadcast_to(inverse, (ROWS, 128))
    unit = centered * inverse
    unit_out[...] = unit
    normed = (unit * (1.0 + scale) + shift).astype(BF)
    wait_copies(0, near, targets, sems)
    q, k, v = (nt(normed, w_qkv[i * ATT : (i + 1) * ATT, :]).astype(BF) for i in range(3))
    q_out[...], k_out[...], v_out[...] = q, k, v

    row = lax.broadcasted_iota(jnp.int32, (HEADS * ROWS, ROWS), 0)
    col = lax.broadcasted_iota(jnp.int32, (HEADS * ROWS, ROWS), 1)
    same = ((row ^ col) & 1) == 0
    _, probs, _, mixed = attend(head_masks(), q, k, v, same)
    probs_out[...] = probs
    mixed_out[...] = mixed

    scaled = (cotangent.astype(F32) * gate_t).astype(BF)
    source = lax.broadcasted_iota(jnp.int32, (ATT, ATT), 0)
    target = lax.broadcasted_iota(jnp.int32, (ATT, ATT), 1)
    order = jnp.where(source == (target & 63) * 9 + (target >> 6), 1.0, 0.0).astype(BF)
    ordered = nn(mixed, order).astype(BF)
    left, right = scaled[:, :ATT], scaled[:, ATT:]
    first = place[0] == 0
    keep = tn(ordered, jnp.where(first, left, right))
    send = tn(ordered, jnp.where(first, right, left)).astype(BF)
    for j in range(9):
        out_keep[:, ATT * j : ATT * j + ATT] = keep[64 * j : 64 * j + 64]
        out_send[:, ATT * j : ATT * j + ATT] = send[64 * j : 64 * j + 64]
    wait_copies(2, near, targets, sems)


def temporal_backward_kernel(
    factors, w_so, w_out, w_qkv, q, k, v, probs, mixed, unit, inverse, project, cotangent, packed
):
    scale, gate_t = factors[2:3, :], factors[3:4, :]
    cot = cotangent[...].astype(F32)
    scaled = (cot * gate_t).astype(BF)
    masks = head_masks()
    q, k, v, probs = q[...], k[...], v[...], probs[...]
    d_mixed = nt(scaled, w_out[...]).astype(BF)
    q_stack = stack_heads(masks, q)
    d_q, d_k, d_v = attend_back(masks, q_stack, k, v, probs, probs.astype(BF), d_mixed)
    wq, wk, wv = (w_qkv[i * ATT : (i + 1) * ATT, :] for i in range(3))
    d_normed = (nn(d_q, wq) + nn(d_k, wk) + nn(d_v, wv)).astype(BF).astype(F32)
    unit = unit[...]
    d_unit = d_normed * (1.0 + scale)
    d_hidden = inverse[:, 0:1] * (
        d_unit
        - jnp.mean(d_unit, -1, keepdims=True)
        - unit * jnp.mean(d_unit * unit, -1, keepdims=True)
    )
    grad = (cot + d_hidden).astype(BF)
    packed[:, :D] = grad
    project_t = nn(mixed[...], w_out[...])
    factor_grads = (
        jnp.sum(grad.astype(F32) * project[...], 0, keepdims=True),
        jnp.sum(d_normed, 0, keepdims=True),
        jnp.sum(d_normed * unit, 0, keepdims=True),
        jnp.sum(cot * project_t, 0, keepdims=True),
    )
    tile = jnp.concatenate(factor_grads * 4, 0).astype(BF)
    for i in range(8):
        packed[16 * i : 16 * i + 16, D:] = tile


HALF = 9 * ATT // 2


def pack_kernel(packed, out_keep, out_other, out):
    out[:, :, : 2 * D] = packed[...].reshape(64, 2, 2 * D)
    pair = (out_keep[...] + out_other[...].astype(F32)).astype(BF)
    out[:, 0, 2 * D :] = pair[:, :HALF]
    out[:, 1, 2 * D :] = pair[:, HALF:]


def unpack_kernel(back, token_grad, out_part, factor_part):
    token_grad[...] = back[:, :, :D].reshape(ROWS, D)
    first = lax.broadcasted_iota(jnp.int32, (64, HALF), 0) & 1 == 0
    for r in range(2):
        factor_part[r : r + 1, :] = jnp.sum(back[:, r, D : 2 * D].astype(F32), 0, keepdims=True)
        rows = back[:, r, 2 * D :].astype(F32)
        for core in range(2):
            total = jnp.sum(jnp.where(first == (core == 0), rows, 0.0), 0, keepdims=True)
            for copy in range(8):
                out_part[copy, core : core + 1, HALF * r : HALF * r + HALF] = total


def call(kernel, outs, *args, scalars=0, hbm=0, scratch=(), flops=10**9):
    vmem = pl.BlockSpec(memory_space=pltpu.VMEM)
    specs = [pl.BlockSpec(memory_space=pltpu.SMEM)] * scalars
    specs += [vmem] * (len(args) - scalars - hbm) + [pl.BlockSpec(memory_space=pltpu.HBM)] * hbm
    return pl.pallas_call(
        kernel,
        out_shape=[jax.ShapeDtypeStruct(s, d) for s, d in outs],
        in_specs=specs,
        out_specs=[vmem] * len(outs),
        scratch_shapes=list(scratch),
        compiler_params=pltpu.CompilerParams(vmem_limit_bytes=32 * 2**20),
        cost_estimate=pl.CostEstimate(flops=flops, bytes_accessed=10**7, transcendentals=10**5),
    )(*args)


def exchange(a):
    return lax.all_to_all(a, SEQ, 0, 0, tiled=True)


AXES = DP + SEQ


def device(x, y, z, core):
    ylo, yhi = y % 2, (y % 8) // 2
    return ((((x % 4) * 2 + ylo) * 4 + yhi) * 8 + z % 8) * 2 + core


def receive(a, source):
    pairs = []
    for x in range(4):
        for y in range(8):
            for z in range(8):
                for core in range(2):
                    pairs.append((device(*source(x, y, z, core), core), device(x, y, z, core)))
    return lax.ppermute(a, AXES, pairs)


def swap_cores(a):
    return lax.ppermute(a, "core", [(0, 1), (1, 0)])


def class_source(x, y, z, core):
    ylo, yhi = y % 2, y // 2
    cls = (x % 2) * 2 + ylo
    return (x // 2) * 2 + yhi // 2, cls * 2 + yhi % 2, z


def near_source(dx, dy):
    def source(x, y, z, core):
        sign = 1 - 2 * core
        return x + sign * dx, y + sign * dy, z

    return source


def gather_weights(w_so, w_qkv, w_out, place, sent):
    shard = jnp.concatenate([w_so, w_out, w_qkv.T, jnp.zeros((3, D), BF)], 0)
    shard, sent = lax.optimization_barrier((receive(shard, class_source), sent))
    mine = lax.all_gather(shard, "z", axis=0, tiled=True)
    other = swap_cores(mine)
    rows = lambda n: ((n, D), BF)
    own, part = call(
        compact_kernel, [rows(720), rows(384)], place, mine, other, scalars=1,
        scratch=[
            pltpu.VMEM((2, 384, D), BF),
            pltpu.VMEM((144, D), F32),
            pltpu.VMEM((144, D), F32),
            pltpu.VMEM((432, D), F32),
        ],
    )
    part, sent = lax.optimization_barrier((part, sent))
    near = [receive(part, near_source(dx, dy)) for dx, dy in ((1, 0), (0, 1), (1, 1))]
    sent = exchange(sent)
    return [own] + near + [swap_cores(a) for a in near], sent


def body(tokens, qkv, w_so, w_qkv, w_out, factors, cotangent):
    tokens, qkv, cotangent, factors = tokens[0, 0], qkv[0, 0], cotangent[0, 0], factors[0]
    core = lax.axis_index("core")
    cls = (lax.axis_index("x") % 2) * 2 + lax.axis_index("ylo")
    place = jnp.stack([core, cls]).astype(jnp.int32)

    (mixed_s,) = call(spatial_forward_kernel, [((ROWS, ATT), BF)], qkv)
    sent = jnp.concatenate([tokens, cotangent, mixed_s], 1).reshape(64, 2, 2 * D + ATT)
    weights, sent = gather_weights(w_so, w_qkv, w_out, place, sent)

    rows = lambda n, kind=BF: ((ROWS, n), kind)
    out_keep, out_send, *saved = call(
        temporal_forward_kernel,
        [
            ((64, 2 * HALF), F32), ((64, 2 * HALF), BF),
            ((ATT, D), BF), ((ATT, D), BF), ((3 * ATT, D), BF),
            rows(ATT), rows(ATT), rows(ATT), ((HEADS * ROWS, ROWS), F32), rows(ATT),
            rows(D, F32), rows(128, F32), rows(D, F32), rows(D),
        ],
        place, sent, factors, *weights,
        scalars=1, hbm=6, flops=4 * 10**9,
        scratch=[pltpu.SemaphoreType.DMA((3 * COPIES,))],
    )
    w_so = saved[0]
    out_other = swap_cores(out_send)
    (packed,) = call(temporal_backward_kernel, [rows(2 * D)], factors, *saved, flops=4 * 10**9)

    (packed,) = call(
        pack_kernel, [((64, 2, 2 * D + HALF), BF)], packed, out_keep, out_other, flops=10**8
    )
    token_grad, out_part, mine = call(
        unpack_kernel,
        [rows(D), ((8, 2, 2 * HALF), F32), ((2, D), F32)],
        exchange(packed), flops=10**8,
    )
    out_part = jnp.sum(lax.all_to_all(out_part, DP, 0, 0, tiled=True), 0)
    out_grad = out_part.reshape(2, 9, ATT).transpose(1, 0, 2).reshape(9, D)

    (qkv_grad,) = call(
        spatial_backward_kernel, [((ROWS, 3 * ATT), BF)], qkv, token_grad, factors, w_so
    )
    other = swap_cores(mine)
    factor_grad = jnp.where(core == 0, jnp.concatenate([mine, other]), jnp.concatenate([other, mine]))
    return token_grad[None, None], qkv_grad[None, None], factor_grad[None], out_grad


def solution(mesh):
    fine = Mesh(mesh.devices.reshape(4, 2, 4, 8, 2), DP + SEQ)
    frames = P(DP, SEQ, None, None)
    return jax.shard_map(
        body,
        mesh=fine,
        in_specs=(
            frames,
            frames,
            P(SEQ, None),
            P(None, SEQ),
            P(SEQ, None),
            P(DP, None, None),
            frames,
        ),
        out_specs=(frames, frames, P(DP, None, None), P(SEQ, None)),
        check_vma=False,
    )
```

```python
import math

import jax
import jax.numpy as jnp
from jax import lax
from jax.experimental import pallas as pl
from jax.experimental.pallas import tpu as pltpu
from jax.sharding import Mesh
from jax.sharding import PartitionSpec as P

D = 1152
HEADS = 8
HS = 72
ATT = 576
ROWS = 128
SCALE = 1.0 / math.sqrt(HS)
SEQ = ("yhi", "z", "core")
CHIPS = ("yhi", "z")
DP = ("x", "ylo")
BF = jnp.bfloat16
F32 = jnp.float32


def nn(a, b):
    return lax.dot_general(a, b, (((1,), (0,)), ((), ())), preferred_element_type=F32)


def nt(a, b):
    return lax.dot_general(a, b, (((1,), (1,)), ((), ())), preferred_element_type=F32)


def tn(a, b):
    return lax.dot_general(a, b, (((0,), (0,)), ((), ())), preferred_element_type=F32)


def head_masks():
    head = lax.broadcasted_iota(jnp.int32, (ROWS, ATT), 1) // HS
    return [head == h for h in range(HEADS)]


def stack_heads(masks, a):
    zero = jnp.zeros_like(a)
    return jnp.concatenate([jnp.where(m, a, zero) for m in masks], 0)


def pick_heads(masks, a):
    out = a[:ROWS]
    for h in range(1, HEADS):
        out = jnp.where(masks[h], a[h * ROWS : (h + 1) * ROWS], out)
    return out


def softmax_rows(scores):
    top = jnp.max(scores, -1, keepdims=True)
    weights = jnp.exp(scores - top)
    return weights / jnp.sum(weights, -1, keepdims=True)


def attend(masks, q, k, v, same):
    q_stack = stack_heads(masks, q)
    scores = nt(q_stack, k) * SCALE
    if same is not None:
        scores = jnp.where(same, scores, -1e30)
    probs = softmax_rows(scores)
    probs_b = probs.astype(BF)
    mixed = pick_heads(masks, nn(probs_b, v)).astype(BF)
    return q_stack, probs, probs_b, mixed


def attend_back(masks, q_stack, k, v, probs, probs_b, d_mixed):
    d_stack = stack_heads(masks, d_mixed)
    d_probs = nt(d_stack, v).astype(BF).astype(F32)
    d_v = tn(probs_b, d_stack)
    d_scores = probs * (d_probs - jnp.sum(d_probs * probs, -1, keepdims=True)) * SCALE
    d_scores = d_scores.astype(BF)
    d_q = pick_heads(masks, nn(d_scores, k))
    d_k = tn(d_scores, q_stack)
    return d_q.astype(BF), d_k.astype(BF), d_v.astype(BF)


def spatial_forward_kernel(qkv, mixed):
    q, k, v = qkv[:, :ATT], qkv[:, ATT : 2 * ATT], qkv[:, 2 * ATT :]
    mixed[...] = attend(head_masks(), q, k, v, None)[3]


def spatial_backward_kernel(qkv, hidden_grad, factors, w_so, out):
    q, k, v = qkv[:, :ATT], qkv[:, ATT : 2 * ATT], qkv[:, 2 * ATT :]
    masks = head_masks()
    gated = (hidden_grad[...].astype(F32) * factors[0:1, :]).astype(BF)
    d_mixed = nt(gated, w_so[...]).astype(BF)
    q_stack, probs, probs_b, _ = attend(masks, q, k, v, None)
    d_q, d_k, d_v = attend_back(masks, q_stack, k, v, probs, probs_b, d_mixed)
    out[:, :ATT] = d_q
    out[:, ATT : 2 * ATT] = d_k
    out[:, 2 * ATT :] = d_v


def compact_kernel(place, mine, other, own, part, both, so, out, qkv):
    core = place[0]
    both[core] = mine[...]
    both[1 - core] = other[...]
    for i in range(16):
        shard = both[i % 2, 48 * (i // 2) : 48 * (i // 2) + 48, :].astype(F32)
        so[9 * i : 9 * i + 9, :] = shard[:9]
        out[9 * i : 9 * i + 9, :] = shard[9:18]
        qkv[27 * i : 27 * i + 27, :] = shard[18:45]
    own[OWN[1] : OWN[1] + 144, :] = so[...].astype(BF)
    own[OWN[2] : OWN[2] + 144, :] = out[...].astype(BF)
    own[OWN[0] : OWN[0] + 432, :] = qkv[...].astype(BF)
    at_qkv = pl.multiple_of(core * 208, 16)
    at = pl.multiple_of(core * 64, 16)
    part[0:224, :] = own[pl.ds(OWN[0] + at_qkv, 224), :]
    part[224:304, :] = own[pl.ds(OWN[1] + at, 80), :]
    part[304:384, :] = own[pl.ds(OWN[2] + at, 80), :]


SECTIONS = ((0, 0, 224), (1, 224, 304), (2, 304, 384))
BLOCK = (432, 144, 144)
OWN = (288, 0, 144)
STEP = (208, 64, 64)


COPIES = 6


def start_copies(place, near, swapped, targets, sems):
    for me in range(2):

        @pl.when(place[0] == me)
        def _():
            for section, first, last in (SECTIONS[1], SECTIONS[0], SECTIONS[2]):
                for i, (flip, ref, other) in enumerate(zip((2, 1, 3), near, swapped)):
                    for half in range(2):
                        source = ref if half == me else other
                        skip = 16 * half
                        row = skip + STEP[section] * half
                        to = pl.multiple_of((place[1] ^ flip) * BLOCK[section] + row, 16)
                        rows = last - first - skip
                        pltpu.make_async_copy(
                            source.at[pl.ds(first + skip, rows)],
                            targets[section].at[pl.ds(to, rows)],
                            sems.at[section * COPIES + 2 * i + half],
                        ).start()


def wait_copies(section, near, targets, sems):
    first, last = SECTIONS[section][1:]
    for i in range(3):
        for half in range(2):
            rows = pl.ds(0, last - first - 16 * half)
            sem = sems.at[section * COPIES + 2 * i + half]
            pltpu.make_async_copy(near[i].at[rows], targets[section].at[rows], sem).wait()


def temporal_forward_kernel(
    place, sent, factors, own, b, c, d, other_b, other_c, other_d,
    out_keep, out_send, w_so, w_out, w_qkv, q_out, k_out, v_out, probs_out, mixed_out,
    unit_out, inverse_out, project_out, cot_out, sems,
):
    near, targets = (b, c, d), (w_qkv, w_so, w_out)
    start_copies(place, near, (other_b, other_c, other_d), targets, sems)
    for section, rows in enumerate(BLOCK):
        to = pl.multiple_of(place[1] * rows, 16)
        targets[section][pl.ds(to, rows), :] = own[OWN[section] : OWN[section] + rows, :]
    received = sent[...].reshape(ROWS, 2 * D + ATT)
    tokens, cotangent, mixed_s = received[:, :D], received[:, D : 2 * D], received[:, 2 * D :]
    cot_out[...] = cotangent
    wait_copies(1, near, targets, sems)
    gate_s, shift, scale, gate_t = (factors[i : i + 1, :] for i in range(4))
    project = nn(mixed_s, w_so[...])
    project_out[...] = project
    hidden = (tokens.astype(F32) + gate_s * project).astype(BF).astype(F32)
    centered = hidden - jnp.mean(hidden, -1, keepdims=True)
    inverse = lax.rsqrt(jnp.mean(centered * centered, -1, keepdims=True) + 1e-06)
    inverse_out[...] = jnp.broadcast_to(inverse, (ROWS, 128))
    unit = centered * inverse
    unit_out[...] = unit
    normed = (unit * (1.0 + scale) + shift).astype(BF)
    wait_copies(0, near, targets, sems)
    q, k, v = (nt(normed, w_qkv[i * ATT : (i + 1) * ATT, :]).astype(BF) for i in range(3))
    q_out[...], k_out[...], v_out[...] = q, k, v

    row = lax.broadcasted_iota(jnp.int32, (HEADS * ROWS, ROWS), 0)
    col = lax.broadcasted_iota(jnp.int32, (HEADS * ROWS, ROWS), 1)
    same = ((row ^ col) & 1) == 0
    _, probs, _, mixed = attend(head_masks(), q, k, v, same)
    probs_out[...] = probs
    mixed_out[...] = mixed

    scaled = (cotangent.astype(F32) * gate_t).astype(BF)
    source = lax.broadcasted_iota(jnp.int32, (ATT, ATT), 0)
    target = lax.broadcasted_iota(jnp.int32, (ATT, ATT), 1)
    order = jnp.where(source == (target & 63) * 9 + (target >> 6), 1.0, 0.0).astype(BF)
    ordered = nn(mixed, order).astype(BF)
    left, right = scaled[:, :ATT], scaled[:, ATT:]
    first = place[0] == 0
    keep = tn(ordered, jnp.where(first, left, right))
    send = tn(ordered, jnp.where(first, right, left)).astype(BF)
    for j in range(9):
        out_keep[:, ATT * j : ATT * j + ATT] = keep[64 * j : 64 * j + 64]
        out_send[:, ATT * j : ATT * j + ATT] = send[64 * j : 64 * j + 64]
    wait_copies(2, near, targets, sems)


def temporal_backward_kernel(
    factors, w_so, w_out, w_qkv, q, k, v, probs, mixed, unit, inverse, project, cotangent, packed
):
    scale, gate_t = factors[2:3, :], factors[3:4, :]
    cot = cotangent[...].astype(F32)
    scaled = (cot * gate_t).astype(BF)
    masks = head_masks()
    q, k, v, probs = q[...], k[...], v[...], probs[...]
    d_mixed = nt(scaled, w_out[...]).astype(BF)
    q_stack = stack_heads(masks, q)
    d_q, d_k, d_v = attend_back(masks, q_stack, k, v, probs, probs.astype(BF), d_mixed)
    wq, wk, wv = (w_qkv[i * ATT : (i + 1) * ATT, :] for i in range(3))
    d_normed = (nn(d_q, wq) + nn(d_k, wk) + nn(d_v, wv)).astype(BF).astype(F32)
    unit = unit[...]
    d_unit = d_normed * (1.0 + scale)
    d_hidden = inverse[:, 0:1] * (
        d_unit
        - jnp.mean(d_unit, -1, keepdims=True)
        - unit * jnp.mean(d_unit * unit, -1, keepdims=True)
    )
    grad = (cot + d_hidden).astype(BF)
    packed[:, :D] = grad
    project_t = nn(mixed[...], w_out[...])
    factor_grads = (
        jnp.sum(grad.astype(F32) * project[...], 0, keepdims=True),
        jnp.sum(d_normed, 0, keepdims=True),
        jnp.sum(d_normed * unit, 0, keepdims=True),
        jnp.sum(cot * project_t, 0, keepdims=True),
    )
    tile = jnp.concatenate(factor_grads * 4, 0).astype(BF)
    for i in range(8):
        packed[16 * i : 16 * i + 16, D:] = tile


HALF = 9 * ATT // 2


def pack_kernel(packed, out_keep, out_other, out):
    out[:, :, : 2 * D] = packed[...].reshape(64, 2, 2 * D)
    pair = (out_keep[...] + out_other[...].astype(F32)).astype(BF)
    out[:, 0, 2 * D :] = pair[:, :HALF]
    out[:, 1, 2 * D :] = pair[:, HALF:]


def unpack_kernel(back, token_grad, out_part, factor_part):
    token_grad[...] = back[:, :, :D].reshape(ROWS, D)
    first = lax.broadcasted_iota(jnp.int32, (64, HALF), 0) & 1 == 0
    for r in range(2):
        factor_part[r : r + 1, :] = jnp.sum(back[:, r, D : 2 * D].astype(F32), 0, keepdims=True)
        rows = back[:, r, 2 * D :].astype(F32)
        for core in range(2):
            total = jnp.sum(jnp.where(first == (core == 0), rows, 0.0), 0, keepdims=True)
            for copy in range(8):
                out_part[copy, core : core + 1, HALF * r : HALF * r + HALF] = total


def call(kernel, outs, *args, scalars=0, hbm=0, scratch=(), flops=10**9):
    vmem = pl.BlockSpec(memory_space=pltpu.VMEM)
    specs = [pl.BlockSpec(memory_space=pltpu.SMEM)] * scalars
    specs += [vmem] * (len(args) - scalars - hbm) + [pl.BlockSpec(memory_space=pltpu.HBM)] * hbm
    return pl.pallas_call(
        kernel,
        out_shape=[jax.ShapeDtypeStruct(s, d) for s, d in outs],
        in_specs=specs,
        out_specs=[vmem] * len(outs),
        scratch_shapes=list(scratch),
        compiler_params=pltpu.CompilerParams(vmem_limit_bytes=32 * 2**20),
        cost_estimate=pl.CostEstimate(flops=flops, bytes_accessed=10**7, transcendentals=10**5),
    )(*args)


def exchange(a):
    return lax.all_to_all(a, SEQ, 0, 0, tiled=True)


AXES = DP + SEQ


def device(x, y, z, core):
    ylo, yhi = y % 2, (y % 8) // 2
    return ((((x % 4) * 2 + ylo) * 4 + yhi) * 8 + z % 8) * 2 + core


def receive(a, source):
    pairs = []
    for x in range(4):
        for y in range(8):
            for z in range(8):
                for core in range(2):
                    pairs.append((device(*source(x, y, z, core), core), device(x, y, z, core)))
    return lax.ppermute(a, AXES, pairs)


def swap_cores(a):
    return lax.ppermute(a, "core", [(0, 1), (1, 0)])


SENDERS = (
    ((0, 0), (1, 2), (0, 1), (3, 3), (1, 1), (0, 3), (3, 0), (0, 2)),
    ((0, 5), (1, 7), (0, 4), (1, 6), (1, 4), (2, 6), (1, 5), (2, 7)),
    ((1, 0), (2, 2), (3, 1), (1, 3), (2, 1), (2, 3), (2, 0), (3, 2)),
    ((3, 5), (0, 7), (2, 4), (0, 6), (3, 4), (3, 6), (2, 5), (3, 7)),
)


def class_source(x, y, z, core):
    return *SENDERS[x][y], z


def near_source(dx, dy):
    def source(x, y, z, core):
        sign = 1 - 2 * core
        return x + sign * dx, y + sign * dy, z

    return source


def gather_weights(w_so, w_qkv, w_out, place, sent):
    shard = jnp.concatenate([w_so, w_out, w_qkv.T, jnp.zeros((3, D), BF)], 0)
    shard, sent = lax.optimization_barrier((receive(shard, class_source), sent))
    mine = lax.all_gather(shard, "z", axis=0, tiled=True)
    other = swap_cores(mine)
    rows = lambda n: ((n, D), BF)
    own, part = call(
        compact_kernel, [rows(720), rows(384)], place, mine, other, scalars=1,
        scratch=[
            pltpu.VMEM((2, 384, D), BF),
            pltpu.VMEM((144, D), F32),
            pltpu.VMEM((144, D), F32),
            pltpu.VMEM((432, D), F32),
        ],
    )
    part, sent = lax.optimization_barrier((part, sent))
    near = [receive(part, near_source(dx, dy)) for dx, dy in ((1, 0), (0, 1), (1, 1))]
    sent = exchange(sent)
    return [own] + near + [swap_cores(a) for a in near], sent


def body(tokens, qkv, w_so, w_qkv, w_out, factors, cotangent):
    tokens, qkv, cotangent, factors = tokens[0, 0], qkv[0, 0], cotangent[0, 0], factors[0]
    core = lax.axis_index("core")
    cls = (lax.axis_index("x") % 2) * 2 + lax.axis_index("ylo")
    place = jnp.stack([core, cls]).astype(jnp.int32)

    (mixed_s,) = call(spatial_forward_kernel, [((ROWS, ATT), BF)], qkv)
    sent = jnp.concatenate([tokens, cotangent, mixed_s], 1).reshape(64, 2, 2 * D + ATT)
    weights, sent = gather_weights(w_so, w_qkv, w_out, place, sent)

    rows = lambda n, kind=BF: ((ROWS, n), kind)
    out_keep, out_send, *saved = call(
        temporal_forward_kernel,
        [
            ((64, 2 * HALF), F32), ((64, 2 * HALF), BF),
            ((ATT, D), BF), ((ATT, D), BF), ((3 * ATT, D), BF),
            rows(ATT), rows(ATT), rows(ATT), ((HEADS * ROWS, ROWS), F32), rows(ATT),
            rows(D, F32), rows(128, F32), rows(D, F32), rows(D),
        ],
        place, sent, factors, *weights,
        scalars=1, hbm=6, flops=4 * 10**9,
        scratch=[pltpu.SemaphoreType.DMA((3 * COPIES,))],
    )
    w_so = saved[0]
    out_other = swap_cores(out_send)
    (packed,) = call(temporal_backward_kernel, [rows(2 * D)], factors, *saved, flops=4 * 10**9)

    (packed,) = call(
        pack_kernel, [((64, 2, 2 * D + HALF), BF)], packed, out_keep, out_other, flops=10**8
    )
    token_grad, out_part, mine = call(
        unpack_kernel,
        [rows(D), ((8, 2, 2 * HALF), F32), ((2, D), F32)],
        exchange(packed), flops=10**8,
    )
    out_part = jnp.sum(lax.all_to_all(out_part, DP, 0, 0, tiled=True), 0)
    out_grad = out_part.reshape(2, 9, ATT).transpose(1, 0, 2).reshape(9, D)

    (qkv_grad,) = call(
        spatial_backward_kernel, [((ROWS, 3 * ATT), BF)], qkv, token_grad, factors, w_so
    )
    other = swap_cores(mine)
    factor_grad = jnp.where(core == 0, jnp.concatenate([mine, other]), jnp.concatenate([other, mine]))
    return token_grad[None, None], qkv_grad[None, None], factor_grad[None], out_grad


def solution(mesh):
    fine = Mesh(mesh.devices.reshape(4, 2, 4, 8, 2), DP + SEQ)
    frames = P(DP, SEQ, None, None)
    return jax.shard_map(
        body,
        mesh=fine,
        in_specs=(
            frames,
            frames,
            P(SEQ, None),
            P(None, SEQ),
            P(SEQ, None),
            P(DP, None, None),
            frames,
        ),
        out_specs=(frames, frames, P(DP, None, None), P(SEQ, None)),
        check_vma=False,
    )
```

```python
import math

import jax
import jax.numpy as jnp
from jax import lax
from jax.experimental import pallas as pl
from jax.experimental.pallas import tpu as pltpu
from jax.sharding import Mesh
from jax.sharding import PartitionSpec as P

D = 1152
HEADS = 8
HS = 72
ATT = 576
ROWS = 128
SCALE = 1.0 / math.sqrt(HS)
SEQ = ("yhi", "z", "core")
CHIPS = ("yhi", "z")
DP = ("x", "ylo")
BF = jnp.bfloat16
F32 = jnp.float32


def nn(a, b):
    return lax.dot_general(a, b, (((1,), (0,)), ((), ())), preferred_element_type=F32)


def nt(a, b):
    return lax.dot_general(a, b, (((1,), (1,)), ((), ())), preferred_element_type=F32)


def tn(a, b):
    return lax.dot_general(a, b, (((0,), (0,)), ((), ())), preferred_element_type=F32)


def head_masks():
    head = lax.broadcasted_iota(jnp.int32, (ROWS, ATT), 1) // HS
    return [head == h for h in range(HEADS)]


def stack_heads(masks, a):
    zero = jnp.zeros_like(a)
    return jnp.concatenate([jnp.where(m, a, zero) for m in masks], 0)


def pick_heads(masks, a):
    out = a[:ROWS]
    for h in range(1, HEADS):
        out = jnp.where(masks[h], a[h * ROWS : (h + 1) * ROWS], out)
    return out


def softmax_rows(scores):
    top = jnp.max(scores, -1, keepdims=True)
    weights = jnp.exp(scores - top)
    return weights / jnp.sum(weights, -1, keepdims=True)


def attend(masks, q, k, v, same):
    q_stack = stack_heads(masks, q)
    scores = nt(q_stack, k) * SCALE
    if same is not None:
        scores = jnp.where(same, scores, -1e30)
    probs = softmax_rows(scores)
    probs_b = probs.astype(BF)
    mixed = pick_heads(masks, nn(probs_b, v)).astype(BF)
    return q_stack, probs, probs_b, mixed


def attend_back(masks, q_stack, k, v, probs, probs_b, d_mixed):
    d_stack = stack_heads(masks, d_mixed)
    d_probs = nt(d_stack, v).astype(BF).astype(F32)
    d_v = tn(probs_b, d_stack)
    d_scores = probs * (d_probs - jnp.sum(d_probs * probs, -1, keepdims=True)) * SCALE
    d_scores = d_scores.astype(BF)
    d_q = pick_heads(masks, nn(d_scores, k))
    d_k = tn(d_scores, q_stack)
    return d_q.astype(BF), d_k.astype(BF), d_v.astype(BF)


def spatial_forward_kernel(qkv, mixed):
    q, k, v = qkv[:, :ATT], qkv[:, ATT : 2 * ATT], qkv[:, 2 * ATT :]
    mixed[...] = attend(head_masks(), q, k, v, None)[3]


def spatial_backward_kernel(qkv, hidden_grad, factors, w_so, out):
    q, k, v = qkv[:, :ATT], qkv[:, ATT : 2 * ATT], qkv[:, 2 * ATT :]
    masks = head_masks()
    gated = (hidden_grad[...].astype(F32) * factors[0:1, :]).astype(BF)
    d_mixed = nt(gated, w_so[...]).astype(BF)
    q_stack, probs, probs_b, _ = attend(masks, q, k, v, None)
    d_q, d_k, d_v = attend_back(masks, q_stack, k, v, probs, probs_b, d_mixed)
    out[:, :ATT] = d_q
    out[:, ATT : 2 * ATT] = d_k
    out[:, 2 * ATT :] = d_v


def compact_kernel(place, mine, other, own_so, own_out, own_qkv, part, both, so, out, qkv):
    core = place[0]
    both[core] = mine[...]
    both[1 - core] = other[...]
    for i in range(16):
        shard = both[i % 2, 48 * (i // 2) : 48 * (i // 2) + 48, :].astype(F32)
        so[9 * i : 9 * i + 9, :] = shard[:9]
        out[9 * i : 9 * i + 9, :] = shard[9:18]
        qkv[27 * i : 27 * i + 27, :] = shard[18:45]
    own_so[...] = so[...].astype(BF)
    own_out[...] = out[...].astype(BF)
    own_qkv[...] = qkv[...].astype(BF)
    at_qkv = pl.multiple_of(core * 208, 16)
    at = pl.multiple_of(core * 64, 16)
    part[0:224, :] = own_qkv[pl.ds(at_qkv, 224), :]
    part[224:304, :] = own_so[pl.ds(at, 80), :]
    part[304:384, :] = own_out[pl.ds(at, 80), :]


SECTIONS = ((0, 0, 224), (1, 224, 304), (2, 304, 384))
BLOCK = (432, 144, 144)
STEP = (208, 64, 64)


COPIES = 6


def start_copies(place, near, swapped, targets, sems):
    for me in range(2):

        @pl.when(place[0] == me)
        def _():
            for section, first, last in (SECTIONS[1], SECTIONS[0], SECTIONS[2]):
                for i, (flip, ref, other) in enumerate(zip((2, 1, 3), near, swapped)):
                    for half in range(2):
                        source = ref if half == me else other
                        skip = 16 * half
                        row = skip + STEP[section] * half
                        to = pl.multiple_of((place[1] ^ flip) * BLOCK[section] + row, 16)
                        rows = last - first - skip
                        pltpu.make_async_copy(
                            source.at[pl.ds(first + skip, rows)],
                            targets[section].at[pl.ds(to, rows)],
                            sems.at[section * COPIES + 2 * i + half],
                        ).start()


def wait_copies(section, near, targets, sems):
    first, last = SECTIONS[section][1:]
    for i in range(3):
        for half in range(2):
            rows = pl.ds(0, last - first - 16 * half)
            sem = sems.at[section * COPIES + 2 * i + half]
            pltpu.make_async_copy(near[i].at[rows], targets[section].at[rows], sem).wait()


def temporal_forward_kernel(
    place, sent, factors, own_qkv, own_so, own_out, b, c, d, other_b, other_c, other_d,
    out_keep, out_send, w_so, w_out, w_qkv, q_out, k_out, v_out, probs_out, mixed_out,
    unit_out, inverse_out, project_out, cot_out, sems,
):
    near, targets = (b, c, d), (w_qkv, w_so, w_out)
    start_copies(place, near, (other_b, other_c, other_d), targets, sems)
    for section, ref in enumerate((own_qkv, own_so, own_out)):
        to = pl.multiple_of(place[1] * BLOCK[section], 16)
        targets[section][pl.ds(to, BLOCK[section]), :] = ref[...]
    received = sent[...].reshape(ROWS, 2 * D + ATT)
    tokens, cotangent, mixed_s = received[:, :D], received[:, D : 2 * D], received[:, 2 * D :]
    cot_out[...] = cotangent
    wait_copies(1, near, targets, sems)
    gate_s, shift, scale, gate_t = (factors[i : i + 1, :] for i in range(4))
    project = nn(mixed_s, w_so[...])
    project_out[...] = project
    hidden = (tokens.astype(F32) + gate_s * project).astype(BF).astype(F32)
    centered = hidden - jnp.mean(hidden, -1, keepdims=True)
    inverse = lax.rsqrt(jnp.mean(centered * centered, -1, keepdims=True) + 1e-06)
    inverse_out[...] = jnp.broadcast_to(inverse, (ROWS, 128))
    unit = centered * inverse
    unit_out[...] = unit
    normed = (unit * (1.0 + scale) + shift).astype(BF)
    wait_copies(0, near, targets, sems)
    q, k, v = (nt(normed, w_qkv[i * ATT : (i + 1) * ATT, :]).astype(BF) for i in range(3))
    q_out[...], k_out[...], v_out[...] = q, k, v

    row = lax.broadcasted_iota(jnp.int32, (HEADS * ROWS, ROWS), 0)
    col = lax.broadcasted_iota(jnp.int32, (HEADS * ROWS, ROWS), 1)
    same = ((row ^ col) & 1) == 0
    _, probs, _, mixed = attend(head_masks(), q, k, v, same)
    probs_out[...] = probs
    mixed_out[...] = mixed

    scaled = (cotangent.astype(F32) * gate_t).astype(BF)
    source = lax.broadcasted_iota(jnp.int32, (ATT, ATT), 0)
    target = lax.broadcasted_iota(jnp.int32, (ATT, ATT), 1)
    order = jnp.where(source == (target & 63) * 9 + (target >> 6), 1.0, 0.0).astype(BF)
    ordered = nn(mixed, order).astype(BF)
    left, right = scaled[:, :ATT], scaled[:, ATT:]
    first = place[0] == 0
    keep = tn(ordered, jnp.where(first, left, right))
    send = tn(ordered, jnp.where(first, right, left)).astype(BF)
    for j in range(9):
        out_keep[:, ATT * j : ATT * j + ATT] = keep[64 * j : 64 * j + 64]
        out_send[:, ATT * j : ATT * j + ATT] = send[64 * j : 64 * j + 64]
    wait_copies(2, near, targets, sems)


def temporal_backward_kernel(
    factors, w_so, w_out, w_qkv, q, k, v, probs, mixed, unit, inverse, project, cotangent, packed
):
    scale, gate_t = factors[2:3, :], factors[3:4, :]
    cot = cotangent[...].astype(F32)
    scaled = (cot * gate_t).astype(BF)
    masks = head_masks()
    q, k, v, probs = q[...], k[...], v[...], probs[...]
    d_mixed = nt(scaled, w_out[...]).astype(BF)
    q_stack = stack_heads(masks, q)
    d_q, d_k, d_v = attend_back(masks, q_stack, k, v, probs, probs.astype(BF), d_mixed)
    wq, wk, wv = (w_qkv[i * ATT : (i + 1) * ATT, :] for i in range(3))
    d_normed = (nn(d_q, wq) + nn(d_k, wk) + nn(d_v, wv)).astype(BF).astype(F32)
    unit = unit[...]
    d_unit = d_normed * (1.0 + scale)
    d_hidden = inverse[:, 0:1] * (
        d_unit
        - jnp.mean(d_unit, -1, keepdims=True)
        - unit * jnp.mean(d_unit * unit, -1, keepdims=True)
    )
    grad = (cot + d_hidden).astype(BF)
    packed[:, :D] = grad
    project_t = nn(mixed[...], w_out[...])
    factor_grads = (
        jnp.sum(grad.astype(F32) * project[...], 0, keepdims=True),
        jnp.sum(d_normed, 0, keepdims=True),
        jnp.sum(d_normed * unit, 0, keepdims=True),
        jnp.sum(cot * project_t, 0, keepdims=True),
    )
    tile = jnp.concatenate(factor_grads * 4, 0).astype(BF)
    for i in range(8):
        packed[16 * i : 16 * i + 16, D:] = tile


HALF = 9 * ATT // 2


def pack_kernel(packed, out_keep, out_other, out):
    out[:, :, : 2 * D] = packed[...].reshape(64, 2, 2 * D)
    pair = (out_keep[...] + out_other[...].astype(F32)).astype(BF)
    out[:, 0, 2 * D :] = pair[:, :HALF]
    out[:, 1, 2 * D :] = pair[:, HALF:]


def unpack_kernel(back, token_grad, out_part, factor_part):
    token_grad[...] = back[:, :, :D].reshape(ROWS, D)
    first = lax.broadcasted_iota(jnp.int32, (64, HALF), 0) & 1 == 0
    for r in range(2):
        factor_part[r : r + 1, :] = jnp.sum(back[:, r, D : 2 * D].astype(F32), 0, keepdims=True)
        rows = back[:, r, 2 * D :].astype(F32)
        for core in range(2):
            total = jnp.sum(jnp.where(first == (core == 0), rows, 0.0), 0, keepdims=True)
            for copy in range(8):
                out_part[copy, core : core + 1, HALF * r : HALF * r + HALF] = total.astype(BF)


def call(kernel, outs, *args, scalars=0, hbm=0, scratch=(), flops=10**9):
    vmem = pl.BlockSpec(memory_space=pltpu.VMEM)
    specs = [pl.BlockSpec(memory_space=pltpu.SMEM)] * scalars
    specs += [vmem] * (len(args) - scalars - hbm) + [pl.BlockSpec(memory_space=pltpu.HBM)] * hbm
    return pl.pallas_call(
        kernel,
        out_shape=[jax.ShapeDtypeStruct(s, d) for s, d in outs],
        in_specs=specs,
        out_specs=[vmem] * len(outs),
        scratch_shapes=list(scratch),
        compiler_params=pltpu.CompilerParams(vmem_limit_bytes=32 * 2**20),
        cost_estimate=pl.CostEstimate(flops=flops, bytes_accessed=10**7, transcendentals=10**5),
    )(*args)


def exchange(a):
    return lax.all_to_all(a, SEQ, 0, 0, tiled=True)


AXES = DP + SEQ


def device(x, y, z, core):
    ylo, yhi = y % 2, (y % 8) // 2
    return ((((x % 4) * 2 + ylo) * 4 + yhi) * 8 + z % 8) * 2 + core


def receive(a, source):
    pairs = []
    for x in range(4):
        for y in range(8):
            for z in range(8):
                for core in range(2):
                    pairs.append((device(*source(x, y, z, core), core), device(x, y, z, core)))
    return lax.ppermute(a, AXES, pairs)


def swap_cores(a):
    return lax.ppermute(a, "core", [(0, 1), (1, 0)])


def class_source(x, y, z, core):
    ylo, yhi = y % 2, y // 2
    cls = (x % 2) * 2 + ylo
    return (x // 2) * 2 + yhi // 2, cls * 2 + yhi % 2, z


def near_source(dx, dy):
    def source(x, y, z, core):
        sign = 1 - 2 * core
        return x + sign * dx, y + sign * dy, z

    return source


def gather_weights(w_so, w_qkv, w_out, place, sent):
    shard = jnp.concatenate([w_so, w_out, w_qkv.T, jnp.zeros((3, D), BF)], 0)
    shard, sent = lax.optimization_barrier((receive(shard, class_source), sent))
    mine = lax.all_gather(shard, "z", axis=0, tiled=True)
    other = swap_cores(mine)
    rows = lambda n: ((n, D), BF)
    own_so, own_out, own_qkv, part = call(
        compact_kernel, [rows(144), rows(144), rows(432), rows(384)], place, mine, other, scalars=1,
        scratch=[
            pltpu.VMEM((2, 384, D), BF),
            pltpu.VMEM((144, D), F32),
            pltpu.VMEM((144, D), F32),
            pltpu.VMEM((432, D), F32),
        ],
    )
    part, sent = lax.optimization_barrier((part, sent))
    near = [receive(part, near_source(dx, dy)) for dx, dy in ((1, 0), (0, 1), (1, 1))]
    sent = exchange(sent)
    return [own_qkv, own_so, own_out] + near + [swap_cores(a) for a in near], sent


def body(tokens, qkv, w_so, w_qkv, w_out, factors, cotangent):
    tokens, qkv, cotangent, factors = tokens[0, 0], qkv[0, 0], cotangent[0, 0], factors[0]
    core = lax.axis_index("core")
    cls = (lax.axis_index("x") % 2) * 2 + lax.axis_index("ylo")
    place = jnp.stack([core, cls]).astype(jnp.int32)

    (mixed_s,) = call(spatial_forward_kernel, [((ROWS, ATT), BF)], qkv)
    sent = jnp.concatenate([tokens, cotangent, mixed_s], 1).reshape(64, 2, 2 * D + ATT)
    weights, sent = gather_weights(w_so, w_qkv, w_out, place, sent)

    rows = lambda n, kind=BF: ((ROWS, n), kind)
    out_keep, out_send, *saved = call(
        temporal_forward_kernel,
        [
            ((64, 2 * HALF), F32), ((64, 2 * HALF), BF),
            ((ATT, D), BF), ((ATT, D), BF), ((3 * ATT, D), BF),
            rows(ATT), rows(ATT), rows(ATT), ((HEADS * ROWS, ROWS), F32), rows(ATT),
            rows(D, F32), rows(128, F32), rows(D, F32), rows(D),
        ],
        place, sent, factors, *weights,
        scalars=1, hbm=6, flops=4 * 10**9,
        scratch=[pltpu.SemaphoreType.DMA((3 * COPIES,))],
    )
    w_so = saved[0]
    out_other = swap_cores(out_send)
    (packed,) = call(temporal_backward_kernel, [rows(2 * D)], factors, *saved, flops=4 * 10**9)

    (packed,) = call(
        pack_kernel, [((64, 2, 2 * D + HALF), BF)], packed, out_keep, out_other, flops=10**8
    )
    token_grad, out_part, mine = call(
        unpack_kernel,
        [rows(D), ((8, 2, 2 * HALF), BF), ((2, D), F32)],
        exchange(packed), flops=10**8,
    )
    out_part = jnp.sum(lax.all_to_all(out_part, DP, 0, 0, tiled=True).astype(F32), 0)
    out_grad = out_part.reshape(2, 9, ATT).transpose(1, 0, 2).reshape(9, D)

    (qkv_grad,) = call(
        spatial_backward_kernel, [((ROWS, 3 * ATT), BF)], qkv, token_grad, factors, w_so
    )
    other = swap_cores(mine)
    factor_grad = jnp.where(core == 0, jnp.concatenate([mine, other]), jnp.concatenate([other, mine]))
    return token_grad[None, None], qkv_grad[None, None], factor_grad[None], out_grad


def solution(mesh):
    fine = Mesh(mesh.devices.reshape(4, 2, 4, 8, 2), DP + SEQ)
    frames = P(DP, SEQ, None, None)
    return jax.shard_map(
        body,
        mesh=fine,
        in_specs=(
            frames,
            frames,
            P(SEQ, None),
            P(None, SEQ),
            P(SEQ, None),
            P(DP, None, None),
            frames,
        ),
        out_specs=(frames, frames, P(DP, None, None), P(SEQ, None)),
        check_vma=False,
    )
```
